32 devices in a mesh: dp: 8 (over z, y), tensor: 4 (over x, core).
Axes of the slice: x: 2, y: 2, z: 4, core: 2. Of those that a mesh axis runs over, the one named last changes fastest.
Arguments:
- inputs: bfloat16 [8192, 768], P(('dp', 'tensor')), may hold values from -6 to 6
- segments: int32 [8, 1024], P('dp'), may hold values from 0 to 7, never falling along the last dimension, each value on 1 to 256 neighbouring positions
- buckets: int32 [2047], replicated, may hold values from 0 to 31
- routes: int32 [8, 1024, 1], P('dp'), may hold values from 0 to 15; in each aligned block of 1024 rows (0 to 1023, 1024 to 2047, ..., all dimensions but the last counted through in order) at most 80 rows name the same one
- qkv_weight: bfloat16 [3, 768, 768], P(None, None, 'tensor'), may hold values from -0.109375 to 0.109375
- out_weight: bfloat16 [768, 768], P('tensor'), may hold values from -0.75 to 0.75
- rel_bias: float32 [32, 12], P(None, 'tensor'), may hold values from -3 to 3
- norm_attn: float32 [768], replicated, may hold values from 0.5 to 1.5
- norm_moe: float32 [768], replicated, may hold values from 0.5 to 1.5
- router_weight: bfloat16 [768, 16], replicated, may hold values from -0.109375 to 0.109375
- expert_in: bfloat16 [16, 768, 3072], P('dp', None, 'tensor'), may hold values from -0.21875 to 0.21875
- expert_out: bfloat16 [16, 3072, 768], P('dp', 'tensor'), may hold values from -3.59375 to 3.59375
- cotangent: bfloat16 [8192, 768], P(('dp', 'tensor')), may hold values from -6 to 6
Outputs:
- output: bfloat16 [8192, 768], P(('dp', 'tensor'))
- grad_inputs: float32 [8192, 768], P(('dp', 'tensor'))
- grad_qkv_weight: float32 [3, 768, 768], P(None, None, 'tensor')
- grad_out_weight: float32 [768, 768], P('tensor')
- grad_rel_bias: float32 [32, 12], P(None, 'tensor')
- grad_norm_attn: float32 [768], replicated
- grad_norm_moe: float32 [768], replicated
- grad_router: float32 [768, 16], replicated
- grad_expert_in: float32 [16, 768, 3072], P('dp', None, 'tensor')
- grad_expert_out: float32 [16, 3072, 768], P('dp', 'tensor')
The draws below stay inside these ranges and needn't reach their ends.
Inputs may be any that keep to these rules, and one draw needn't show every extreme that they name: `routes`: at most 80 tokens of one sequence have the same route, and in every draw some expert gets exactly 80 tokens of some sequence. `segments`: along a sequence the ids never fall; each document holds 1 to 256 positions.
All inputs are finite; a program needn't handle non-finite values.
Results may differ from the reference program's by a relative error of at most 0.018.
The reference program's roundings to bfloat16 on the way count: a program that leaves them out, or rounds other values in their place, can miss the bound.
Values may be sent and summed in bfloat16 or wider, within the bound.
No kernel may reach another device: no remote copies, remote signals or barrier semaphores. Data moves between devices by JAX's collectives and lax.ppermute only.
A program may use at most 192 MiB of HBM per device.

```python
import math
import jax
import jax.numpy as jnp
import numpy as np
from jax import lax

D = 768
HEADS = 12
HEAD_SIZE = 64
FF = 3072
BUCKETS = 32
EXPERTS = 16
SEQ = 1024
SEQS = 8
TOKENS = 8192
CAP = 80
N_TENSOR = 4


def place_ends(entries, stream_key, least, top_value):
    longest = entries.shape.index(max(entries.shape))
    spots = []
    for shift in (0, 1):
        where = [jax.random.randint(jax.random.fold_in(stream_key, axis), (), 0, length) for axis, length in enumerate(entries.shape)]
        where[longest] = (where[longest] + shift) % entries.shape[longest]
        spots.append(tuple(where))
    return entries.at[spots[0]].set(least).at[spots[1]].set(top_value)


def steps_of(own_key, dims, pieces, smallest, high):
    level, own = 1.0, jax.random.fold_in(own_key, 6)
    for dim, shards_of in pieces:
        heights = jnp.exp(jax.random.uniform(jax.random.fold_in(own, dim), (shards_of,), jnp.float32, smallest / len(pieces), high / len(pieces)))
        level = level * jnp.repeat(heights, dims[dim] // shards_of).reshape([-1 if axis == dim else 1 for axis in range(len(dims))])
    return level


def split_up(count, total, most, slope):
    loads = [(1 << 20) // math.isqrt(rank ** slope) + 1 for rank in range(2, count + 1)]
    spare, counts = total - most - (count - 1), [1] * (count - 1)
    while spare > 0:
        free = [i for i in range(count - 1) if counts[i] < most]
        pool, budget = sum([loads[i] for i in free]), spare
        for i in free:
            addition = min(most - counts[i], max(1, budget * loads[i] // pool), spare)
            counts[i] = counts[i] + addition
            spare = spare - addition
    return np.array([most] + counts)


def uneven_parts(stream_key, count, total, most, skew):
    if count == 2:
        one = jax.random.randint(stream_key, (), max(1, total - most), min(most, total - 1) + 1)
        return jnp.stack([one, total - one])
    lengths = jnp.asarray(split_up(count, total, most, skew), jnp.int32)
    couples = (count - 1) // 2
    giver, receiver = lengths[1:1 + 2 * couples:2], lengths[2:2 + 2 * couples:2]
    margin = jnp.minimum(giver - 1, most - receiver)
    shifted = jax.random.randint(jax.random.fold_in(stream_key, 1), (couples,), 0, 1 << 20) % (margin + 1)
    lengths = lengths.at[1:1 + 2 * couples:2].set(giver - shifted).at[2:2 + 2 * couples:2].set(receiver + shifted)
    return lengths[jax.random.permutation(jax.random.fold_in(stream_key, 2), count)]


def deal_out(key, own, number, rows, count, top, limit, slope):
    order = jax.random.permutation(key, count)
    crowded, common = portions_of(count, rows * top, limit, slope, True), portions_of(count, rows * top, limit, slope, False)
    places = jnp.arange(count)

    def named(tallies, offset_by):
        used = int((tallies > 0).sum())
        fixed = max(1, used // 4)
        shifted = fixed + (places - fixed + offset_by * (used - fixed)) % max(1, count - fixed)
        return jnp.zeros((count,), jnp.int32).at[order[jnp.where(places < fixed, places, shifted)]].set(jnp.asarray(tallies, jnp.int32))

    tallies = jnp.where(number % 4 == 0, named(crowded, number // 4), named(common, number - number // 4 - 1))
    mixed = jax.random.permutation(jax.random.fold_in(own, 3), count)
    source_of, sink = mixed[0:count // 2 * 2:2], mixed[1:count // 2 * 2:2]
    margin = jnp.minimum(tallies[source_of] - 1, limit - tallies[sink]) // 2
    margin = jnp.where((source_of == order[0]) | (sink == order[0]) | (tallies[sink] == 0), 0, jnp.maximum(margin, 0))
    shifted = jax.random.randint(jax.random.fold_in(own, 4), (count // 2,), 0, 1 << 20) % (margin + 1)
    tallies = tallies.at[source_of].add(-shifted).at[sink].add(shifted)
    items = jnp.searchsorted(jnp.cumsum(tallies), jnp.arange(rows * top), side="right").astype(jnp.int32)
    table = items.reshape(top, rows).T
    table = table[jax.random.permutation(jax.random.fold_in(own, 1), rows)]
    offset_by = jax.random.randint(jax.random.fold_in(own, 2), (rows, 1), 0, top)
    return jnp.take_along_axis(table, (jnp.arange(top)[None, :] + offset_by) % top, axis=1)


def portions_of(amount, total, bound, skew, full):
    weights = [(1 << 20) // math.isqrt(standing ** skew) + 1 for standing in range(1, amount + 1)]
    largest = bound if full else min(bound, max(-(-total // amount), total * weights[0] // sum(weights)))
    least = 1 if total - largest >= amount - 1 else 0
    given, spare = [largest] + [least] * (amount - 1), total - largest - least * (amount - 1)
    while spare > 0:
        movable = [i for i in range(1, amount) if given[i] < largest] or [i for i in range(1, amount) if given[i] < bound]
        whole, budget = sum([weights[i] for i in movable]), spare
        for i in movable:
            more = min(bound - given[i], max(1, budget * weights[i] // whole), spare)
            given[i] = given[i] + more
            spare = spare - more
    return np.array(given)


def gaussian(key, dims, spread, limit, cuts=(), kind=jnp.bfloat16):
    values = spread * jax.random.normal(key, dims, jnp.float32)
    if cuts:
        values = values * steps_of(key, dims, cuts, -0.22, 0.18)
    return jnp.clip(values, -limit, limit).astype(kind)


def setup_inputs(seed: int = 0) -> dict:
    seeds = jax.random.split(jax.random.key(seed), 14)
    inputs = gaussian(seeds[0], (TOKENS, D), 1.0, 6.0, ((0, 32),))
    segments = jax.vmap(lambda own: jnp.searchsorted(jnp.cumsum(uneven_parts(own, 8, SEQ, SEQ // 4, 1)), jnp.arange(SEQ), side="right"))(jax.random.split(seeds[1], SEQS)).reshape((SEQS, SEQ)).astype(jnp.int32)
    buckets = place_ends(jax.random.randint(seeds[2], (2 * SEQ - 1,), 0, BUCKETS), jax.random.fold_in(seeds[2], 1), 0, BUCKETS - 1).astype(jnp.int32)
    routes_keys = jax.random.split(jax.random.fold_in(seeds[3], 1), SEQS * SEQ // SEQ)
    routes_turns = jax.random.permutation(jax.random.fold_in(seeds[3], 3), SEQS * SEQ // SEQ)
    routes = jax.vmap(lambda own, number: deal_out(jax.random.fold_in(seeds[3], 2), own, number, SEQ, EXPERTS, 1, CAP, 1))(routes_keys, routes_turns).reshape((SEQS, SEQ, 1))
    qkv_weight = gaussian(seeds[4], (3, D, HEADS * HEAD_SIZE), (4 * D) ** -0.5, 0.109375, ((2, 4),))
    out_weight = gaussian(seeds[5], (HEADS * HEAD_SIZE, D), 64 ** -0.5, 0.75, ((0, 4),))
    rel_bias = gaussian(seeds[6], (BUCKETS, HEADS), 0.5, 3.0, ((1, 4),), jnp.float32)
    norm_attn = jnp.clip(1.0 + 0.1 * jax.random.normal(seeds[7], (D,), jnp.float32), 0.5, 1.5)
    norm_moe = jnp.clip(1.0 + 0.1 * jax.random.normal(seeds[8], (D,), jnp.float32), 0.5, 1.5)
    router_weight = gaussian(seeds[9], (D, EXPERTS), (4 * D) ** -0.5, 0.109375)
    expert_in = gaussian(seeds[10], (EXPERTS, D, FF), D ** -0.5, 0.21875, ((0, 8), (2, 4)))
    expert_out = gaussian(seeds[11], (EXPERTS, FF, D), (EXPERTS * 0.0375), 3.59375, ((0, 8), (1, 4)))
    cotangent = gaussian(seeds[12], (TOKENS, D), 1.0, 6.0, ((0, 32),))
    return {"inputs": inputs, "segments": segments, "buckets": buckets, "routes": routes, "qkv_weight": qkv_weight, "out_weight": out_weight, "rel_bias": rel_bias, "norm_attn": norm_attn, "norm_moe": norm_moe, "router_weight": router_weight, "expert_in": expert_in, "expert_out": expert_out, "cotangent": cotangent}


@jax.custom_vjp
def low(v):
    return lax.optimization_barrier(v.astype(jnp.bfloat16)).astype(jnp.float32)

@jax.custom_vjp
def low_back(v):
    return v

def low_keep(v):
    return (low(v), None)

def low_pass(kept, grad):
    return (grad,)

def back_keep(v):
    return (v, None)

def back_low(kept, grad):
    return (low(grad),)
low.defvjp(low_keep, low_pass)
low_back.defvjp(back_keep, back_low)
epsilon = 1e-06
negative = -1000000000.0
highest = lax.Precision.HIGHEST

def smooth_act(values):
    return jax.nn.gelu(values, approximate=True)

def rms_apply(values, gain_vec):
    inv_rms = lax.rsqrt(lax.optimization_barrier(jnp.mean(values * values, axis=-1, keepdims=True)) + epsilon)
    return values * inv_rms * gain_vec

def attend(seq_inputs, segment_row, qkv_weight, out_weight, dist_bias, norm_attn):
    seq_len = seq_inputs.shape[0]
    normed = low(rms_apply(seq_inputs, norm_attn))
    qkv = jnp.einsum('sd,cdf->csf', normed, qkv_weight, precision=highest)
    qkv = low(low_back(qkv))
    query_rows = qkv[0].reshape(seq_len, HEADS, HEAD_SIZE)
    key_rows = qkv[1].reshape(seq_len, HEADS, HEAD_SIZE)
    value_rows = qkv[2].reshape(seq_len, HEADS, HEAD_SIZE)
    raw_scores = jnp.einsum('qhe,khe->hqk', query_rows, key_rows, precision=highest)
    dist_index = (jnp.arange(seq_len, dtype=jnp.int32)[None, :] - jnp.arange(seq_len, dtype=jnp.int32)[:, None] + seq_len - 1).astype(jnp.int32)
    bias_rows = jnp.take(dist_bias, dist_index, axis=1)
    same_doc = segment_row[:, None] == segment_row[None, :]
    scores = low_back(jnp.where(same_doc[None], raw_scores + bias_rows, negative))
    attn_probs = jax.nn.softmax(scores, axis=-1)
    context = jnp.einsum('hqk,khe->qhe', low(attn_probs), value_rows, precision=highest).reshape(seq_len, HEADS * HEAD_SIZE)
    context = low(low_back(context))
    attn_out = low_back(jnp.dot(context, out_weight, precision=highest))
    return seq_inputs + attn_out

def expert_rows_fn(packed):
    rows_in, w_first, w_second = packed
    col_width = FF // N_TENSOR
    summed = jnp.zeros(rows_in.shape, jnp.float32)
    for quarter in range(N_TENSOR):
        inputs_part = low_back(rows_in)
        pre_act = low_back(jnp.dot(inputs_part, w_first[:, quarter * col_width:(quarter + 1) * col_width], precision=highest))
        hidden = low(smooth_act(pre_act))
        summed = summed + low(jnp.dot(hidden, w_second[quarter * col_width:(quarter + 1) * col_width, :], precision=highest))
    return summed

def forward(inputs, qkv_weight, out_weight, rel_bias, norm_attn, norm_moe, router_weight, expert_in, expert_out, segments, buckets, routes):
    bucket_table = (buckets[:, None] == jnp.arange(BUCKETS, dtype=jnp.int32)[None, :]).astype(jnp.float32)
    dist_bias = jnp.dot(bucket_table, rel_bias, precision=highest).T

    def one_seq(packed):
        return attend(packed[0], packed[1], qkv_weight, out_weight, dist_bias, norm_attn)
    h_one = lax.map(jax.checkpoint(one_seq), (inputs.reshape(SEQS, SEQ, D), segments))
    normed = low(rms_apply(h_one, norm_moe))
    logits = low_back(jnp.einsum('tsd,de->tse', normed, router_weight, precision=highest))
    router_probs = jax.nn.softmax(logits, axis=-1)
    route_ids = routes[:, :, 0]
    chosen = route_ids[:, :, None] == jnp.arange(EXPERTS, dtype=jnp.int32)[None, None, :]
    gate_value = lax.optimization_barrier(jnp.sum(jnp.where(chosen, router_probs, 0.0), axis=-1))
    running = jnp.cumsum(chosen.astype(jnp.int32), axis=1)
    slot_index = lax.optimization_barrier(jnp.sum(jnp.where(chosen, running - 1, 0), axis=-1)).astype(jnp.int32)
    position = (route_ids * CAP + slot_index).astype(jnp.int32)
    seq_index = jnp.broadcast_to(jnp.arange(SEQS, dtype=jnp.int32)[:, None], (SEQS, SEQ))
    slot_rows = jnp.zeros((SEQS, EXPERTS * CAP, D), jnp.float32).at[seq_index, position].add(normed)
    by_expert = slot_rows.reshape(SEQS, EXPERTS, CAP, D).transpose(1, 0, 2, 3).reshape(EXPERTS, SEQS * CAP, D)
    returned = lax.map(jax.checkpoint(expert_rows_fn), (by_expert, expert_in, expert_out))
    by_seq = returned.reshape(EXPERTS, SEQS, CAP, D).transpose(1, 0, 2, 3).reshape(SEQS, EXPERTS * CAP, D)
    expert_sum = low_back(by_seq[seq_index, position])
    mixed_rows = h_one + gate_value[:, :, None] * expert_sum
    return mixed_rows.reshape(SEQS * SEQ, D)

def reference(inputs, segments, buckets, routes, qkv_weight, out_weight, rel_bias, norm_attn, norm_moe, router_weight, expert_in, expert_out, cotangent):

    def closed(x_in, w_qkv, w_out_attn, bias_table, gain_one, gain_two, w_router, w_first, w_second):
        return forward(x_in, w_qkv, w_out_attn, bias_table, gain_one, gain_two, w_router, w_first, w_second, segments, buckets, routes)
    result, pullback = jax.vjp(closed, inputs.astype(jnp.float32), qkv_weight.astype(jnp.float32), out_weight.astype(jnp.float32), rel_bias.astype(jnp.float32), norm_attn.astype(jnp.float32), norm_moe.astype(jnp.float32), router_weight.astype(jnp.float32), expert_in.astype(jnp.float32), expert_out.astype(jnp.float32))
    grads = pullback(cotangent.astype(jnp.float32))
    return (result.astype(jnp.bfloat16), grads[0], grads[1], grads[2], grads[3], grads[4], grads[5], grads[6], grads[7], grads[8])
```

```python
import functools

import jax
import jax.numpy as jnp
from jax import lax
from jax.experimental import pallas as pl
from jax.experimental.pallas import tpu as pltpu
from jax.sharding import PartitionSpec as P

epsilon = 1e-06
negative = -1000000000.0
bf16 = jnp.bfloat16
f32 = jnp.float32
reach = 256
rows_q = 128
window = rows_q + 2 * reach
table = window + rows_q
head_size = 64
mega = 1024 * 1024

core_pairs = [(0, 1), (1, 0), (2, 3), (3, 2)]
x_pairs = [(0, 2), (2, 0), (1, 3), (3, 1)]


def core_hop(value):
    return lax.ppermute(value, "tensor", core_pairs)


def x_hop(value):
    return lax.ppermute(value, "tensor", x_pairs)


def gather4(value):
    other = x_hop(value)
    return value, core_hop(value), other, core_hop(other)


def dot(a, b, dims):
    return lax.dot_general(a, b, (dims, ((), ())), preferred_element_type=f32)


def mm(a, b):
    return dot(a, b, ((1,), (0,)))


def mm_nt(a, b):
    return dot(a, b, ((1,), (1,)))


def mm_tn(a, b):
    return dot(a, b, ((0,), (0,)))


def shape(dims, kind):
    return jax.ShapeDtypeStruct(dims, kind)


def run(body, outs, args, smem=(), scratch=(), limit=48, flops=0, name=None):
    specs = [
        pl.BlockSpec(memory_space=pltpu.SMEM if i in smem else pltpu.VMEM)
        for i in range(len(args))
    ]
    moved = sum(a.size * a.dtype.itemsize for a in args) + sum(
        o.size * jnp.dtype(o.dtype).itemsize for o in outs
    )
    return pl.pallas_call(
        body,
        out_shape=outs,
        in_specs=specs,
        out_specs=[pl.BlockSpec(memory_space=pltpu.VMEM)] * len(outs),
        scratch_shapes=list(scratch),
        compiler_params=pltpu.CompilerParams(vmem_limit_bytes=limit * mega),
        cost_estimate=pl.CostEstimate(flops=flops, bytes_accessed=moved, transcendentals=0),
        name=name,
    )(*args)


def slots_body(experts, capacity, row_ref, col_ref, code_row, code_col):
    seq = row_ref.shape[1]
    half = capacity // 2
    quarter = (experts // 2) * half
    first = lax.broadcasted_iota(jnp.int32, (seq, seq), 0)
    second = lax.broadcasted_iota(jnp.int32, (seq, seq), 1)

    def code(route, slot):
        upper = jnp.where(slot >= half, 1, 0)
        return (2 * (route & 1) + upper) * quarter + (route >> 1) * half + slot - half * upper

    route = col_ref[...]
    chosen = route == lax.broadcasted_iota(jnp.int32, (seq, experts), 1)
    count = mm((second < first).astype(bf16), chosen.astype(bf16))
    slot = jnp.sum(jnp.where(chosen, count, 0.0), axis=1, keepdims=True).astype(jnp.int32)
    code_col[...] = code(route, slot)
    route = row_ref[...]
    chosen = route == lax.broadcasted_iota(jnp.int32, (experts, seq), 0)
    count = mm(chosen.astype(bf16), (first < second).astype(bf16))
    slot = jnp.sum(jnp.where(chosen, count, 0.0), axis=0, keepdims=True).astype(jnp.int32)
    code_row[...] = code(route, slot)


def span(i0, seq):
    start = max(0, i0 - reach)
    end = min(seq, i0 + rows_q + reach)
    return start, end, start - (i0 - reach)


def attend_body(
    t_ref, x0, x1, x2, x3, gain, weight, seg_row, seg_col, near, bias,
    x_all, normed, qkv, probs, ctx, tile,
):
    t = t_ref[0]
    own = x0.shape[0]
    seq = 4 * own
    heads = bias.shape[1]
    columns = heads * head_size
    for k, ref in enumerate((x0, x1, x2, x3)):
        at = pl.ds(pl.multiple_of((t ^ k) * own, own), own)
        x = ref[...]
        x_all[at, :] = x
        x = x.astype(f32)
        inv = lax.rsqrt(jnp.mean(x * x, axis=1, keepdims=True) + epsilon)
        normed[at, :] = (x * inv * gain[...]).astype(bf16)
    for c in range(3):
        full = mm(normed[...], weight[c])
        for h in range(heads):
            qkv[c * heads + h] = full[:, h * head_size : (h + 1) * head_size].astype(bf16)
    bucket = near[...]
    for h in range(heads):
        line = jnp.zeros(bucket.shape, f32)
        for b in range(bias.shape[0]):
            line = jnp.where(bucket == b, bias[b, h], line)
        wide = jnp.broadcast_to(line, (rows_q, table))
        tile[h] = pltpu.roll(wide, 0, 1, stride=1, stride_axis=0)[:, :window]
    for i0 in range(0, seq, rows_q):
        start, end, off = span(i0, seq)
        same = seg_col[i0 : i0 + rows_q, :] == seg_row[:, start:end]
        parts = []
        for h in range(heads):
            query = qkv[h, i0 : i0 + rows_q, :]
            score = mm_nt(query, qkv[heads + h, start:end, :])
            score = jnp.where(same, score + tile[h, :, off : off + end - start], negative)
            score = jnp.exp(score - jnp.max(score, axis=1, keepdims=True))
            inv = 1.0 / jnp.sum(score, axis=1, keepdims=True)
            prob = (score * inv).astype(bf16)
            probs[h, i0 : i0 + rows_q, 0 : end - start] = prob
            parts.append(mm(prob, qkv[2 * heads + h, start:end, :]).astype(bf16))
        ctx[i0 : i0 + rows_q, :] = jnp.concatenate(parts[:2], axis=1)
        lane = 0 if i0 < seq // 2 else head_size
        at = seq + i0 % (seq // 2)
        ctx[at : at + rows_q, lane : lane + head_size] = parts[2]


def third(ctx, r0, rows, seq):
    lane = 0 if r0 < seq // 2 else head_size
    at = seq + r0 % (seq // 2)
    return ctx[at : at + rows, lane : lane + head_size]


def mid_body(
    t_ref, x_all, c0, c1, c2, c3, w0, w1, w2, w3, gain, code_row,
    h_one, h_own, rows, normed,
):
    t = t_ref[0]
    seq = x_all.shape[0]
    own = seq // 4
    quarter = rows.shape[0]
    ctxs = (c0, c1, c2, c3)
    weights = (w0, w1, w2, w3)
    pair = 2 * head_size
    packed = [
        jnp.concatenate([weights[2 * i][0:pair, :], weights[2 * i + 1][0:pair, :]], axis=0)
        for i in range(2)
    ]
    last = jnp.concatenate([w[pair : pair + head_size, :] for w in weights], axis=0)
    for r0 in range(0, seq, own):
        at = slice(r0, r0 + own)
        total = x_all[at, :].astype(f32)
        for i in range(2):
            left = jnp.concatenate([ctxs[2 * i][at, :], ctxs[2 * i + 1][at, :]], axis=1)
            total = total + mm(left, packed[i])
        left = jnp.concatenate([third(c, r0, own, seq) for c in ctxs], axis=1)
        total = total + mm(left, last)
        h_one[at, :] = total
        inv = lax.rsqrt(jnp.mean(total * total, axis=1, keepdims=True) + epsilon)
        normed[at, :] = (total * inv * gain[...]).astype(bf16)
    h_own[...] = h_one[pl.ds(pl.multiple_of(t * own, own), own), :]
    place = lax.broadcasted_iota(jnp.int32, (quarter, seq), 0) + t * quarter
    rows[...] = mm((place == code_row[...]).astype(bf16), normed[...]).astype(bf16)


def spread_body(t_ref, g0, g1, g2, g3, code_row, g_all, rows):
    t = t_ref[0]
    own = g0.shape[0]
    quarter = rows.shape[0]
    for k, ref in enumerate((g0, g1, g2, g3)):
        g_all[pl.ds(pl.multiple_of((t ^ k) * own, own), own), :] = ref[...]
    place = lax.broadcasted_iota(jnp.int32, (quarter, g_all.shape[0]), 0) + t * quarter
    rows[...] = mm((place == code_row[...]).astype(bf16), g_all[...]).astype(bf16)


gelu_scale = 0.7978845608028654
gelu_cubic = 0.044715


def expert_body(
    e_ref, r0, r1, g0, g1, w_in, w_out, router,
    back0, back1, grad0, grad1, hidden_out, gated_out, pre_out, rows_out, router_out,
):
    rows = jnp.concatenate([r0[...], r1[...]], axis=0)
    cot = jnp.concatenate([g0[...], g1[...]], axis=0).astype(f32)
    half = r0.shape[0]
    experts = router.shape[1]
    logits = mm(rows, router[...])
    logits = jnp.exp(logits - jnp.max(logits, axis=1, keepdims=True))
    prob = logits / jnp.sum(logits, axis=1, keepdims=True)
    mine = lax.broadcasted_iota(jnp.int32, prob.shape, 1) == e_ref[1]
    gate = jnp.sum(jnp.where(mine, prob, 0.0), axis=1, keepdims=True)
    pre = mm(rows, w_in[0])
    inner = jnp.tanh(gelu_scale * (pre + gelu_cubic * pre * pre * pre))
    hidden = (0.5 * pre * (1.0 + inner)).astype(bf16)
    slope = 0.5 * (1.0 + inner) + 0.5 * pre * (1.0 - inner * inner) * gelu_scale * (
        1.0 + 3.0 * gelu_cubic * pre * pre
    )
    part = mm(hidden, w_out[0])
    back = (gate * part).astype(bf16)
    back0[...] = back[:half]
    back1[...] = back[half:]
    grad_gate = jnp.sum(cot * part, axis=1, keepdims=True)
    gated = (gate * cot).astype(bf16)
    grad_pre = (mm_nt(gated, w_out[0]) * slope).astype(bf16)
    grad_logits = (gate * grad_gate * (jnp.where(mine, 1.0, 0.0) - prob)).astype(bf16)
    grad = mm_nt(grad_pre, w_in[0]) + mm_nt(grad_logits, router[...])
    grad = grad.astype(bf16)
    grad0[...] = grad[:half]
    grad1[...] = grad[half:]
    hidden_out[...] = hidden
    gated_out[...] = gated
    pre_out[...] = grad_pre
    rows_out[...] = rows
    router_out[...] = mm_tn(grad_logits, rows)


def expert(e_index, e_global, r0, r1, g0, g1, w_in, w_out, router):
    scalars = jnp.stack([e_index, e_global])
    half, width = r0.shape
    hidden = w_in.shape[2]
    rows = 2 * half
    experts = router.shape[1]
    outs = [shape((half, width), bf16)] * 4 + [
        shape((rows, hidden), bf16),
        shape((rows, width), bf16),
        shape((rows, hidden), bf16),
        shape((rows, width), bf16),
        shape((experts, width), f32),
    ]

    def whole(dims):
        return pl.BlockSpec(dims, lambda i, s: (0,) * len(dims))

    spec = pltpu.PrefetchScalarGridSpec(
        num_scalar_prefetch=1,
        grid=(1,),
        in_specs=[whole(r0.shape)] * 4
        + [
            pl.BlockSpec((1,) + w_in.shape[1:], lambda i, s: (s[0], 0, 0)),
            pl.BlockSpec((1,) + w_out.shape[1:], lambda i, s: (s[0], 0, 0)),
            whole(router.shape),
        ],
        out_specs=[whole(o.shape) for o in outs],
    )
    return pl.pallas_call(
        expert_body,
        out_shape=outs,
        grid_spec=spec,
        compiler_params=pltpu.CompilerParams(vmem_limit_bytes=56 * mega),
        cost_estimate=pl.CostEstimate(
            flops=8 * rows * hidden * width, bytes_accessed=12 * mega, transcendentals=0
        ),
        name="expert",
    )(scalars, r0, r1, g0, g1, w_in, w_out, router)


def expert_grad_body(e_ref, hid0, gat0, pre0, row0, hid1, gat1, pre1, row1, d_in, d_out):
    near = pl.program_id(0) == 0

    @pl.when(near)
    def _():
        d_in[0] = mm_tn(row0[...], pre0[...])
        d_out[0] = mm_tn(hid0[...], gat0[...])

    @pl.when(jnp.logical_not(near))
    def _():
        d_in[0] = mm_tn(row1[...], pre1[...])
        d_out[0] = mm_tn(hid1[...], gat1[...])


def expert_grads(e_index, first, second):
    rows, hidden = first[0].shape
    width = first[3].shape[1]

    def whole(a):
        return pl.BlockSpec(a.shape, lambda i, s: (0, 0))

    def place(i, s):
        return (s[0] * (1 - i) + (1 - s[0]) * i, 0, 0)

    spec = pltpu.PrefetchScalarGridSpec(
        num_scalar_prefetch=1,
        grid=(2,),
        in_specs=[whole(a) for a in (*first, *second)],
        out_specs=[
            pl.BlockSpec((1, width, hidden), place),
            pl.BlockSpec((1, hidden, width), place),
        ],
    )
    return pl.pallas_call(
        expert_grad_body,
        out_shape=[shape((2, width, hidden), f32), shape((2, hidden, width), f32)],
        grid_spec=spec,
        compiler_params=pltpu.CompilerParams(vmem_limit_bytes=56 * mega),
        cost_estimate=pl.CostEstimate(
            flops=8 * rows * hidden * width, bytes_accessed=20 * mega, transcendentals=0
        ),
        name="expert_grads",
    )(e_index[None], *first, *second)


def back_body(
    t_ref, b0, b1, b2, b3, code_col, h_one, gain, g_all, weight, ctx, probs, qkv, normed, router,
    grad_h, h_own, gctx, grad_v, early,
):
    t = t_ref[0]
    seq, width = h_one.shape
    own = seq // 4
    quarter = b0.shape[0]
    heads = gctx.shape[0]
    columns = heads * head_size
    sum_gain = jnp.zeros((1, width), f32)
    for r0 in range(0, seq, own):
        at = slice(r0, r0 + own)
        total = jnp.zeros((own, width), f32)
        for k, ref in enumerate((b0, b1, b2, b3)):
            place = lax.broadcasted_iota(jnp.int32, (own, quarter), 1) + (t ^ k) * quarter
            total = total + mm((place == code_col[at, :]).astype(bf16), ref[...])
        h = h_one[at, :]
        inv = lax.rsqrt(jnp.mean(h * h, axis=1, keepdims=True) + epsilon)
        n2 = h * inv
        sum_gain = sum_gain + jnp.sum(total * n2, axis=0, keepdims=True)
        a = total * gain[...]
        mean = jnp.mean(a * n2, axis=1, keepdims=True)
        full = g_all[at, :].astype(f32) + inv * (a - n2 * mean)
        grad_h[at, :] = full.astype(bf16)

        @pl.when(t * own == r0)
        def _():
            h_own[...] = full

        wide = mm_nt(grad_h[at, :], weight[...])
        for j in range(heads):
            gctx[j, at, :] = wide[:, j * head_size : (j + 1) * head_size].astype(bf16)
    for h in range(heads):
        sums = [None] * (seq // rows_q)
        for i0 in range(0, seq, rows_q):
            start, end, _ = span(i0, seq)
            add = mm_tn(probs[h, i0 : i0 + rows_q, 0 : end - start], gctx[h, i0 : i0 + rows_q, :])
            for j in range(start, end, rows_q):
                piece = add[j - start : j - start + rows_q]
                n = j // rows_q
                sums[n] = piece if sums[n] is None else sums[n] + piece
        for n, piece in enumerate(sums):
            grad_v[n * rows_q : (n + 1) * rows_q, h * head_size : (h + 1) * head_size] = (
                piece.astype(bf16)
            )
    early[0:columns, :] = mm_tn(grad_v[...], normed[...]).astype(bf16)
    flat = jnp.concatenate(
        [
            ctx[0:seq, :],
            jnp.concatenate([third(ctx, r, own, seq) for r in range(0, seq, own)], axis=0),
        ],
        axis=1,
    )
    early[columns : 2 * columns, :] = mm_tn(flat, grad_h[...]).astype(bf16)
    early[2 * columns :, :] = jnp.zeros((early.shape[0] - 2 * columns, width), bf16)
    experts = router.shape[0]
    early[2 * columns : 2 * columns + experts, :] = router[...].astype(bf16)
    early[2 * columns + experts : 2 * columns + experts + 1, :] = sum_gain.astype(bf16)


def attend_back_body(
    probs, qkv, gctx, normed, near,
    grad_q, grad_k, late, grad_bias, spill,
):
    heads, seq, _ = gctx.shape
    columns = heads * head_size
    buckets = grad_bias.shape[0]
    places = lax.broadcasted_iota(jnp.int32, (buckets, 128), 1)
    found = jnp.zeros((buckets, 128), f32)
    for h in range(heads):
        cols = slice(h * head_size, (h + 1) * head_size)
        sums = [None] * (seq // rows_q)
        spill[...] = jnp.zeros(spill.shape, f32)
        for i0 in range(0, seq, rows_q):
            start, end, off = span(i0, seq)
            at = slice(i0, i0 + rows_q)
            prob = probs[h, at, 0 : end - start].astype(f32)
            grad = mm_nt(gctx[h, at, :], qkv[2 * heads + h, start:end, :])
            both = prob * grad
            delta = jnp.sum(both, axis=1, keepdims=True)
            score = both - prob * delta
            spill[:, off : off + end - start] += score
            score = score.astype(bf16)
            grad_q[at, cols] = mm(score, qkv[heads + h, start:end, :]).astype(bf16)
            add = mm_tn(score, qkv[h, at, :])
            for j in range(start, end, rows_q):
                piece = add[j - start : j - start + rows_q]
                n = j // rows_q
                sums[n] = piece if sums[n] is None else sums[n] + piece
        for n, piece in enumerate(sums):
            grad_k[n * rows_q : (n + 1) * rows_q, cols] = piece.astype(bf16)
        strip = jnp.zeros((8, table), f32)
        for a in range(0, rows_q, 8):
            strip = strip + pltpu.roll(spill[a : a + 8, :], (table - a) % table, 1)
        line = lax.broadcasted_iota(jnp.int32, strip.shape, 0)
        for bit in (1, 2, 4):
            strip = jnp.where((line & bit) != 0, pltpu.roll(strip, table - bit, 1), strip)
        strip = jnp.sum(strip, axis=0, keepdims=True)
        chosen = near[...] == lax.broadcasted_iota(jnp.int32, (buckets, table), 0)
        per = jnp.sum(jnp.where(chosen, strip, 0.0), axis=1, keepdims=True)
        found = found + jnp.where(places == h, per, 0.0)
    grad_bias[...] = found
    late[0:columns, :] = mm_tn(grad_q[...], normed[...]).astype(bf16)
    late[columns : 2 * columns, :] = mm_tn(grad_k[...], normed[...]).astype(bf16)


def input_grad_body(t_ref, grad_q, grad_k, grad_v, weight, normed, gain, keep, send, sums):
    t = t_ref[0]
    seq, width = normed.shape
    own = seq // 4
    total_gain = jnp.zeros((1, width), f32)
    for k in range(4):
        at = pl.ds(pl.multiple_of((t ^ k) * own, own), own)
        part = mm_nt(grad_q[at, :], weight[0])
        part = part + mm_nt(grad_k[at, :], weight[1])
        part = part + mm_nt(grad_v[at, :], weight[2])
        total_gain = total_gain + jnp.sum(part * normed[at, :].astype(f32), axis=0, keepdims=True)
        out = keep if k in (0, 2) else send
        out[(k // 2) * own : (k // 2 + 1) * own, :] = part.astype(bf16)
    sums[...] = total_gain / gain[...]


def last_body(kept, got, far, x_ref, gain, h_own, grad):
    total = kept[...].astype(f32) + got[...].astype(f32) + far[...].astype(f32)
    x = x_ref[...].astype(f32)
    inv = lax.rsqrt(jnp.mean(x * x, axis=1, keepdims=True) + epsilon)
    n1 = x * inv
    a = total * gain[...]
    grad[...] = h_own[...] + inv * (a - n1 * jnp.mean(a * n1, axis=1, keepdims=True))


def output_body(t_ref, f0, f1, f2, f3, code_col, h_own, out):
    t = t_ref[0]
    own = h_own.shape[0]
    quarter = f0.shape[0]
    total = h_own[...]
    codes = code_col[pl.ds(pl.multiple_of(t * own, own), own), :]
    for k, ref in enumerate((f0, f1, f2, f3)):
        place = lax.broadcasted_iota(jnp.int32, (own, quarter), 1) + (t ^ k) * quarter
        total = total + mm((place == codes).astype(bf16), ref[...])
    out[...] = total.astype(bf16)


def turn(value):
    return lax.all_to_all(value, "dp", split_axis=0, concat_axis=0, tiled=True)


def reduce_dp(part):
    n = lax.axis_size("dp")
    got = turn(part).reshape(n, part.shape[0] // n, part.shape[1])
    return jnp.sum(got.astype(f32), axis=0).astype(bf16)


def gather_dp(share):
    n = lax.axis_size("dp")
    wide = jnp.broadcast_to(share[None], (n,) + share.shape)
    return turn(wide.reshape(n * share.shape[0], share.shape[1])).reshape((n,) + share.shape)


def per_device(
    inputs,
    segments,
    buckets,
    routes,
    qkv_weight,
    out_weight,
    rel_bias,
    norm_attn,
    norm_moe,
    router_weight,
    expert_in,
    expert_out,
    cotangent,
):
    own, width = inputs.shape
    seq = 4 * own
    dp = lax.axis_size("dp")
    experts = router_weight.shape[1]
    capacity = max(2, 5 * seq // (4 * experts))
    quarter = (experts // 2) * (capacity // 2)
    columns = qkv_weight.shape[2]
    heads = rel_bias.shape[1]
    t = lax.axis_index("tensor").astype(jnp.int32)
    t_one = t[None]
    x_side = t // 2
    first_expert = 2 * lax.axis_index("dp").astype(jnp.int32)
    gain_attn = norm_attn[None, :]
    gain_moe = norm_moe[None, :]
    near = lax.slice_in_dim(buckets, seq - 1 - reach, seq - 1 - reach + table, axis=0)[None, :]
    seg_col = segments.reshape(seq, 1)
    route_row = routes.reshape(1, seq)
    route_col = routes.reshape(seq, 1)

    xs = gather4(inputs)
    gs = gather4(cotangent)
    ws = gather4(out_weight)
    code_row, code_col = run(
        functools.partial(slots_body, experts, capacity),
        [shape((1, seq), jnp.int32), shape((seq, 1), jnp.int32)],
        [route_row, route_col],
        name="slots",
    )
    x_all, normed, qkv, probs, ctx = run(
        attend_body,
        [
            shape((seq, width), bf16),
            shape((seq, width), bf16),
            shape((3 * heads, seq, head_size), bf16),
            shape((heads, seq, window), bf16),
            shape((seq + seq // 2, 2 * head_size), bf16),
        ],
        [t_one, *xs, gain_attn, qkv_weight, segments, seg_col, near, rel_bias],
        smem=(0, 10),
        scratch=[pltpu.VMEM((heads, rows_q, window), f32)],
        flops=4 * 1024 * mega,
        name="attend",
    )
    g_all, g_rows = run(
        spread_body,
        [shape((seq, width), bf16), shape((quarter, width), bf16)],
        [t_one, *gs, code_row],
        smem=(0,),
        flops=512 * mega,
        name="spread",
    )
    g_rows = turn(g_rows)
    gr = gather4(g_rows)
    cs = gather4(ctx)
    h_one, h_own, rows = run(
        mid_body,
        [
            shape((seq, width), f32),
            shape((own, width), f32),
            shape((quarter, width), bf16),
        ],
        [t_one, x_all, *cs, *ws, gain_moe, code_row],
        smem=(0,),
        scratch=[pltpu.VMEM((seq, width), bf16)],
        flops=2 * 1024 * mega,
        name="mid",
    )
    rows = turn(rows)
    rs = gather4(rows)
    near_out = expert(
        x_side, first_expert + x_side, rs[0], rs[1], gr[0], gr[1], expert_in, expert_out, router_weight
    )
    far_out = expert(
        1 - x_side, first_expert + 1 - x_side, rs[2], rs[3], gr[2], gr[3],
        expert_in, expert_out, router_weight,
    )
    grad_expert_in, grad_expert_out = expert_grads(x_side, near_out[4:8], far_out[4:8])

    def back_home(near_mine, near_peer, far_mine, far_peer):
        far = far_mine + core_hop(far_peer)
        kept = near_mine + core_hop(near_peer)
        return turn(kept + x_hop(far))

    home = back_home(near_out[2], near_out[3], far_out[2], far_out[3])
    bs = gather4(home)
    fwd = back_home(near_out[0], near_out[1], far_out[0], far_out[1])
    fs = gather4(fwd)
    router_part = near_out[8] + far_out[8]
    router_part = router_part + core_hop(router_part)
    router_part = router_part + x_hop(router_part)
    small = -(-(experts + 1) // 64) * 64
    grad_h, gh_own, gctx, grad_v, early = run(
        back_body,
        [
            shape((seq, width), bf16),
            shape((own, width), f32),
            shape((heads, seq, head_size), bf16),
            shape((seq, columns), bf16),
            shape((2 * columns + small, width), bf16),
        ],
        [t_one, *bs, code_col, h_one, gain_moe, g_all, out_weight, ctx, probs, qkv, normed, router_part],
        smem=(0,),
        limit=56,
        flops=5 * 1024 * mega,
        name="back",
    )
    early_share = reduce_dp(early)
    grad_q, grad_k, late, grad_bias = run(
        attend_back_body,
        [
            shape((seq, columns), bf16),
            shape((seq, columns), bf16),
            shape((2 * columns, width), bf16),
            shape((rel_bias.shape[0], 128), f32),
        ],
        [probs, qkv, gctx, normed, near],
        scratch=[pltpu.VMEM((rows_q, table), f32)],
        limit=56,
        flops=4 * 1024 * mega,
        name="attend_back",
    )
    late_share = reduce_dp(late)
    keep, send, gain_part = run(
        input_grad_body,
        [
            shape((2 * own, width), bf16),
            shape((2 * own, width), bf16),
            shape((1, width), f32),
        ],
        [t_one, grad_q, grad_k, grad_v, qkv_weight, normed, gain_attn],
        smem=(0,),
        flops=1024 * mega,
        name="input_grad",
    )
    got = core_hop(send)
    far = x_hop(keep[own:] + got[own:])
    (grad_inputs,) = run(
        last_body,
        [shape((own, width), f32)],
        [keep[:own], got[:own], far, inputs, gain_attn, gh_own],
        name="last",
    )
    gain_part = gain_part + core_hop(gain_part)
    gain_part = gain_part + x_hop(gain_part)
    (output,) = run(
        output_body,
        [shape((own, width), bf16)],
        [t_one, *fs, code_col, h_own],
        smem=(0,),
        name="output",
    )
    bias_line = jnp.pad(
        grad_bias[:, :heads].reshape(1, -1), ((0, 0), (0, width - heads * rel_bias.shape[0]))
    )
    extra = jnp.pad(jnp.concatenate([gain_part, bias_line], axis=0), ((0, 14), (0, 0))).astype(bf16)
    early_all = gather_dp(early_share).reshape(early.shape)
    late_rows = late_share.shape[0]
    late_all = gather_dp(jnp.concatenate([late_share, extra], axis=0))
    extra = jnp.sum(late_all[:, late_rows : late_rows + 2].astype(f32), axis=0)
    late_all = late_all[:, :late_rows].reshape(late.shape)
    grad_qkv_weight = jnp.stack(
        [late_all[:columns].T, late_all[columns:].T, early_all[:columns].T]
    ).astype(f32)
    grad_out_weight = early_all[columns : 2 * columns].astype(f32)
    grad_router = early_all[2 * columns : 2 * columns + experts].T.astype(f32)
    grad_norm_moe = early_all[2 * columns + experts].astype(f32)
    grad_rel_bias = extra[1, : heads * rel_bias.shape[0]].reshape(rel_bias.shape)
    return (
        output,
        grad_inputs,
        grad_qkv_weight,
        grad_out_weight,
        grad_rel_bias,
        extra[0],
        grad_norm_moe,
        grad_router,
        grad_expert_in,
        grad_expert_out,
    )


def solution(mesh):
    placed = (
        P(("dp", "tensor"), None),
        P("dp", None),
        P(),
        P("dp", None, None),
        P(None, None, "tensor"),
        P("tensor", None),
        P(None, "tensor"),
        P(),
        P(),
        P(),
        P("dp", None, "tensor"),
        P("dp", "tensor", None),
        P(("dp", "tensor"), None),
    )
    return jax.shard_map(
        per_device,
        mesh=mesh,
        in_specs=placed,
        out_specs=(
            P(("dp", "tensor"), None),
            P(("dp", "tensor"), None),
            P(None, None, "tensor"),
            P("tensor", None),
            P(None, "tensor"),
            P(),
            P(),
            P(),
            P("dp", None, "tensor"),
            P("dp", "tensor", None),
        ),
        check_vma=False,
    )
```

```python
import functools

import jax
import jax.numpy as jnp
from jax import lax
from jax.experimental import pallas as pl
from jax.experimental.pallas import tpu as pltpu
from jax.sharding import PartitionSpec as P

epsilon = 1e-06
negative = -1000000000.0
bf16 = jnp.bfloat16
f32 = jnp.float32
reach = 256
rows_q = 128
window = rows_q + 2 * reach
table = window + rows_q
head_size = 64
mega = 1024 * 1024

core_pairs = [(0, 1), (1, 0), (2, 3), (3, 2)]
x_pairs = [(0, 2), (2, 0), (1, 3), (3, 1)]


def core_hop(value):
    return lax.ppermute(value, "tensor", core_pairs)


def x_hop(value):
    return lax.ppermute(value, "tensor", x_pairs)


def after(value, *deps):
    return lax.optimization_barrier((value, *deps))[0]


def gather4(value, *deps):
    other = x_hop(value)
    if deps:
        other = after(other, *deps)
    return value, core_hop(value), other, core_hop(other)


def dot(a, b, dims):
    return lax.dot_general(a, b, (dims, ((), ())), preferred_element_type=f32)


def mm(a, b):
    return dot(a, b, ((1,), (0,)))


def mm_nt(a, b):
    return dot(a, b, ((1,), (1,)))


def mm_tn(a, b):
    return dot(a, b, ((0,), (0,)))


def shape(dims, kind):
    return jax.ShapeDtypeStruct(dims, kind)


class Loaded:
    def __init__(self, source, buffer, sem):
        self.buffer = buffer
        self.copy = pltpu.make_async_copy(source, buffer, sem)
        self.copy.start()
        self.here = False
        self.shape, self.dtype = buffer.shape, buffer.dtype

    def wait(self):
        if not self.here:
            self.copy.wait()
            self.here = True

    def __getitem__(self, place):
        self.wait()
        return self.buffer[place]


class Stored:
    def __init__(self, target, buffer, sem):
        self.buffer = buffer
        self.copy = pltpu.make_async_copy(buffer, target, sem)
        self.gone = False
        self.shape, self.dtype = buffer.shape, buffer.dtype

    def flush(self):
        if not self.gone:
            self.copy.start()
            self.gone = True

    def __getitem__(self, place):
        return self.buffer[place]

    def __setitem__(self, place, value):
        self.buffer[place] = value


def run(
    body, outs, args, smem=(), loads=(), stores=(), hbm=(), hbm_outs=(), deps=(), aliases=None,
    scratch=(), us=2, name=None,
):
    args = list(args)
    if deps:
        args[0] = after(args[0], *deps)
    n_in, n_out, n_own = len(args), len(outs), len(scratch)

    def inner(*refs):
        ins = list(refs[:n_in])
        results = list(refs[n_in : n_in + n_out])
        own = refs[n_in + n_out : n_in + n_out + n_own]
        rest = refs[n_in + n_out + n_own :]
        buffers, sems = rest[:-1], rest[-1]
        for n, i in enumerate(loads):
            ins[i] = Loaded(ins[i], buffers[n], sems.at[n])
        for n, i in enumerate(stores, len(loads)):
            results[i] = Stored(results[i], buffers[n], sems.at[n])
        body(*ins, *results, *own)
        for i in loads:
            ins[i].wait()
        for i in stores:
            results[i].flush()
        for i in stores:
            results[i].copy.wait()

    def space(i):
        if i in smem:
            return pltpu.SMEM
        return pltpu.HBM if i in hbm or i in loads else pltpu.VMEM

    for i in (*loads, *hbm):
        if i < n_in:
            args[i] = pltpu.with_memory_space_constraint(args[i], pltpu.HBM)
    kinds = [
        pltpu.HBM(o.shape, o.dtype) if i in hbm_outs or i in stores else o
        for i, o in enumerate(outs)
    ]
    staged = [pltpu.VMEM(args[i].shape, args[i].dtype) for i in loads]
    staged += [pltpu.VMEM(outs[i].shape, outs[i].dtype) for i in stores]
    return pl.pallas_call(
        inner,
        out_shape=kinds,
        in_specs=[pl.BlockSpec(memory_space=space(i)) for i in range(n_in)],
        out_specs=[
            pl.BlockSpec(
                memory_space=pltpu.HBM if i in hbm_outs or i in stores else pltpu.VMEM
            )
            for i in range(n_out)
        ],
        scratch_shapes=[
            *scratch, *staged, pltpu.SemaphoreType.DMA((max(1, len(staged)),))
        ],
        input_output_aliases=aliases or {},
        compiler_params=pltpu.CompilerParams(vmem_limit_bytes=44 * mega),
        cost_estimate=pl.CostEstimate(
            flops=int(us * 1.1e9), bytes_accessed=mega // 4, transcendentals=0
        ),
        name=name,
    )(*args)


def as_column(row):
    wide = jnp.broadcast_to(row.astype(f32), (8, row.shape[1]))
    return wide.T[:, 0:1].astype(jnp.int32)


def slots_body(
    experts, capacity, row_ref, seg_row, near, bias, code_row, code_col, seg_col, tile
):
    seq = row_ref.shape[1]
    half = capacity // 2
    quarter = (experts // 2) * half
    first = lax.broadcasted_iota(jnp.int32, (seq, seq), 0)
    second = lax.broadcasted_iota(jnp.int32, (seq, seq), 1)
    route = row_ref[...]
    chosen = route == lax.broadcasted_iota(jnp.int32, (experts, seq), 0)
    count = mm(chosen.astype(bf16), (first < second).astype(bf16))
    slot = jnp.sum(jnp.where(chosen, count, 0.0), axis=0, keepdims=True).astype(jnp.int32)
    upper = jnp.where(slot >= half, 1, 0)
    code = (2 * (route & 1) + upper) * quarter + (route >> 1) * half + slot - half * upper
    code_row[...] = code
    code_col[...] = as_column(code)
    seg_col[...] = as_column(seg_row[...])
    bucket = near[...]
    for h in range(bias.shape[0]):
        line = jnp.zeros(bucket.shape, f32)
        for b in range(bias.shape[1]):
            line = jnp.where(bucket == b, bias[h, b], line)
        wide = jnp.broadcast_to(line, (rows_q, table))
        tile[h] = pltpu.roll(wide, 0, 1, stride=1, stride_axis=0)[:, :window]


def span(i0, seq):
    start = max(0, i0 - reach)
    end = min(seq, i0 + rows_q + reach)
    return start, end, start - (i0 - reach)


def masked_probs(score, same, tile):
    score = jnp.where(same, score + tile, negative)
    score = jnp.exp(score - jnp.max(score, axis=1, keepdims=True))
    return (score * (1.0 / jnp.sum(score, axis=1, keepdims=True))).astype(bf16)


def split_heads(full, out):
    for h in range(out.shape[0]):
        out[h] = full[:, h * head_size : (h + 1) * head_size].astype(bf16)


def attend_body(
    t_ref, x0, x1, x2, x3, gain, weight, seg_row, seg_col, tile,
    x_all, normed, ctx, query, key, value,
):
    t = t_ref[0]
    own = x0.shape[0]
    seq = 4 * own
    heads = tile.shape[0]
    for k, ref in enumerate((x0, x1, x2, x3)):
        at = pl.ds(pl.multiple_of((t ^ k) * own, own), own)
        x = ref[...]
        x_all[at, :] = x
        x = x.astype(f32)
        inv = lax.rsqrt(jnp.mean(x * x, axis=1, keepdims=True) + epsilon)
        normed[at, :] = (x * inv * gain[...]).astype(bf16)
    x_all.flush()
    normed.flush()
    split_heads(mm_nt(normed[...], weight[0]), query)
    key[...] = mm_nt(weight[1], normed[...]).astype(bf16)
    split_heads(mm_nt(normed[...], weight[2]), value)
    for i0 in range(0, seq, rows_q):
        start, end, off = span(i0, seq)
        same = seg_col[i0 : i0 + rows_q, :] == seg_row[:, start:end]
        parts = []
        for h in range(heads):
            score = mm(
                query[h, i0 : i0 + rows_q, :],
                key[h * head_size : (h + 1) * head_size, start:end],
            )
            prob = masked_probs(score, same, tile[h, :, off : off + end - start])
            parts.append(mm(prob, value[h, start:end, :]).astype(bf16))
        ctx[i0 : i0 + rows_q, :] = jnp.concatenate(parts[:2], axis=1)
        lane = 0 if i0 < seq // 2 else head_size
        at = seq + i0 % (seq // 2)
        ctx[at : at + rows_q, lane : lane + head_size] = parts[2]


def prepare_body(
    normed, weight, seg_row, seg_col, tile, ctx,
    probs, key_rows, query_cols, value_cols, ctx_cols, query, key,
):
    seq = normed.shape[0]
    heads = tile.shape[0]
    columns = heads * head_size
    full = mm_nt(normed[...], weight[0])
    split_heads(full, query)
    query_cols[...] = full.T.astype(bf16)
    full = mm_nt(normed[...], weight[1])
    split_heads(full, key_rows)
    key[...] = full.T.astype(bf16)
    value_cols[...] = mm_nt(weight[2], normed[...]).astype(bf16)
    for i0 in range(0, seq, rows_q):
        start, end, off = span(i0, seq)
        same = seg_col[i0 : i0 + rows_q, :] == seg_row[:, start:end]
        for h in range(heads):
            score = mm(
                query[h, i0 : i0 + rows_q, :],
                key[h * head_size : (h + 1) * head_size, start:end],
            )
            probs[h, i0 : i0 + rows_q, 0 : end - start] = masked_probs(
                score, same, tile[h, :, off : off + end - start]
            )
    pair = 2 * head_size
    ctx_cols[0:pair, :] = ctx[0:seq, :].T
    last = ctx[seq:, :].T
    ctx_cols[pair:columns, 0 : seq // 2] = last[0:head_size, :]
    ctx_cols[pair:columns, seq // 2 :] = last[head_size:, :]


def third(ctx, r0, rows, seq):
    lane = 0 if r0 < seq // 2 else head_size
    at = seq + r0 % (seq // 2)
    return ctx[at : at + rows, lane : lane + head_size]


def mid_body(
    t_ref, x_all, c0, c1, c2, c3, w0, w1, w2, w3, gain, code_row,
    h_one, h_own, rows, normed,
):
    t = t_ref[0]
    seq = x_all.shape[0]
    own = seq // 4
    quarter = rows.shape[0]
    ctxs = (c0, c1, c2, c3)
    weights = (w0, w1, w2, w3)
    pair = 2 * head_size
    packed = [
        jnp.concatenate([weights[2 * i][0:pair, :], weights[2 * i + 1][0:pair, :]], axis=0)
        for i in range(2)
    ]
    last = jnp.concatenate([w[pair : pair + head_size, :] for w in weights], axis=0)
    for r0 in range(0, seq, own):
        at = slice(r0, r0 + own)
        total = x_all[at, :].astype(f32)
        for i in range(2):
            left = jnp.concatenate([ctxs[2 * i][at, :], ctxs[2 * i + 1][at, :]], axis=1)
            total = total + mm(left, packed[i])
        left = jnp.concatenate([third(c, r0, own, seq) for c in ctxs], axis=1)
        total = total + mm(left, last)
        h_one[at, :] = total
        inv = lax.rsqrt(jnp.mean(total * total, axis=1, keepdims=True) + epsilon)
        normed[at, :] = (total * inv * gain[...]).astype(bf16)
    h_own[...] = h_one[pl.ds(pl.multiple_of(t * own, own), own), :]
    h_one.flush()
    h_own.flush()
    place = lax.broadcasted_iota(jnp.int32, (quarter, seq), 0) + t * quarter
    rows[...] = mm((place == code_row[...]).astype(bf16), normed[...]).astype(bf16)


def spread_body(t_ref, g0, g1, g2, g3, code_row, g_all, rows):
    t = t_ref[0]
    own = g0.shape[0]
    quarter = rows.shape[0]
    for k, ref in enumerate((g0, g1, g2, g3)):
        g_all[pl.ds(pl.multiple_of((t ^ k) * own, own), own), :] = ref[...]
    g_all.flush()
    place = lax.broadcasted_iota(jnp.int32, (quarter, g_all.shape[0]), 0) + t * quarter
    rows[...] = mm((place == code_row[...]).astype(bf16), g_all[...]).astype(bf16)


gelu_scale = 0.7978845608028654
gelu_cubic = 0.044715


def expert_body(
    e_ref, r0, r1, g0, g1, router, w_in_all, w_out_all,
    back0, back1, grad0, grad1, hidden_out, gated_out, pre_out, router_out,
    w_in, w_out, sem,
):
    load_in = pltpu.make_async_copy(w_in_all.at[e_ref[0]], w_in, sem.at[0])
    load_out = pltpu.make_async_copy(w_out_all.at[e_ref[0]], w_out, sem.at[1])
    load_in.start()
    load_out.start()
    half = r0.shape[0]
    total = jnp.zeros(router_out.shape, f32)
    for i, (r, g, back, grad) in enumerate(((r0, g0, back0, grad0), (r1, g1, back1, grad1))):
        at = slice(i * half, (i + 1) * half)
        rows = r[...]
        cot = g[...].astype(f32)
        logits = mm_nt(rows, router[...])
        logits = jnp.exp(logits - jnp.max(logits, axis=1, keepdims=True))
        prob = logits / jnp.sum(logits, axis=1, keepdims=True)
        mine = lax.broadcasted_iota(jnp.int32, prob.shape, 1) == e_ref[1]
        gate = jnp.sum(jnp.where(mine, prob, 0.0), axis=1, keepdims=True)
        gated = (gate * cot).astype(bf16)
        gated_out[at, :] = gated
        if i == 0:
            load_in.wait()
        pre = mm(rows, w_in[...])
        square = pre * pre
        inner = jnp.tanh(gelu_scale * pre * (1.0 + gelu_cubic * square))
        half_up = 0.5 + 0.5 * inner
        hidden = (pre * half_up).astype(bf16)
        hidden_out[at, :] = hidden
        slope = half_up + (0.5 * gelu_scale) * pre * (1.0 - inner * inner) * (
            1.0 + (3.0 * gelu_cubic) * square
        )
        if i == 0:
            load_out.wait()
        part = mm(hidden, w_out[...])
        back[...] = (gate * part).astype(bf16)
        grad_gate = jnp.sum(cot * part, axis=1, keepdims=True)
        grad_pre = (mm_nt(gated, w_out[...]) * slope).astype(bf16)
        pre_out[at, :] = grad_pre
        grad_logits = (gate * grad_gate * (jnp.where(mine, 1.0, 0.0) - prob)).astype(bf16)
        grad[...] = (mm_nt(grad_pre, w_in[...]) + mm(grad_logits, router[...])).astype(bf16)
        if i == 1:
            hidden_out.flush()
            gated_out.flush()
            pre_out.flush()
        total = total + mm_tn(grad_logits, rows)
    router_out[...] = total


def expert(scalars, r0, r1, g0, g1, router, w_in, w_out):
    half, width = r0.shape
    hidden = w_in.shape[2]
    rows = 2 * half
    return run(
        expert_body,
        [shape((half, width), bf16)] * 4
        + [
            shape((rows, hidden), bf16),
            shape((rows, width), bf16),
            shape((rows, hidden), bf16),
            shape(router.shape, f32),
        ],
        [scalars, r0, r1, g0, g1, router, w_in, w_out],
        smem=(0,),
        hbm=(6, 7),
        stores=(0, 1, 2, 3, 4, 5, 6),
        scratch=[
            pltpu.VMEM((width, hidden), bf16),
            pltpu.VMEM((hidden, width), bf16),
            pltpu.SemaphoreType.DMA((2,)),
        ],
        us=7,
        name="expert",
    )


def expert_grad_body(first, e_ref, r0, r1, hidden, gated, pre, *refs):
    d_in, d_out, sum_in, sum_out, sem = refs[-5:]
    rows = jnp.concatenate([r0[...], r1[...]], axis=0)
    sum_in[...] = mm_tn(rows, pre[...])
    store_in = pltpu.make_async_copy(sum_in, d_in.at[e_ref[0]], sem.at[0])
    store_in.start()
    sum_out[...] = mm_tn(hidden[...], gated[...])
    store_out = pltpu.make_async_copy(sum_out, d_out.at[e_ref[0]], sem.at[1])
    store_out.start()
    store_in.wait()
    store_out.wait()


def expert_grads(scalars, r0, r1, hidden, gated, pre, so_far=(), deps=()):
    columns, width = hidden.shape[1], gated.shape[1]
    return run(
        functools.partial(expert_grad_body, not so_far),
        [shape((2, width, columns), f32), shape((2, columns, width), f32)],
        [scalars, r0, r1, hidden, gated, pre, *so_far],
        smem=(0,),
        loads=(3, 4, 5),
        hbm=(6, 7),
        hbm_outs=(0, 1),
        aliases={6: 0, 7: 1} if so_far else None,
        deps=deps,
        scratch=[
            pltpu.VMEM((width, columns), f32),
            pltpu.VMEM((columns, width), f32),
            pltpu.SemaphoreType.DMA((2,)),
        ],
        us=4,
        name="expert_grads",
    )


def back_body(
    t_ref, b0, b1, b2, b3, code_col, h_one, gain, g_all, weight, ctx_cols, probs, normed, router,
    h_own, gctx, grad_v, early, grad_h, sums,
):
    t = t_ref[0]
    seq, width = h_one.shape
    own = seq // 4
    quarter = b0.shape[0]
    heads = gctx.shape[0]
    columns = heads * head_size
    sum_gain = jnp.zeros((1, width), f32)
    for r0 in range(0, seq, own):
        at = slice(r0, r0 + own)
        total = jnp.zeros((own, width), f32)
        for k, ref in enumerate((b0, b1, b2, b3)):
            place = lax.broadcasted_iota(jnp.int32, (own, quarter), 1) + (t ^ k) * quarter
            total = total + mm((place == code_col[at, :]).astype(bf16), ref[...])
        h = h_one[at, :]
        inv = lax.rsqrt(jnp.mean(h * h, axis=1, keepdims=True) + epsilon)
        n2 = h * inv
        sum_gain = sum_gain + jnp.sum(total * n2, axis=0, keepdims=True)
        a = total * gain[...]
        mean = jnp.mean(a * n2, axis=1, keepdims=True)
        full = g_all[at, :].astype(f32) + inv * (a - n2 * mean)
        grad_h[at, :] = full.astype(bf16)

        @pl.when(t * own == r0)
        def _():
            h_own[...] = full

    wide = mm_nt(grad_h[...], weight[...])
    split_heads(wide, gctx)
    cols = wide.T.astype(bf16)
    sums[...] = jnp.zeros(sums.shape, f32)
    for h in range(heads):
        at = slice(h * head_size, (h + 1) * head_size)
        for i0 in range(0, seq, rows_q):
            start, end, _ = span(i0, seq)
            sums[at, start:end] += mm(
                cols[at, i0 : i0 + rows_q], probs[h, i0 : i0 + rows_q, 0 : end - start]
            )
    grad_v[...] = sums[...].astype(bf16)
    gctx.flush()
    h_own.flush()
    grad_v.flush()
    early[0:columns, :] = mm(grad_v[...], normed[...]).astype(bf16)
    early[columns : 2 * columns, :] = mm(ctx_cols[...], grad_h[...]).astype(bf16)
    rest = jnp.concatenate([router[...], sum_gain], axis=0)
    spare = early.shape[0] - 2 * columns - rest.shape[0]
    rest = jnp.concatenate([rest, jnp.zeros((spare, width), f32)], axis=0)
    early[2 * columns :, :] = rest.astype(bf16)


def attend_back_body(
    probs, key_rows, query_cols, value_cols, gctx, normed, near,
    grad_q, grad_k, late, grad_bias, spill, sums,
):
    heads, seq, _ = gctx.shape
    columns = heads * head_size
    buckets = grad_bias.shape[0]
    places = lax.broadcasted_iota(jnp.int32, (buckets, 128), 1)
    found = jnp.zeros((buckets, 128), f32)
    sums[...] = jnp.zeros(sums.shape, f32)
    for h in range(heads):
        cols = slice(h * head_size, (h + 1) * head_size)
        spill[...] = jnp.zeros(spill.shape, f32)
        for i0 in range(0, seq, rows_q):
            start, end, off = span(i0, seq)
            at = slice(i0, i0 + rows_q)
            prob = probs[h, at, 0 : end - start].astype(f32)
            grad = mm(gctx[h, at, :], value_cols[cols, start:end])
            both = prob * grad
            delta = jnp.sum(both, axis=1, keepdims=True)
            score = both - prob * delta
            spill[:, off : off + end - start] += score
            score = score.astype(bf16)
            grad_q[at, cols] = mm(score, key_rows[h, start:end, :]).astype(bf16)
            sums[cols, start:end] += mm(query_cols[cols, at], score)
        strip = jnp.zeros((8, table), f32)
        for a in range(0, rows_q, 8):
            strip = strip + pltpu.roll(spill[a : a + 8, :], (table - a) % table, 1)
        line = lax.broadcasted_iota(jnp.int32, strip.shape, 0)
        for bit in (1, 2, 4):
            strip = jnp.where((line & bit) != 0, pltpu.roll(strip, table - bit, 1), strip)
        strip = jnp.sum(strip, axis=0, keepdims=True)
        chosen = near[...] == lax.broadcasted_iota(jnp.int32, (buckets, table), 0)
        per = jnp.sum(jnp.where(chosen, strip, 0.0), axis=1, keepdims=True)
        found = found + jnp.where(places == h, per, 0.0)
    grad_bias[...] = found
    grad_k[...] = sums[...].astype(bf16)
    grad_q.flush()
    grad_k.flush()
    late[0:columns, :] = mm_tn(grad_q[...], normed[...]).astype(bf16)
    late[columns : 2 * columns, :] = mm(grad_k[...], normed[...]).astype(bf16)


def input_grad_body(t_ref, grad_q, grad_k, grad_v, weight, normed, gain, keep, send, sums):
    t = t_ref[0]
    seq, width = normed.shape
    own = seq // 4
    total_gain = jnp.zeros((1, width), f32)
    for k in range(4):
        at = pl.ds(pl.multiple_of((t ^ k) * own, own), own)
        part = mm(grad_q[at, :], weight[0])
        part = part + mm_tn(grad_k[:, at], weight[1])
        part = part + mm_tn(grad_v[:, at], weight[2])
        total_gain = total_gain + jnp.sum(part * normed[at, :].astype(f32), axis=0, keepdims=True)
        out = keep if k in (0, 2) else send
        out[(k // 2) * own : (k // 2 + 1) * own, :] = part.astype(bf16)
    sums[...] = total_gain / gain[...]


def share_body(copies, got, out):
    rows = got.shape[0] // copies
    full = got[...].astype(f32)
    total = full[0:rows]
    for i in range(1, copies):
        total = total + full[i * rows : (i + 1) * rows]
    out[...] = jnp.concatenate([total] * copies, axis=0).astype(bf16)


def late_share_body(copies, got, sums, grad_bias, out):
    rows = got.shape[0] // copies
    width = got.shape[1]
    heads = 3
    full = got[...].astype(f32)
    total = full[0:rows]
    for i in range(1, copies):
        total = total + full[i * rows : (i + 1) * rows]
    found = grad_bias[...]
    lanes = found.shape[1]
    found = jnp.concatenate([found, jnp.zeros((lanes - found.shape[0], lanes), f32)], axis=0).T
    found = jnp.concatenate([found[0:8], jnp.zeros((8, width - lanes), f32)], axis=1)
    line = lax.broadcasted_iota(jnp.int32, found.shape, 0)
    first = jnp.where(line == 0, sums[...], 0.0)
    total = jnp.concatenate([total, found, first], axis=0)
    out[...] = jnp.concatenate([total] * copies, axis=0).astype(bf16)


def finish_body(copies, late_rows, early, late, qkv, out, bias, gain_attn, gain_moe, router):
    columns = out.shape[0]
    experts = router.shape[0]
    first = early[...].astype(f32)
    qkv[2] = first[0:columns]
    out[...] = first[columns : 2 * columns]
    router[...] = first[2 * columns : 2 * columns + experts]
    gain_moe[...] = first[2 * columns + experts : 2 * columns + experts + 1]
    second = late[...].astype(f32)
    step = second.shape[0] // copies
    pieces = [second[i * step : i * step + late_rows] for i in range(copies)]
    pieces = jnp.concatenate(pieces, axis=0)
    qkv[0] = pieces[0:columns]
    qkv[1] = pieces[columns : 2 * columns]
    small = second[late_rows : late_rows + 16]
    for i in range(1, copies):
        small = small + second[i * step + late_rows : i * step + late_rows + 16]
    bias[...] = small[0 : bias.shape[0], 0 : bias.shape[1]]
    gain_attn[...] = small[8:9]


def last_body(kept, got, far, x_ref, gain, h_own, grad):
    total = kept[...].astype(f32) + got[...].astype(f32) + far[...].astype(f32)
    x = x_ref[...].astype(f32)
    inv = lax.rsqrt(jnp.mean(x * x, axis=1, keepdims=True) + epsilon)
    n1 = x * inv
    a = total * gain[...]
    grad[...] = h_own[...] + inv * (a - n1 * jnp.mean(a * n1, axis=1, keepdims=True))


def output_body(t_ref, f0, f1, f2, f3, code_col, h_own, out):
    t = t_ref[0]
    own = h_own.shape[0]
    quarter = f0.shape[0]
    total = h_own[...]
    codes = code_col[pl.ds(pl.multiple_of(t * own, own), own), :]
    for k, ref in enumerate((f0, f1, f2, f3)):
        place = lax.broadcasted_iota(jnp.int32, (own, quarter), 1) + (t ^ k) * quarter
        total = total + mm((place == codes).astype(bf16), ref[...])
    out[...] = total.astype(bf16)


def turn(value):
    return lax.all_to_all(value, "dp", split_axis=0, concat_axis=0, tiled=True)


def per_device(
    inputs,
    segments,
    buckets,
    routes,
    qkv_weight,
    out_weight,
    rel_bias,
    norm_attn,
    norm_moe,
    router_weight,
    expert_in,
    expert_out,
    cotangent,
):
    own, width = inputs.shape
    seq = 4 * own
    dp = lax.axis_size("dp")
    experts = router_weight.shape[1]
    capacity = max(2, 5 * seq // (4 * experts))
    quarter = (experts // 2) * (capacity // 2)
    heads = rel_bias.shape[1]
    columns = heads * head_size
    t_one = lax.axis_index("tensor").astype(jnp.int32)[None]
    x_side = t_one >> 1
    first_expert = 2 * lax.axis_index("dp").astype(jnp.int32)
    near_expert = jnp.concatenate([x_side, first_expert + x_side])
    far_expert = jnp.concatenate([1 - x_side, first_expert + 1 - x_side])
    inputs, t_one, near_expert, far_expert = lax.optimization_barrier(
        (inputs, t_one, near_expert, far_expert)
    )
    gain_attn = norm_attn[None, :]
    gain_moe = norm_moe[None, :]
    near = lax.slice_in_dim(buckets, seq - 1 - reach, seq - 1 - reach + table, axis=0)[None, :]
    weight = jnp.swapaxes(qkv_weight, 1, 2)
    router = router_weight.T

    code_row, code_col, seg_col, tile = run(
        functools.partial(slots_body, experts, capacity),
        [
            shape((1, seq), jnp.int32),
            shape((seq, 1), jnp.int32),
            shape((seq, 1), jnp.int32),
            shape((heads, rows_q, window), f32),
        ],
        [routes.reshape(1, seq), segments, near, rel_bias.T],
        smem=(3,),
        us=2,
        stores=(3,),
        name="slots",
    )
    xs = gather4(inputs, code_row)
    x_all, normed, ctx = run(
        attend_body,
        [
            shape((seq, width), bf16),
            shape((seq, width), bf16),
            shape((seq + seq // 2, 2 * head_size), bf16),
        ],
        [t_one, *xs, gain_attn, weight, segments, seg_col, tile],
        smem=(0,),
        scratch=[
            pltpu.VMEM((heads, seq, head_size), bf16),
            pltpu.VMEM((columns, seq), bf16),
            pltpu.VMEM((heads, seq, head_size), bf16),
        ],
        us=10,
        loads=(1, 6, 9),
        stores=(0, 1, 2),
        name="attend",
    )
    gs = gather4(cotangent, ctx)
    ws = gather4(out_weight, ctx)
    g_all, g_rows = run(
        spread_body,
        [shape((seq, width), bf16), shape((quarter, width), bf16)],
        [t_one, *gs, code_row],
        smem=(0,),
        us=2,
        loads=(1,),
        stores=(0,),
        name="spread",
    )
    g_got = turn(g_rows)
    cs = gather4(ctx, g_rows)
    h_one, h_own, rows = run(
        mid_body,
        [
            shape((seq, width), f32),
            shape((own, width), f32),
            shape((quarter, width), bf16),
        ],
        [t_one, x_all, *cs, *ws, gain_moe, code_row],
        smem=(0,),
        scratch=[pltpu.VMEM((seq, width), bf16)],
        us=4,
        loads=(1, 2, 6),
        stores=(0, 1),
        name="mid",
    )
    probs, key_rows, query_cols, value_cols, ctx_cols = run(
        prepare_body,
        [
            shape((heads, seq, window), bf16),
            shape((heads, seq, head_size), bf16),
            shape((columns, seq), bf16),
            shape((columns, seq), bf16),
            shape((columns, seq), bf16),
        ],
        [normed, weight, segments, seg_col, tile, ctx],
        deps=[rows],
        scratch=[
            pltpu.VMEM((heads, seq, head_size), bf16),
            pltpu.VMEM((columns, seq), bf16),
        ],
        us=10,
        loads=(0, 1, 4, 5),
        stores=(0, 1, 2, 3, 4),
        name="prepare",
    )
    gr = gather4(g_got, probs)
    row_got = after(turn(rows), probs)
    near_rows = (row_got, core_hop(row_got))
    near_out = expert(near_expert, *near_rows, gr[0], gr[1], router, expert_in, expert_out)
    far_mine = after(x_hop(row_got), near_out[0])
    far_rows = (far_mine, core_hop(far_mine))
    far_out = expert(far_expert, *far_rows, gr[2], gr[3], router, expert_in, expert_out)
    far = far_out[2] + core_hop(far_out[3])
    weight_grads = expert_grads(near_expert, *near_rows, *near_out[4:7], deps=[far])
    far = after(x_hop(far), weight_grads[0])
    kept = near_out[2] + core_hop(near_out[3]) + far
    home = turn(kept)
    far = after(far_out[0], kept) + core_hop(far_out[1])
    weight_grads = expert_grads(
        far_expert, *far_rows, *far_out[4:7], so_far=weight_grads, deps=[far]
    )
    home = after(home, weight_grads[0])
    fwd = after(near_out[0], home) + core_hop(near_out[1]) + x_hop(far)
    bs = gather4(home, fwd)
    fwd = turn(fwd)
    router_part = near_out[7] + far_out[7]
    router_part = router_part + core_hop(router_part)
    router_part = router_part + x_hop(router_part)
    small = -(-(experts + 1) // 64) * 64
    gh_own, gctx, grad_v, early = run(
        back_body,
        [
            shape((own, width), f32),
            shape((heads, seq, head_size), bf16),
            shape((columns, seq), bf16),
            shape((2 * columns + small, width), bf16),
        ],
        [
            t_one, *bs, code_col, h_one, gain_moe, g_all, out_weight, ctx_cols, probs, normed,
            router_part,
        ],
        smem=(0,),
        scratch=[pltpu.VMEM((seq, width), bf16), pltpu.VMEM((columns, seq), f32)],
        us=12,
        loads=(6, 8, 9, 10, 11, 12),
        stores=(0, 1, 2),
        name="back",
    )
    early_got = turn(early)
    grad_q, grad_k, late, grad_bias = run(
        attend_back_body,
        [
            shape((seq, columns), bf16),
            shape((columns, seq), bf16),
            shape((2 * columns, width), bf16),
            shape((rel_bias.shape[0], 128), f32),
        ],
        [probs, key_rows, query_cols, value_cols, gctx, normed, near],
        deps=[fwd],
        scratch=[pltpu.VMEM((rows_q, table), f32), pltpu.VMEM((columns, seq), f32)],
        us=10,
        loads=(0, 1, 2, 3, 4, 5),
        stores=(0, 1),
        name="attend_back",
    )
    fs = gather4(fwd, late)
    late_got = turn(late)
    (early_wide,) = run(
        functools.partial(share_body, dp),
        [shape(early_got.shape, bf16)],
        [early_got],
        us=1,
        name="share_early",
    )
    early_all = turn(early_wide)
    keep, send, gain_part = run(
        input_grad_body,
        [
            shape((2 * own, width), bf16),
            shape((2 * own, width), bf16),
            shape((1, width), f32),
        ],
        [t_one, grad_q, grad_k, grad_v, weight, normed, gain_attn],
        smem=(0,),
        deps=[early_wide],
        us=2,
        loads=(1, 2, 3, 4, 5),
        name="input_grad",
    )
    got = core_hop(send)
    far = x_hop(keep[own:] + got[own:])
    gain_part = gain_part + core_hop(gain_part)
    gain_part = gain_part + x_hop(gain_part)
    late_rows = late_got.shape[0] // dp
    (late_wide,) = run(
        functools.partial(late_share_body, dp),
        [shape((dp * (late_rows + 16), width), bf16)],
        [late_got, gain_part, grad_bias],
        us=1,
        name="share_late",
    )
    late_all = turn(late_wide)
    (grad_inputs,) = run(
        last_body,
        [shape((own, width), f32)],
        [keep[:own], got[:own], far, inputs, gain_attn, gh_own],
        loads=(3, 5),
        name="last",
    )
    (output,) = run(
        output_body,
        [shape((own, width), bf16)],
        [t_one, *fs, code_col, h_own],
        smem=(0,),
        loads=(6,),
        name="output",
    )
    qkv_grad, out_grad, bias_grad, gain_attn_grad, gain_moe_grad, router_grad = run(
        functools.partial(finish_body, dp, late_rows),
        [
            shape((3, columns, width), f32),
            shape((columns, width), f32),
            shape((heads, rel_bias.shape[0]), f32),
            shape((1, width), f32),
            shape((1, width), f32),
            shape((experts, width), f32),
        ],
        [early_all, late_all],
        us=2,
        name="finish",
    )
    return (
        output,
        grad_inputs,
        jnp.swapaxes(qkv_grad, 1, 2),
        out_grad,
        bias_grad.T,
        gain_attn_grad[0],
        gain_moe_grad[0],
        router_grad.T,
        *weight_grads,
    )


def solution(mesh):
    placed = (
        P(("dp", "tensor"), None),
        P("dp", None),
        P(),
        P("dp", None, None),
        P(None, None, "tensor"),
        P("tensor", None),
        P(None, "tensor"),
        P(),
        P(),
        P(),
        P("dp", None, "tensor"),
        P("dp", "tensor", None),
        P(("dp", "tensor"), None),
    )
    return jax.shard_map(
        per_device,
        mesh=mesh,
        in_specs=placed,
        out_specs=(
            P(("dp", "tensor"), None),
            P(("dp", "tensor"), None),
            P(None, None, "tensor"),
            P("tensor", None),
            P(None, "tensor"),
            P(),
            P(),
            P(),
            P("dp", None, "tensor"),
            P("dp", "tensor", None),
        ),
        check_vma=False,
    )
```

```python
import functools

import jax
import jax.numpy as jnp
from jax import lax
from jax.experimental import pallas as pl
from jax.experimental.pallas import tpu as pltpu
from jax.sharding import PartitionSpec as P

epsilon = 1e-06
negative = -1000000000.0
bf16 = jnp.bfloat16
f32 = jnp.float32
reach = 256
rows_q = 128
window = rows_q + 2 * reach
table = window + rows_q
head_size = 64
mega = 1024 * 1024

core_pairs = [(0, 1), (1, 0), (2, 3), (3, 2)]
x_pairs = [(0, 2), (2, 0), (1, 3), (3, 1)]


def core_hop(value):
    return lax.ppermute(value, "tensor", core_pairs)


def x_hop(value):
    return lax.ppermute(value, "tensor", x_pairs)


def after(value, *deps):
    return lax.optimization_barrier((value, *deps))[0]


def gather4(value, *deps):
    other = x_hop(value)
    if deps:
        other = after(other, *deps)
    return value, core_hop(value), other, core_hop(other)


def dot(a, b, dims):
    return lax.dot_general(a, b, (dims, ((), ())), preferred_element_type=f32)


def mm(a, b):
    return dot(a, b, ((1,), (0,)))


def mm_nt(a, b):
    return dot(a, b, ((1,), (1,)))


def mm_tn(a, b):
    return dot(a, b, ((0,), (0,)))


def shape(dims, kind):
    return jax.ShapeDtypeStruct(dims, kind)


class Loaded:
    def __init__(self, source, buffer, sems, axis=0):
        self.buffer, self.axis = buffer, axis
        self.shape, self.dtype = buffer.shape, buffer.dtype
        count = len(sems)
        self.step = self.shape[axis] // count
        self.copies = []
        for i, sem in enumerate(sems):
            at = self.place(i) if count > 1 else ()
            part = (source.at[at], buffer.at[at]) if at else (source, buffer)
            self.copies.append(pltpu.make_async_copy(*part, sem))
            self.copies[-1].start()
        self.here = [False] * count

    def place(self, i):
        return (slice(None),) * self.axis + (pl.ds(i * self.step, self.step),)

    def piece(self, i):
        if not self.here[i]:
            self.copies[i].wait()
            self.here[i] = True

    def wait(self):
        for i in range(len(self.copies)):
            self.piece(i)

    def __getitem__(self, place):
        self.wait()
        return self.buffer[place]


class Stored:
    def __init__(self, target, buffer, sem):
        self.buffer, self.target, self.sem = buffer, target, sem
        self.shape, self.dtype = buffer.shape, buffer.dtype
        self.gone = 0

    def flush(self, first=0, rows=None):
        rows = self.shape[0] if rows is None else rows
        at = pl.ds(first, rows)
        pltpu.make_async_copy(self.buffer.at[at], self.target.at[at], self.sem).start()
        self.gone += rows

    def close(self):
        if not self.gone:
            self.flush()

    def wait(self):
        pltpu.make_async_copy(self.buffer, self.target, self.sem).wait()

    def __getitem__(self, place):
        return self.buffer[place]

    def __setitem__(self, place, value):
        self.buffer[place] = value


def run(
    body, outs, args, smem=(), loads=(), stores=(), hbm=(), hbm_outs=(), deps=(), aliases=None,
    scratch=(), us=2, name=None,
):
    args = list(args)
    if deps:
        args[0] = after(args[0], *deps)
    n_in, n_out, n_own = len(args), len(outs), len(scratch)
    cuts = [one if isinstance(one, tuple) else (one, 1, 0) for one in loads]
    loads = [one[0] for one in cuts]
    n_sems = sum(one[1] for one in cuts) + len(stores)

    def inner(*refs):
        ins = list(refs[:n_in])
        results = list(refs[n_in : n_in + n_out])
        own = refs[n_in + n_out : n_in + n_out + n_own]
        rest = refs[n_in + n_out + n_own :]
        buffers, sems = rest[:-1], rest[-1]
        used = 0
        for n, (i, pieces, axis) in enumerate(cuts):
            mine = [sems.at[used + j] for j in range(pieces)]
            ins[i] = Loaded(ins[i], buffers[n], mine, axis)
            used += pieces
        for n, i in enumerate(stores):
            results[i] = Stored(results[i], buffers[len(loads) + n], sems.at[used + n])
        body(*ins, *results, *own)
        for i in loads:
            ins[i].wait()
        for i in stores:
            results[i].close()
        for i in stores:
            results[i].wait()

    def space(i):
        if i in smem:
            return pltpu.SMEM
        return pltpu.HBM if i in hbm or i in loads else pltpu.VMEM

    for i in (*loads, *hbm):
        if i < n_in:
            args[i] = pltpu.with_memory_space_constraint(args[i], pltpu.HBM)
    kinds = [
        pltpu.HBM(o.shape, o.dtype) if i in hbm_outs or i in stores else o
        for i, o in enumerate(outs)
    ]
    staged = [pltpu.VMEM(args[i].shape, args[i].dtype) for i in loads]
    staged += [pltpu.VMEM(outs[i].shape, outs[i].dtype) for i in stores]
    return pl.pallas_call(
        inner,
        out_shape=kinds,
        in_specs=[pl.BlockSpec(memory_space=space(i)) for i in range(n_in)],
        out_specs=[
            pl.BlockSpec(
                memory_space=pltpu.HBM if i in hbm_outs or i in stores else pltpu.VMEM
            )
            for i in range(n_out)
        ],
        scratch_shapes=[
            *scratch, *staged, pltpu.SemaphoreType.DMA((max(1, n_sems),))
        ],
        input_output_aliases=aliases or {},
        compiler_params=pltpu.CompilerParams(vmem_limit_bytes=44 * mega),
        cost_estimate=pl.CostEstimate(
            flops=int(us * 1.1e9), bytes_accessed=mega // 4, transcendentals=0
        ),
        name=name,
    )(*args)


def as_column(row):
    wide = jnp.broadcast_to(row.astype(f32), (8, row.shape[1]))
    return wide.T[:, 0:1].astype(jnp.int32)


def slots_body(
    experts, capacity, row_ref, seg_row, near, bias, code_row, code_col, seg_col, tile
):
    seq = row_ref.shape[1]
    half = capacity // 2
    quarter = (experts // 2) * half
    first = lax.broadcasted_iota(jnp.int32, (seq, seq), 0)
    second = lax.broadcasted_iota(jnp.int32, (seq, seq), 1)
    route = row_ref[...]
    chosen = route == lax.broadcasted_iota(jnp.int32, (experts, seq), 0)
    count = mm(chosen.astype(bf16), (first < second).astype(bf16))
    slot = jnp.sum(jnp.where(chosen, count, 0.0), axis=0, keepdims=True).astype(jnp.int32)
    upper = jnp.where(slot >= half, 1, 0)
    code = (2 * (route & 1) + upper) * quarter + (route >> 1) * half + slot - half * upper
    code_row[...] = code
    code_col[...] = as_column(code)
    seg_col[...] = as_column(seg_row[...])
    bucket = near[...]
    for h in range(bias.shape[0]):
        line = jnp.zeros(bucket.shape, f32)
        for b in range(bias.shape[1]):
            line = jnp.where(bucket == b, bias[h, b], line)
        wide = jnp.broadcast_to(line, (rows_q, table))
        tile[h] = pltpu.roll(wide, 0, 1, stride=1, stride_axis=0)[:, :window]


def span(i0, seq):
    start = max(0, i0 - reach)
    end = min(seq, i0 + rows_q + reach)
    return start, end, start - (i0 - reach)


def masked_probs(score, same, tile):
    score = jnp.where(same, score + tile, negative)
    score = jnp.exp(score - jnp.max(score, axis=1, keepdims=True))
    return (score * (1.0 / jnp.sum(score, axis=1, keepdims=True))).astype(bf16)


def stack_heads(block, heads):
    lane = lax.broadcasted_iota(jnp.int32, block.shape, 1) // head_size
    return jnp.concatenate(
        [jnp.where(lane == h, block, jnp.zeros_like(block)) for h in range(heads)], axis=0
    )


def own_heads(stacked, heads):
    rows = stacked.shape[0] // heads
    lane = lax.broadcasted_iota(jnp.int32, (rows, stacked.shape[1]), 1) // head_size
    out = stacked[(heads - 1) * rows :]
    for h in range(heads - 1):
        out = jnp.where(lane == h, stacked[h * rows : (h + 1) * rows], out)
    return out


def masked_exp(score, same, tile):
    heads, rows, keys = tile.shape
    score = score.reshape(heads, rows, keys) + tile
    score = jnp.where(same[None], score, negative)
    return jnp.exp(score - jnp.max(score, axis=2, keepdims=True))


def attend_body(
    t_ref, x0, x1, x2, x3, gain, weight, seg_row, seg_col, tile, out_weight,
    x_all, normed, ctx, query, key, value,
):
    t = t_ref[0]
    own = x0.shape[0]
    seq = 4 * own
    heads = tile.shape[0]
    columns = heads * head_size
    for k, ref in enumerate((x0, x1, x2, x3)):
        at = pl.ds(pl.multiple_of((t ^ k) * own, own), own)
        x = ref[...]
        x_all[at, :] = x
        x = x.astype(f32)
        inv = lax.rsqrt(jnp.mean(x * x, axis=1, keepdims=True) + epsilon)
        normed[at, :] = (x * inv * gain[...]).astype(bf16)
    x_all.flush()
    normed.flush()
    query[...] = mm_nt(normed[...], weight[0]).astype(bf16)
    key[...] = mm_nt(weight[1], normed[...]).astype(bf16)
    value[:, 0:columns] = mm_nt(normed[...], weight[2]).astype(bf16)
    value[:, columns:] = jnp.ones((seq, head_size), bf16)
    for i0 in range(0, seq, rows_q):
        start, end, off = span(i0, seq)
        same = seg_col[i0 : i0 + rows_q, :] == seg_row[:, start:end]
        score = mm(stack_heads(query[i0 : i0 + rows_q, :], heads), key[:, start:end])
        weights = masked_exp(score, same, tile[:, :, off : off + end - start]).astype(bf16)
        out = mm(weights.reshape(heads * rows_q, end - start), value[start:end, :])
        out = out[:, 0:columns] * (1.0 / out[:, columns : columns + 1])
        out = own_heads(out, heads).astype(bf16)
        ctx[i0 : i0 + rows_q, :] = out[:, 0 : 2 * head_size]
        lane = 0 if i0 < seq // 2 else head_size
        at = seq + i0 % (seq // 2)
        ctx[at : at + rows_q, lane : lane + head_size] = out[:, 2 * head_size :]
    first = seq + seq // 2
    for j in range(out_weight.shape[1] // 128):
        ctx[first + j * columns : first + (j + 1) * columns, :] = out_weight[
            :, j * 128 : (j + 1) * 128
        ]


def probs_body(normed, weight, seg_row, seg_col, tile, probs, key_rows, query):
    seq = normed.shape[0]
    heads = tile.shape[0]
    query[...] = mm_nt(normed[...], weight[0]).astype(bf16)
    key_rows[...] = mm_nt(normed[...], weight[1]).astype(bf16)
    for i0 in range(0, seq, rows_q):
        start, end, off = span(i0, seq)
        same = seg_col[i0 : i0 + rows_q, :] == seg_row[:, start:end]
        score = mm_nt(stack_heads(query[i0 : i0 + rows_q, :], heads), key_rows[start:end, :])
        weights = masked_exp(score, same, tile[:, :, off : off + end - start])
        inv = 1.0 / jnp.sum(weights, axis=2, keepdims=True)
        probs[:, i0 : i0 + rows_q, 0 : end - start] = (weights * inv).astype(bf16)


def columns_body(normed, weight, ctx, query_cols, value_cols, ctx_cols):
    seq = normed.shape[0]
    columns = weight.shape[1]
    query_cols[...] = mm_nt(weight[0], normed[...]).astype(bf16)
    value_cols[...] = mm_nt(weight[2], normed[...]).astype(bf16)
    pair = 2 * head_size
    ctx_cols[0:pair, :] = ctx[0:seq, :].T
    last = ctx[seq : seq + seq // 2, :].T
    ctx_cols[pair:columns, 0 : seq // 2] = last[0:head_size, :]
    ctx_cols[pair:columns, seq // 2 :] = last[head_size:, :]


def third(ctx, r0, rows, seq):
    lane = 0 if r0 < seq // 2 else head_size
    at = seq + r0 % (seq // 2)
    return ctx[at : at + rows, lane : lane + head_size]


def mid_body(
    t_ref, x_all, c0, c1, c2, c3, gain, code_row,
    h_one, h_own, rows, normed,
):
    t = t_ref[0]
    seq, width = x_all.shape
    own = seq // 4
    quarter = rows.shape[0]
    ctxs = (c0, c1, c2, c3)
    columns = 3 * head_size
    first = seq + seq // 2
    weights = [
        jnp.concatenate(
            [c[first + j * columns : first + (j + 1) * columns, :] for j in range(width // 128)],
            axis=1,
        )
        for c in ctxs
    ]
    pair = 2 * head_size
    packed = [
        jnp.concatenate([weights[2 * i][0:pair, :], weights[2 * i + 1][0:pair, :]], axis=0)
        for i in range(2)
    ]
    last = jnp.concatenate([w[pair : pair + head_size, :] for w in weights], axis=0)
    for r0 in range(0, seq, own):
        at = slice(r0, r0 + own)
        left = jnp.concatenate([third(c, r0, own, seq) for c in ctxs], axis=1)
        total = mm(left, last)
        for i in range(2):
            left = jnp.concatenate([ctxs[2 * i][at, :], ctxs[2 * i + 1][at, :]], axis=1)
            total = total + mm(left, packed[i])
        total = total + x_all[at, :].astype(f32)
        h_one[at, :] = total.astype(bf16)
        h_one.flush(r0, own)

        @pl.when(t * own == r0)
        def _(total=total):
            h_own[...] = total

        inv = lax.rsqrt(jnp.mean(total * total, axis=1, keepdims=True) + epsilon)
        normed[at, :] = (total * inv * gain[...]).astype(bf16)
    h_own.flush()
    place = lax.broadcasted_iota(jnp.int32, (quarter, seq), 0) + t * quarter
    rows[...] = mm((place == code_row[...]).astype(bf16), normed[...]).astype(bf16)


def spread_body(t_ref, g0, g1, g2, g3, code_row, g_all, rows):
    t = t_ref[0]
    own = g0.shape[0]
    quarter = rows.shape[0]
    for k, ref in enumerate((g0, g1, g2, g3)):
        g_all[pl.ds(pl.multiple_of((t ^ k) * own, own), own), :] = ref[...]
    g_all.flush()
    place = lax.broadcasted_iota(jnp.int32, (quarter, g_all.shape[0]), 0) + t * quarter
    rows[...] = mm((place == code_row[...]).astype(bf16), g_all[...]).astype(bf16)


gelu_scale = 0.7978845608028654
gelu_cubic = 0.044715


def expert_body(
    e_ref, r0, r1, g0, g1, router, w_in_all, w_out_all,
    back0, back1, grad0, grad1, hidden_out, gated_out, pre_out, router_out,
    w_in, w_out, rows_all, g_rows, backs, grads, sem, out_sem,
):
    half = r0.shape[0]
    load_in = pltpu.make_async_copy(w_in_all.at[e_ref[0]], w_in, sem.at[0])
    load_out = pltpu.make_async_copy(w_out_all.at[e_ref[0]], w_out, sem.at[1])
    load_in.start()

    load_out.start()
    rows_all[0] = r0[...]
    rows_all[1] = r1[...]
    g_rows[0] = g0[...]
    g_rows[1] = g1[...]
    router_out[...] = jnp.zeros(router_out.shape, f32)
    load_in.wait()
    load_out.wait()
    sends = [
        [
            pltpu.make_async_copy(backs.at[i], back, out_sem.at[2 * i]),
            pltpu.make_async_copy(grads.at[i], grad, out_sem.at[2 * i + 1]),
        ]
        for i, (back, grad) in enumerate(((back0, grad0), (back1, grad1)))
    ]

    def one_half(i, carry):
        first = pl.multiple_of(i * half, half)
        at = pl.ds(first, half)
        rows = rows_all[i]
        cot = g_rows[i].astype(f32)
        logits = mm_nt(rows, router[...])
        logits = jnp.exp(logits - jnp.max(logits, axis=1, keepdims=True))
        prob = logits / jnp.sum(logits, axis=1, keepdims=True)
        mine = lax.broadcasted_iota(jnp.int32, prob.shape, 1) == e_ref[1]
        gate = jnp.sum(jnp.where(mine, prob, 0.0), axis=1, keepdims=True)
        gated = (gate * cot).astype(bf16)
        gated_out[at, :] = gated
        pre = mm(rows, w_in[...])
        square = pre * pre
        inner = jnp.tanh(gelu_scale * pre * (1.0 + gelu_cubic * square))
        half_up = 0.5 + 0.5 * inner
        hidden = (pre * half_up).astype(bf16)
        hidden_out[at, :] = hidden
        slope = half_up + (0.5 * gelu_scale) * pre * (1.0 - inner * inner) * (
            1.0 + (3.0 * gelu_cubic) * square
        )
        part = mm(hidden, w_out[...])
        backs[i] = (gate * part).astype(bf16)
        grad_gate = jnp.sum(cot * part, axis=1, keepdims=True)
        grad_pre = (mm_nt(gated, w_out[...]) * slope).astype(bf16)
        pre_out[at, :] = grad_pre
        grad_logits = (gate * grad_gate * (jnp.where(mine, 1.0, 0.0) - prob)).astype(bf16)
        grads[i] = (mm_nt(grad_pre, w_in[...]) + mm(grad_logits, router[...])).astype(bf16)
        for n in range(2):

            @pl.when(i == n)
            def _(n=n):
                sends[n][0].start()
                sends[n][1].start()

        router_out[...] += mm_tn(grad_logits, rows)
        return carry

    lax.fori_loop(0, 2, one_half, 0)
    hidden_out.flush()
    gated_out.flush()
    pre_out.flush()
    for pair in sends:
        for one in pair:
            one.wait()


def expert(scalars, r0, r1, g0, g1, router, w_in, w_out):
    half, width = r0.shape
    hidden = w_in.shape[2]
    rows = 2 * half
    return run(
        expert_body,
        [shape((half, width), bf16)] * 4
        + [
            shape((rows, hidden), bf16),
            shape((rows, width), bf16),
            shape((rows, hidden), bf16),
            shape(router.shape, f32),
        ],
        [scalars, r0, r1, g0, g1, router, w_in, w_out],
        smem=(0,),
        hbm=(6, 7),
        hbm_outs=(0, 1, 2, 3),
        stores=(4, 5, 6),
        scratch=[
            pltpu.VMEM((width, hidden), bf16),
            pltpu.VMEM((hidden, width), bf16),
            pltpu.VMEM((2, half, width), bf16),
            pltpu.VMEM((2, half, width), bf16),
            pltpu.VMEM((2, half, width), bf16),
            pltpu.VMEM((2, half, width), bf16),
            pltpu.SemaphoreType.DMA((2,)),
            pltpu.SemaphoreType.DMA((4,)),
        ],
        us=7,
        name="expert",
    )


def expert_grad_body(first, e_ref, r0, r1, hidden, gated, pre, *refs):
    d_in, d_out, sum_in, sum_out, sem = refs[-5:]
    rows = jnp.concatenate([r0[...], r1[...]], axis=0)
    sum_in[...] = mm_tn(rows, pre[...])
    store_in = pltpu.make_async_copy(sum_in, d_in.at[e_ref[0]], sem.at[0])
    store_in.start()
    sum_out[...] = mm_tn(hidden[...], gated[...])
    store_out = pltpu.make_async_copy(sum_out, d_out.at[e_ref[0]], sem.at[1])
    store_out.start()
    store_in.wait()
    store_out.wait()


def expert_grads(scalars, r0, r1, hidden, gated, pre, so_far=(), deps=()):
    columns, width = hidden.shape[1], gated.shape[1]
    return run(
        functools.partial(expert_grad_body, not so_far),
        [shape((2, width, columns), f32), shape((2, columns, width), f32)],
        [scalars, r0, r1, hidden, gated, pre, *so_far],
        smem=(0,),
        loads=(3, 4, 5),
        hbm=(6, 7),
        hbm_outs=(0, 1),
        aliases={6: 0, 7: 1} if so_far else None,
        deps=deps,
        scratch=[
            pltpu.VMEM((width, columns), f32),
            pltpu.VMEM((columns, width), f32),
            pltpu.SemaphoreType.DMA((2,)),
        ],
        us=4,
        name="expert_grads",
    )


def back_body(
    t_ref, b0, b1, b2, b3, code_col, h_one, gain, g_all, weight, ctx_cols, router,
    h_own, gctx, early, grad_h, slots,
):
    t = t_ref[0]
    seq, width = h_one.shape
    own = seq // 4
    quarter = b0.shape[0]
    columns = gctx.shape[1]
    for j, ref in enumerate((b0, b1, b2, b3)):
        slots[pl.ds(pl.multiple_of((t ^ j) * quarter, quarter), quarter), :] = ref[...]
    sum_gain = jnp.zeros((1, width), f32)
    place = lax.broadcasted_iota(jnp.int32, (own, 4 * quarter), 1)
    for n, r0 in enumerate(range(0, seq, own)):
        at = slice(r0, r0 + own)
        total = mm((place == code_col[at, :]).astype(bf16), slots[...])
        h_one.piece(n)
        g_all.piece(n)
        h = h_one.buffer[at, :].astype(f32)
        inv = lax.rsqrt(jnp.mean(h * h, axis=1, keepdims=True) + epsilon)
        n2 = h * inv
        sum_gain = sum_gain + jnp.sum(total * n2, axis=0, keepdims=True)
        a = total * gain[...]
        mean = jnp.mean(a * n2, axis=1, keepdims=True)
        full = g_all.buffer[at, :].astype(f32) + inv * (a - n2 * mean)
        grad_h[at, :] = full.astype(bf16)

        @pl.when(t * own == r0)
        def _(full=full):
            h_own[...] = full

    h_own.flush()
    gctx[...] = mm_nt(grad_h[...], weight[...]).astype(bf16)
    gctx.flush()
    early[0:columns, :] = mm(ctx_cols[...], grad_h[...]).astype(bf16)
    rest = jnp.concatenate([router[...], sum_gain], axis=0)
    spare = early.shape[0] - columns - rest.shape[0]
    rest = jnp.concatenate([rest, jnp.zeros((spare, width), f32)], axis=0)
    early[columns:, :] = rest.astype(bf16)


def attend_back_body(
    gctx, value_cols, key_rows, query_cols, probs, normed, near,
    grad_q, grad_k, grad_v, late, grad_bias, spill, sum_k, sum_v,
):
    seq, columns = gctx.shape
    heads = columns // head_size
    buckets = grad_bias.shape[0]
    spill[...] = jnp.zeros(spill.shape, f32)
    sum_k[...] = jnp.zeros(sum_k.shape, f32)
    sum_v[...] = jnp.zeros(sum_v.shape, f32)
    gctx_cols = gctx[...].T
    for n, i0 in enumerate(range(0, seq, rows_q)):
        start, end, off = span(i0, seq)
        keys = end - start
        at = slice(i0, i0 + rows_q)
        grad = mm(stack_heads(gctx[at, :], heads), value_cols[:, start:end])
        probs.piece(n)
        prob = probs.buffer[:, at, 0:keys].reshape(heads * rows_q, keys)
        wide = prob.astype(f32)
        both = wide * grad
        score = both - wide * jnp.sum(both, axis=1, keepdims=True)
        spill[:, :, off : off + keys] += score.reshape(heads, rows_q, keys)
        score = score.astype(bf16)
        grad_q[at, :] = own_heads(mm(score, key_rows[start:end, :]), heads).astype(bf16)
        for h in range(heads):
            cols = slice(h * head_size, (h + 1) * head_size)
            mine = slice(h * rows_q, (h + 1) * rows_q)
            sum_k[cols, start:end] += mm(query_cols[cols, at], score[mine])
            sum_v[cols, start:end] += mm(gctx_cols[cols, at], prob[mine])
    grad_k[...] = sum_k[...].astype(bf16)
    grad_v[...] = sum_v[...].astype(bf16)
    grad_q.flush()
    grad_k.flush()
    grad_v.flush()
    late[0:columns, :] = mm_tn(grad_q[...], normed[...]).astype(bf16)
    late[columns : 2 * columns, :] = mm(grad_k[...], normed[...]).astype(bf16)
    late[2 * columns : 3 * columns, :] = mm(grad_v[...], normed[...]).astype(bf16)
    chosen = near[...] == lax.broadcasted_iota(jnp.int32, (buckets, table), 0)
    places = lax.broadcasted_iota(jnp.int32, (buckets, 128), 1)
    found = jnp.zeros((buckets, 128), f32)
    for h in range(heads):
        strip = jnp.zeros((8, table), f32)
        for a in range(0, rows_q, 8):
            strip = strip + pltpu.roll(spill[h, a : a + 8, :], (table - a) % table, 1)
        line = lax.broadcasted_iota(jnp.int32, strip.shape, 0)
        for bit in (1, 2, 4):
            strip = jnp.where((line & bit) != 0, pltpu.roll(strip, table - bit, 1), strip)
        strip = jnp.sum(strip, axis=0, keepdims=True)
        per = jnp.sum(jnp.where(chosen, strip, 0.0), axis=1, keepdims=True)
        found = found + jnp.where(places == h, per, 0.0)
    grad_bias[...] = found


def input_grad_body(t_ref, grad_q, grad_k, grad_v, weight, normed, gain, keep, send, sums):
    t = t_ref[0]
    seq, width = normed.shape
    own = seq // 4
    total_gain = jnp.zeros((1, width), f32)
    for k in range(4):
        at = pl.ds(pl.multiple_of((t ^ k) * own, own), own)
        part = mm(grad_q[at, :], weight[0])
        part = part + mm_tn(grad_k[:, at], weight[1])
        part = part + mm_tn(grad_v[:, at], weight[2])
        total_gain = total_gain + jnp.sum(part * normed[at, :].astype(f32), axis=0, keepdims=True)
        out = keep if k in (0, 2) else send
        out[(k // 2) * own : (k // 2 + 1) * own, :] = part.astype(bf16)
    sums[...] = total_gain / gain[...]


def sum_copies(copies, ref):
    full = ref[...].astype(f32)
    rows = full.shape[0] // copies
    total = full[0:rows]
    for i in range(1, copies):
        total = total + full[i * rows : (i + 1) * rows]
    return total


def share_body(copies, early, late, sums, grad_bias, out):
    width = early.shape[1]
    found = grad_bias[...]
    lanes = found.shape[1]
    found = jnp.concatenate([found, jnp.zeros((lanes - found.shape[0], lanes), f32)], axis=0).T
    found = jnp.concatenate([found[0:8], jnp.zeros((8, width - lanes), f32)], axis=1)
    line = lax.broadcasted_iota(jnp.int32, found.shape, 0)
    found = jnp.where(line == 7, sums[...], found)
    total = [found, sum_copies(copies, early), sum_copies(copies, late)]
    out[...] = jnp.concatenate(total, axis=0).astype(bf16)


def finish_body(early_rows, i_ref, *refs):
    shares = refs[:-7]
    qkv, out, bias, gain_attn, gain_moe, router, early = refs[-7:]
    columns = out.shape[0]
    experts = router.shape[0]
    small = None
    for j, ref in enumerate(shares):
        full = ref[...].astype(f32)
        owner = i_ref[0] ^ j
        small = full[0:8] if small is None else small + full[0:8]
        early[owner] = full[8 : 8 + early_rows]
        qkv[owner] = full[8 + early_rows :]
    whole = jnp.concatenate([early[i] for i in range(early.shape[0])], axis=0)
    out[...] = whole[0:columns]
    router[...] = whole[columns : columns + experts]
    gain_moe[...] = whole[columns + experts : columns + experts + 1]
    bias[...] = small[0 : bias.shape[0], 0 : bias.shape[1]]
    gain_attn[...] = small[7:8]


def last_body(kept, got, far, x_ref, gain, h_own, grad):
    total = kept[...].astype(f32) + got[...].astype(f32) + far[...].astype(f32)
    x = x_ref[...].astype(f32)
    inv = lax.rsqrt(jnp.mean(x * x, axis=1, keepdims=True) + epsilon)
    n1 = x * inv
    a = total * gain[...]
    grad[...] = h_own[...] + inv * (a - n1 * jnp.mean(a * n1, axis=1, keepdims=True))


def output_body(t_ref, f0, f1, f2, f3, code_col, h_own, out, slots):
    t = t_ref[0]
    own = h_own.shape[0]
    quarter = f0.shape[0]
    for j, ref in enumerate((f0, f1, f2, f3)):
        slots[pl.ds(pl.multiple_of((t ^ j) * quarter, quarter), quarter), :] = ref[...]
    codes = code_col[pl.ds(pl.multiple_of(t * own, own), own), :]
    place = lax.broadcasted_iota(jnp.int32, (own, 4 * quarter), 1)
    out[...] = (h_own[...] + mm((place == codes).astype(bf16), slots[...])).astype(bf16)


def turn(value):
    return lax.all_to_all(value, "dp", split_axis=0, concat_axis=0, tiled=True)


def per_device(
    inputs,
    segments,
    buckets,
    routes,
    qkv_weight,
    out_weight,
    rel_bias,
    norm_attn,
    norm_moe,
    router_weight,
    expert_in,
    expert_out,
    cotangent,
):
    own, width = inputs.shape
    seq = 4 * own
    dp = lax.axis_size("dp")
    experts = router_weight.shape[1]
    capacity = max(2, 5 * seq // (4 * experts))
    quarter = (experts // 2) * (capacity // 2)
    heads = rel_bias.shape[1]
    columns = heads * head_size
    t_one = lax.axis_index("tensor").astype(jnp.int32)[None]
    x_side = t_one >> 1
    dp_one = lax.axis_index("dp").astype(jnp.int32)[None]
    first_expert = 2 * dp_one
    near_expert = jnp.concatenate([x_side, first_expert + x_side])
    far_expert = jnp.concatenate([1 - x_side, first_expert + 1 - x_side])
    inputs, t_one, dp_one, near_expert, far_expert = lax.optimization_barrier(
        (inputs, t_one, dp_one, near_expert, far_expert)
    )
    gain_attn = norm_attn[None, :]
    gain_moe = norm_moe[None, :]
    near = lax.slice_in_dim(buckets, seq - 1 - reach, seq - 1 - reach + table, axis=0)[None, :]
    weight = jnp.swapaxes(qkv_weight, 1, 2)
    router = router_weight.T

    code_row, code_col, seg_col, tile = run(
        functools.partial(slots_body, experts, capacity),
        [
            shape((1, seq), jnp.int32),
            shape((seq, 1), jnp.int32),
            shape((seq, 1), jnp.int32),
            shape((heads, rows_q, window), f32),
        ],
        [routes.reshape(1, seq), segments, near, rel_bias.T],
        smem=(3,),
        us=2,
        stores=(3,),
        name="slots",
    )
    xs = gather4(inputs, code_row)
    x_all, normed, ctx = run(
        attend_body,
        [
            shape((seq, width), bf16),
            shape((seq, width), bf16),
            shape((seq + seq // 2 + columns * width // 128, 128), bf16),
        ],
        [t_one, *xs, gain_attn, weight, segments, seg_col, tile, out_weight],
        smem=(0,),
        scratch=[
            pltpu.VMEM((seq, columns), bf16),
            pltpu.VMEM((columns, seq), bf16),
            pltpu.VMEM((seq, columns + head_size), bf16),
        ],
        us=10,
        loads=(1, 6, 9, 10),
        stores=(0, 1, 2),
        name="attend",
    )
    gs = gather4(cotangent, ctx)
    g_all, g_rows = run(
        spread_body,
        [shape((seq, width), bf16), shape((quarter, width), bf16)],
        [t_one, *gs, code_row],
        smem=(0,),
        us=2,
        loads=(1,),
        stores=(0,),
        name="spread",
    )
    cs = gather4(ctx, g_rows)
    h_one, h_own, rows = run(
        mid_body,
        [
            shape((seq, width), bf16),
            shape((own, width), f32),
            shape((quarter, width), bf16),
        ],
        [t_one, x_all, *cs, gain_moe, code_row],
        smem=(0,),
        scratch=[pltpu.VMEM((seq, width), bf16)],
        us=4,
        loads=(2, 1),
        stores=(0, 1),
        name="mid",
    )
    g_got = turn(g_rows)
    query_cols, value_cols, ctx_cols = run(
        columns_body,
        [shape((columns, seq), bf16)] * 3,
        [normed, weight, ctx],
        deps=[rows],
        us=3,
        loads=(0, 1, 2),
        stores=(0, 1, 2),
        name="columns",
    )
    g_far = x_hop(after(g_got, query_cols))
    probs, key_rows = run(
        probs_body,
        [shape((heads, seq, window), bf16), shape((seq, columns), bf16)],
        [normed, weight, segments, seg_col, tile],
        deps=[query_cols],
        scratch=[pltpu.VMEM((seq, columns), bf16)],
        us=7,
        loads=(0, 1, 4),
        stores=(0, 1),
        name="probs",
    )
    row_got = after(turn(rows), probs)
    near_rows = (row_got, core_hop(row_got))
    near_out = expert(
        near_expert, *near_rows, g_got, core_hop(g_got), router, expert_in, expert_out
    )
    far_mine = after(x_hop(row_got), near_out[0])
    far_rows = (far_mine, core_hop(far_mine))
    far_out = expert(
        far_expert, *far_rows, g_far, core_hop(g_far), router, expert_in, expert_out
    )
    far = far_out[2] + core_hop(far_out[3])
    router_part = near_out[7] + far_out[7]
    router_part = router_part + core_hop(router_part)
    router_part = router_part + x_hop(router_part)
    weight_grads = expert_grads(near_expert, *near_rows, *near_out[4:7], deps=[far])
    far = after(x_hop(far), weight_grads[0])
    kept = near_out[2] + core_hop(near_out[3]) + far
    home = turn(kept)
    far = after(far_out[0], kept) + core_hop(far_out[1])
    weight_grads = expert_grads(
        far_expert, *far_rows, *far_out[4:7], so_far=weight_grads, deps=[far, router_part]
    )
    home = after(home, weight_grads[0])
    fwd = after(near_out[0], home) + core_hop(near_out[1]) + x_hop(far)
    bs = gather4(home, fwd)
    fwd = turn(fwd)
    small = -(-(experts + 1) // 64) * 64
    gh_own, gctx, early = run(
        back_body,
        [
            shape((own, width), f32),
            shape((seq, columns), bf16),
            shape((columns + small, width), bf16),
        ],
        [t_one, *bs, code_col, h_one, gain_moe, g_all, out_weight, ctx_cols, router_part],
        smem=(0,),
        loads=((6, 4, 0), (8, 4, 0), 9, 10),
        stores=(0, 1),
        scratch=[pltpu.VMEM((seq, width), bf16), pltpu.VMEM((4 * quarter, width), bf16)],
        us=2,
        name="back",
    )
    early_got = turn(early)
    grad_q, grad_k, grad_v, late, grad_bias = run(
        attend_back_body,
        [
            shape((seq, columns), bf16),
            shape((columns, seq), bf16),
            shape((columns, seq), bf16),
            shape((3 * columns, width), bf16),
            shape((rel_bias.shape[0], 128), f32),
        ],
        [gctx, value_cols, key_rows, query_cols, probs, normed, near],
        loads=(0, 1, 2, 3, (4, seq // rows_q, 1), 5),
        stores=(0, 1, 2),
        deps=[fwd],
        scratch=[
            pltpu.VMEM((heads, rows_q, table), f32),
            pltpu.VMEM((columns, seq), f32),
            pltpu.VMEM((columns, seq), f32),
        ],
        us=10,
        name="attend_back",
    )
    late_got = turn(late)
    keep, send, gain_part = run(
        input_grad_body,
        [
            shape((2 * own, width), bf16),
            shape((2 * own, width), bf16),
            shape((1, width), f32),
        ],
        [t_one, grad_q, grad_k, grad_v, weight, normed, gain_attn],
        smem=(0,),
        us=2,
        loads=(1, 2, 3, 4, 5),
        name="input_grad",
    )
    gain_part = gain_part + core_hop(gain_part)
    gain_part = gain_part + x_hop(gain_part)
    keep, send, fwd = lax.optimization_barrier((keep, send, fwd, gain_part))[:3]
    fs = gather4(fwd)
    got = core_hop(send)
    far = x_hop(keep[own:] + got[own:])
    early_rows = early.shape[0] // dp
    late_rows = late.shape[0] // dp
    (share,) = run(
        functools.partial(share_body, dp),
        [shape((8 + early_rows + late_rows, width), bf16)],
        [early_got, late_got, gain_part, grad_bias],
        us=1,
        name="share",
    )
    shares = [share]
    for j in range(2, dp, 2):
        shares.append(lax.ppermute(share, "dp", [(i, i ^ j) for i in range(dp)]))
    shares = [
        one
        for share in shares
        for one in (share, lax.ppermute(share, "dp", [(i, i ^ 1) for i in range(dp)]))
    ]
    (grad_inputs,) = run(
        last_body,
        [shape((own, width), f32)],
        [keep[:own], got[:own], far, inputs, gain_attn, gh_own],
        loads=(3, 5),
        name="last",
    )
    (output,) = run(
        output_body,
        [shape((own, width), bf16)],
        [t_one, *fs, code_col, h_own],
        smem=(0,),
        loads=(6,),
        scratch=[pltpu.VMEM((4 * quarter, width), bf16)],
        name="output",
    )
    qkv_grad, out_grad, bias_grad, gain_attn_grad, gain_moe_grad, router_grad = run(
        functools.partial(finish_body, early_rows),
        [
            shape((dp, late_rows, width), f32),
            shape((columns, width), f32),
            shape((heads, rel_bias.shape[0]), f32),
            shape((1, width), f32),
            shape((1, width), f32),
            shape((experts, width), f32),
        ],
        [dp_one, *shares],
        smem=(0,),
        scratch=[pltpu.VMEM((dp, early_rows, width), f32)],
        us=2,
        name="finish",
    )
    return (
        output,
        grad_inputs,
        jnp.swapaxes(qkv_grad.reshape(3, columns, width), 1, 2),
        out_grad,
        bias_grad.T,
        gain_attn_grad[0],
        gain_moe_grad[0],
        router_grad.T,
        *weight_grads,
    )


def solution(mesh):
    placed = (
        P(("dp", "tensor"), None),
        P("dp", None),
        P(),
        P("dp", None, None),
        P(None, None, "tensor"),
        P("tensor", None),
        P(None, "tensor"),
        P(),
        P(),
        P(),
        P("dp", None, "tensor"),
        P("dp", "tensor", None),
        P(("dp", "tensor"), None),
    )
    return jax.shard_map(
        per_device,
        mesh=mesh,
        in_specs=placed,
        out_specs=(
            P(("dp", "tensor"), None),
            P(("dp", "tensor"), None),
            P(None, None, "tensor"),
            P("tensor", None),
            P(None, "tensor"),
            P(),
            P(),
            P(),
            P("dp", None, "tensor"),
            P("dp", "tensor", None),
        ),
        check_vma=False,
    )
```

```python
import functools

import jax
import jax.numpy as jnp
from jax import lax
from jax.experimental import pallas as pl
from jax.experimental.pallas import tpu as pltpu
from jax.sharding import PartitionSpec as P

epsilon = 1e-06
negative = -1000000000.0
bf16 = jnp.bfloat16
f32 = jnp.float32
reach = 256
rows_q = 128
window = rows_q + 2 * reach
table = window + rows_q
head_size = 64
mega = 1024 * 1024

core_pairs = [(0, 1), (1, 0), (2, 3), (3, 2)]
x_pairs = [(0, 2), (2, 0), (1, 3), (3, 1)]


def core_hop(value):
    return lax.ppermute(value, "tensor", core_pairs)


def x_hop(value):
    return lax.ppermute(value, "tensor", x_pairs)


def after(value, *deps):
    return lax.optimization_barrier((value, *deps))[0]


def gather4(value, *deps):
    other = x_hop(value)
    if deps:
        other = after(other, *deps)
    return value, core_hop(value), other, core_hop(other)


def dot(a, b, dims):
    return lax.dot_general(a, b, (dims, ((), ())), preferred_element_type=f32)


def mm(a, b):
    return dot(a, b, ((1,), (0,)))


def mm_nt(a, b):
    return dot(a, b, ((1,), (1,)))


def mm_tn(a, b):
    return dot(a, b, ((0,), (0,)))


def shape(dims, kind):
    return jax.ShapeDtypeStruct(dims, kind)


class Loaded:
    def __init__(self, source, buffer, sems, axis=0):
        self.buffer, self.axis = buffer, axis
        self.shape, self.dtype = buffer.shape, buffer.dtype
        count = len(sems)
        self.step = self.shape[axis] // count
        self.copies = []
        for i, sem in enumerate(sems):
            at = self.place(i) if count > 1 else ()
            part = (source.at[at], buffer.at[at]) if at else (source, buffer)
            self.copies.append(pltpu.make_async_copy(*part, sem))
            self.copies[-1].start()
        self.here = [False] * count

    def place(self, i):
        return (slice(None),) * self.axis + (pl.ds(i * self.step, self.step),)

    def piece(self, i):
        if not self.here[i]:
            self.copies[i].wait()
            self.here[i] = True

    def wait(self):
        for i in range(len(self.copies)):
            self.piece(i)

    def __getitem__(self, place):
        self.wait()
        return self.buffer[place]


class Stored:
    def __init__(self, target, buffer, sem):
        self.buffer, self.target, self.sem = buffer, target, sem
        self.shape, self.dtype = buffer.shape, buffer.dtype
        self.gone = 0

    def flush(self, first=0, rows=None):
        rows = self.shape[0] if rows is None else rows
        at = pl.ds(first, rows)
        pltpu.make_async_copy(self.buffer.at[at], self.target.at[at], self.sem).start()
        self.gone += rows

    def close(self):
        if not self.gone:
            self.flush()

    def wait(self):
        pltpu.make_async_copy(self.buffer, self.target, self.sem).wait()

    def __getitem__(self, place):
        return self.buffer[place]

    def __setitem__(self, place, value):
        self.buffer[place] = value


def run(
    body, outs, args, smem=(), loads=(), stores=(), hbm=(), hbm_outs=(), deps=(), aliases=None,
    scratch=(), us=2, name=None,
):
    args = list(args)
    if deps:
        args[0] = after(args[0], *deps)
    n_in, n_out, n_own = len(args), len(outs), len(scratch)
    cuts = [one if isinstance(one, tuple) else (one, 1, 0) for one in loads]
    loads = [one[0] for one in cuts]
    n_sems = sum(one[1] for one in cuts) + len(stores)

    def inner(*refs):
        ins = list(refs[:n_in])
        results = list(refs[n_in : n_in + n_out])
        own = refs[n_in + n_out : n_in + n_out + n_own]
        rest = refs[n_in + n_out + n_own :]
        buffers, sems = rest[:-1], rest[-1]
        used = 0
        for n, (i, pieces, axis) in enumerate(cuts):
            mine = [sems.at[used + j] for j in range(pieces)]
            ins[i] = Loaded(ins[i], buffers[n], mine, axis)
            used += pieces
        for n, i in enumerate(stores):
            results[i] = Stored(results[i], buffers[len(loads) + n], sems.at[used + n])
        body(*ins, *results, *own)
        for i in loads:
            ins[i].wait()
        for i in stores:
            results[i].close()
        for i in stores:
            results[i].wait()

    def space(i):
        if i in smem:
            return pltpu.SMEM
        return pltpu.HBM if i in hbm or i in loads else pltpu.VMEM

    for i in (*loads, *hbm):
        if i < n_in:
            args[i] = pltpu.with_memory_space_constraint(args[i], pltpu.HBM)
    kinds = [
        pltpu.HBM(o.shape, o.dtype) if i in hbm_outs or i in stores else o
        for i, o in enumerate(outs)
    ]
    staged = [pltpu.VMEM(args[i].shape, args[i].dtype) for i in loads]
    staged += [pltpu.VMEM(outs[i].shape, outs[i].dtype) for i in stores]
    return pl.pallas_call(
        inner,
        out_shape=kinds,
        in_specs=[pl.BlockSpec(memory_space=space(i)) for i in range(n_in)],
        out_specs=[
            pl.BlockSpec(
                memory_space=pltpu.HBM if i in hbm_outs or i in stores else pltpu.VMEM
            )
            for i in range(n_out)
        ],
        scratch_shapes=[
            *scratch, *staged, pltpu.SemaphoreType.DMA((max(1, n_sems),))
        ],
        input_output_aliases=aliases or {},
        compiler_params=pltpu.CompilerParams(vmem_limit_bytes=44 * mega),
        cost_estimate=pl.CostEstimate(
            flops=int(us * 1.1e9), bytes_accessed=mega // 4, transcendentals=0
        ),
        name=name,
    )(*args)


def as_column(row):
    wide = jnp.broadcast_to(row.astype(f32), (8, row.shape[1]))
    return wide.T[:, 0:1].astype(jnp.int32)


def slots_body(
    experts, capacity, row_ref, seg_row, near, bias, code_row, code_col, seg_col, tile
):
    seq = row_ref.shape[1]
    half = capacity // 2
    quarter = (experts // 2) * half
    first = lax.broadcasted_iota(jnp.int32, (seq, seq), 0)
    second = lax.broadcasted_iota(jnp.int32, (seq, seq), 1)
    route = row_ref[...]
    chosen = route == lax.broadcasted_iota(jnp.int32, (experts, seq), 0)
    count = mm(chosen.astype(bf16), (first < second).astype(bf16))
    slot = jnp.sum(jnp.where(chosen, count, 0.0), axis=0, keepdims=True).astype(jnp.int32)
    upper = jnp.where(slot >= half, 1, 0)
    code = (2 * (route & 1) + upper) * quarter + (route >> 1) * half + slot - half * upper
    code_row[...] = code
    code_col[...] = as_column(code)
    seg_col[...] = as_column(seg_row[...])
    bucket = near[...]
    for h in range(bias.shape[0]):
        line = jnp.zeros(bucket.shape, f32)
        for b in range(bias.shape[1]):
            line = jnp.where(bucket == b, bias[h, b], line)
        wide = jnp.broadcast_to(line, (rows_q, table))
        tile[h] = pltpu.roll(wide, 0, 1, stride=1, stride_axis=0)[:, :window]


def span(i0, seq):
    start = max(0, i0 - reach)
    end = min(seq, i0 + rows_q + reach)
    return start, end, start - (i0 - reach)


def masked_probs(score, same, tile):
    score = jnp.where(same, score + tile, negative)
    score = jnp.exp(score - jnp.max(score, axis=1, keepdims=True))
    return (score * (1.0 / jnp.sum(score, axis=1, keepdims=True))).astype(bf16)


def stack_heads(block, heads):
    lane = lax.broadcasted_iota(jnp.int32, block.shape, 1) // head_size
    return jnp.concatenate(
        [jnp.where(lane == h, block, jnp.zeros_like(block)) for h in range(heads)], axis=0
    )


def own_heads(stacked, heads):
    rows = stacked.shape[0] // heads
    lane = lax.broadcasted_iota(jnp.int32, (rows, stacked.shape[1]), 1) // head_size
    out = stacked[(heads - 1) * rows :]
    for h in range(heads - 1):
        out = jnp.where(lane == h, stacked[h * rows : (h + 1) * rows], out)
    return out


def masked_exp(score, same, tile):
    heads, rows, keys = tile.shape
    score = score.reshape(heads, rows, keys) + tile
    score = jnp.where(same[None], score, negative)
    return jnp.exp(score - jnp.max(score, axis=2, keepdims=True))


def attend_body(
    t_ref, x0, x1, x2, x3, gain, weight, seg_row, seg_col, tile, out_weight,
    x_all, normed, ctx, query, key, value,
):
    t = t_ref[0]
    own = x0.shape[0]
    seq = 4 * own
    heads = tile.shape[0]
    columns = heads * head_size
    for k, ref in enumerate((x0, x1, x2, x3)):
        at = pl.ds(pl.multiple_of((t ^ k) * own, own), own)
        x = ref[...]
        x_all[at, :] = x
        x = x.astype(f32)
        inv = lax.rsqrt(jnp.mean(x * x, axis=1, keepdims=True) + epsilon)
        normed[at, :] = (x * inv * gain[...]).astype(bf16)
    x_all.flush()
    normed.flush()
    query[...] = mm_nt(normed[...], weight[0]).astype(bf16)
    key[...] = mm_nt(weight[1], normed[...]).astype(bf16)
    value[:, 0:columns] = mm_nt(normed[...], weight[2]).astype(bf16)
    value[:, columns:] = jnp.ones((seq, head_size), bf16)
    for i0 in range(0, seq, rows_q):
        start, end, off = span(i0, seq)
        same = seg_col[i0 : i0 + rows_q, :] == seg_row[:, start:end]
        score = mm(stack_heads(query[i0 : i0 + rows_q, :], heads), key[:, start:end])
        weights = masked_exp(score, same, tile[:, :, off : off + end - start]).astype(bf16)
        out = mm(weights.reshape(heads * rows_q, end - start), value[start:end, :])
        out = out[:, 0:columns] * (1.0 / out[:, columns : columns + 1])
        out = own_heads(out, heads).astype(bf16)
        ctx[i0 : i0 + rows_q, :] = out[:, 0 : 2 * head_size]
        lane = 0 if i0 < seq // 2 else head_size
        at = seq + i0 % (seq // 2)
        ctx[at : at + rows_q, lane : lane + head_size] = out[:, 2 * head_size :]
    first = seq + seq // 2
    for j in range(out_weight.shape[1] // 128):
        ctx[first + j * columns : first + (j + 1) * columns, :] = out_weight[
            :, j * 128 : (j + 1) * 128
        ]


def probs_body(normed, weight, seg_row, seg_col, tile, probs, key_rows, query):
    seq = normed.shape[0]
    heads = tile.shape[0]
    query[...] = mm_nt(normed[...], weight[0]).astype(bf16)
    key_rows[...] = mm_nt(normed[...], weight[1]).astype(bf16)
    for i0 in range(0, seq, rows_q):
        start, end, off = span(i0, seq)
        same = seg_col[i0 : i0 + rows_q, :] == seg_row[:, start:end]
        score = mm_nt(stack_heads(query[i0 : i0 + rows_q, :], heads), key_rows[start:end, :])
        weights = masked_exp(score, same, tile[:, :, off : off + end - start])
        inv = 1.0 / jnp.sum(weights, axis=2, keepdims=True)
        probs[:, i0 : i0 + rows_q, 0 : end - start] = (weights * inv).astype(bf16)


def columns_body(normed, weight, ctx, query_cols, value_cols, ctx_cols):
    seq = normed.shape[0]
    columns = weight.shape[1]
    query_cols[...] = mm_nt(weight[0], normed[...]).astype(bf16)
    value_cols[...] = mm_nt(weight[2], normed[...]).astype(bf16)
    pair = 2 * head_size
    ctx_cols[0:pair, :] = ctx[0:seq, :].T
    last = ctx[seq : seq + seq // 2, :].T
    ctx_cols[pair:columns, 0 : seq // 2] = last[0:head_size, :]
    ctx_cols[pair:columns, seq // 2 :] = last[head_size:, :]


def third(ctx, r0, rows, seq):
    lane = 0 if r0 < seq // 2 else head_size
    at = seq + r0 % (seq // 2)
    return ctx[at : at + rows, lane : lane + head_size]


def mid_body(
    t_ref, x_all, c0, c1, c2, c3, gain, code_row,
    h_one, h_own, rows, normed, sums,
):
    t = t_ref[0]
    seq, width = x_all.shape
    own = seq // 4
    quarter = rows.shape[0]
    ctxs = (c0, c1, c2, c3)
    columns = 3 * head_size
    first = seq + seq // 2
    weights = [
        jnp.concatenate(
            [c[first + j * columns : first + (j + 1) * columns, :] for j in range(width // 128)],
            axis=1,
        )
        for c in ctxs
    ]
    pair = 2 * head_size
    packed = [
        jnp.concatenate([weights[2 * i][0:pair, :], weights[2 * i + 1][0:pair, :]], axis=0)
        for i in range(2)
    ]
    last = jnp.concatenate([w[pair : pair + head_size, :] for w in weights], axis=0)
    for r0 in range(0, seq, own):
        at = slice(r0, r0 + own)
        left = jnp.concatenate([third(c, r0, own, seq) for c in ctxs], axis=1)
        total = mm(left, last)
        for i in range(2):
            left = jnp.concatenate([ctxs[2 * i][at, :], ctxs[2 * i + 1][at, :]], axis=1)
            total = total + mm(left, packed[i])
        total = total + x_all[at, :].astype(f32)
        h_one[at, :] = total.astype(bf16)
        h_one.flush(r0, own)
        sums[at, :] = total
        inv = lax.rsqrt(jnp.mean(total * total, axis=1, keepdims=True) + epsilon)
        normed[at, :] = (total * inv * gain[...]).astype(bf16)
    h_own[...] = sums[pl.ds(pl.multiple_of(t * own, own), own), :]
    h_own.flush()
    place = lax.broadcasted_iota(jnp.int32, (quarter, seq), 0) + t * quarter
    rows[...] = mm((place == code_row[...]).astype(bf16), normed[...]).astype(bf16)


def spread_body(t_ref, g0, g1, g2, g3, code_row, g_all, rows):
    t = t_ref[0]
    own = g0.shape[0]
    quarter = rows.shape[0]
    for k, ref in enumerate((g0, g1, g2, g3)):
        g_all[pl.ds(pl.multiple_of((t ^ k) * own, own), own), :] = ref[...]
    g_all.flush()
    place = lax.broadcasted_iota(jnp.int32, (quarter, g_all.shape[0]), 0) + t * quarter
    rows[...] = mm((place == code_row[...]).astype(bf16), g_all[...]).astype(bf16)


gelu_scale = 0.7978845608028654
gelu_cubic = 0.044715


def expert_body(
    near, e_ref, r0, r1, g0, g1, router, w_in_all, w_out_all,
    back0, back1, grad0, grad1, hidden_out, gated_out, pre_out, router_out,
    w_in, w_out, rows_all, g_rows, backs, grads, sem, out_sem,
):
    half = r0.shape[0]
    if near:
        load_in = pltpu.make_async_copy(w_in_all.at[e_ref[0]], w_in, sem.at[0])
        load_out = pltpu.make_async_copy(w_out_all.at[e_ref[0]], w_out, sem.at[1])
        load_in.start()
        load_out.start()
    else:
        w_in = w_in_all.at[e_ref[0]]
        w_out = w_out_all.at[e_ref[0]]
    rows_all[0] = r0[...]
    rows_all[1] = r1[...]
    g_rows[0] = g0[...]
    g_rows[1] = g1[...]
    router_out[...] = jnp.zeros(router_out.shape, f32)
    if near:
        load_in.wait()
        load_out.wait()
    sends = [
        [
            pltpu.make_async_copy(backs.at[i], back, out_sem.at[2 * i]),
            pltpu.make_async_copy(grads.at[i], grad, out_sem.at[2 * i + 1]),
        ]
        for i, (back, grad) in enumerate(((back0, grad0), (back1, grad1)))
    ]

    def one_half(i, carry):
        first = pl.multiple_of(i * half, half)
        at = pl.ds(first, half)
        rows = rows_all[i]
        cot = g_rows[i].astype(f32)
        logits = mm_nt(rows, router[...])
        logits = jnp.exp(logits - jnp.max(logits, axis=1, keepdims=True))
        prob = logits / jnp.sum(logits, axis=1, keepdims=True)
        mine = lax.broadcasted_iota(jnp.int32, prob.shape, 1) == e_ref[1]
        gate = jnp.sum(jnp.where(mine, prob, 0.0), axis=1, keepdims=True)
        gated = (gate * cot).astype(bf16)
        gated_out[at, :] = gated
        pre = mm(rows, w_in[...])
        square = pre * pre
        inner = jnp.tanh(gelu_scale * pre * (1.0 + gelu_cubic * square))
        half_up = 0.5 + 0.5 * inner
        hidden = (pre * half_up).astype(bf16)
        hidden_out[at, :] = hidden
        slope = half_up + (0.5 * gelu_scale) * pre * (1.0 - inner * inner) * (
            1.0 + (3.0 * gelu_cubic) * square
        )
        part = mm(hidden, w_out[...])
        backs[i] = (gate * part).astype(bf16)
        grad_gate = jnp.sum(cot * part, axis=1, keepdims=True)
        grad_pre = (mm_nt(gated, w_out[...]) * slope).astype(bf16)
        pre_out[at, :] = grad_pre
        grad_logits = (gate * grad_gate * (jnp.where(mine, 1.0, 0.0) - prob)).astype(bf16)
        grads[i] = (mm_nt(grad_pre, w_in[...]) + mm(grad_logits, router[...])).astype(bf16)
        for n in range(2):

            @pl.when(i == n)
            def _(n=n):
                sends[n][0].start()
                sends[n][1].start()

        router_out[...] += mm_tn(grad_logits, rows)
        return carry

    lax.fori_loop(0, 2, one_half, 0)
    hidden_out.flush()
    gated_out.flush()
    pre_out.flush()
    for pair in sends:
        for one in pair:
            one.wait()


def expert(near, scalars, r0, r1, g0, g1, router, w_in, w_out):
    half, width = r0.shape
    hidden = w_in.shape[2]
    rows = 2 * half
    return run(
        functools.partial(expert_body, near),
        [shape((half, width), bf16)] * 4
        + [
            shape((rows, hidden), bf16),
            shape((rows, width), bf16),
            shape((rows, hidden), bf16),
            shape(router.shape, f32),
        ],
        [scalars, r0, r1, g0, g1, router, w_in, w_out],
        smem=(0,),
        hbm=(6, 7) if near else (),
        hbm_outs=(0, 1, 2, 3),
        stores=(4, 5, 6),
        scratch=[
            pltpu.VMEM((width, hidden), bf16),
            pltpu.VMEM((hidden, width), bf16),
            pltpu.VMEM((2, half, width), bf16),
            pltpu.VMEM((2, half, width), bf16),
            pltpu.VMEM((2, half, width), bf16),
            pltpu.VMEM((2, half, width), bf16),
            pltpu.SemaphoreType.DMA((2,)),
            pltpu.SemaphoreType.DMA((4,)),
        ],
        us=7,
        name="expert",
    )


def expert_grad_body(first, e_ref, r0, r1, hidden, gated, pre, *refs):
    d_in, d_out, sum_in, sum_out, sem = refs[-5:]
    rows = jnp.concatenate([r0[...], r1[...]], axis=0)
    sum_in[...] = mm_tn(rows, pre[...])
    store_in = pltpu.make_async_copy(sum_in, d_in.at[e_ref[0]], sem.at[0])
    store_in.start()
    sum_out[...] = mm_tn(hidden[...], gated[...])
    store_out = pltpu.make_async_copy(sum_out, d_out.at[e_ref[0]], sem.at[1])
    store_out.start()
    store_in.wait()
    store_out.wait()


def expert_grads(scalars, r0, r1, hidden, gated, pre, so_far=(), deps=()):
    columns, width = hidden.shape[1], gated.shape[1]
    return run(
        functools.partial(expert_grad_body, not so_far),
        [shape((2, width, columns), f32), shape((2, columns, width), f32)],
        [scalars, r0, r1, hidden, gated, pre, *so_far],
        smem=(0,),
        loads=(3, 4, 5),
        hbm=(6, 7),
        hbm_outs=(0, 1),
        aliases={6: 0, 7: 1} if so_far else None,
        deps=deps,
        scratch=[
            pltpu.VMEM((width, columns), f32),
            pltpu.VMEM((columns, width), f32),
            pltpu.SemaphoreType.DMA((2,)),
        ],
        us=4,
        name="expert_grads",
    )


def back_body(
    t_ref, b0, b1, b2, b3, code_col, h_one, gain, g_all, weight, ctx_cols, router,
    h_own, gctx, early, grad_h, slots, sums,
):
    t = t_ref[0]
    seq, width = h_one.shape
    own = seq // 4
    quarter = b0.shape[0]
    columns = gctx.shape[1]
    for j, ref in enumerate((b0, b1, b2, b3)):
        slots[pl.ds(pl.multiple_of((t ^ j) * quarter, quarter), quarter), :] = ref[...]
    sum_gain = jnp.zeros((1, width), f32)
    place = lax.broadcasted_iota(jnp.int32, (own, 4 * quarter), 1)
    for n, r0 in enumerate(range(0, seq, own)):
        at = slice(r0, r0 + own)
        total = mm((place == code_col[at, :]).astype(bf16), slots[...])
        h_one.piece(n)
        g_all.piece(n)
        h = h_one.buffer[at, :].astype(f32)
        inv = lax.rsqrt(jnp.mean(h * h, axis=1, keepdims=True) + epsilon)
        n2 = h * inv
        sum_gain = sum_gain + jnp.sum(total * n2, axis=0, keepdims=True)
        a = total * gain[...]
        mean = jnp.mean(a * n2, axis=1, keepdims=True)
        full = g_all.buffer[at, :].astype(f32) + inv * (a - n2 * mean)
        grad_h[at, :] = full.astype(bf16)
        sums[at, :] = full
    h_own[...] = sums[pl.ds(pl.multiple_of(t * own, own), own), :]
    h_own.flush()
    gctx[...] = mm_nt(grad_h[...], weight[...]).astype(bf16)
    gctx.flush()
    early[0:columns, :] = mm(ctx_cols[...], grad_h[...]).astype(bf16)
    rest = jnp.concatenate([router[...], sum_gain], axis=0)
    spare = early.shape[0] - columns - rest.shape[0]
    rest = jnp.concatenate([rest, jnp.zeros((spare, width), f32)], axis=0)
    early[columns:, :] = rest.astype(bf16)


def attend_back_body(
    gctx, value_cols, key_rows, query_cols, probs, normed, near,
    grad_q, grad_k, grad_v, late, grad_bias, spill, sum_k, sum_v,
):
    seq, columns = gctx.shape
    heads = columns // head_size
    buckets = grad_bias.shape[0]
    spill[...] = jnp.zeros(spill.shape, f32)
    sum_k[...] = jnp.zeros(sum_k.shape, f32)
    sum_v[...] = jnp.zeros(sum_v.shape, f32)
    gctx_cols = gctx[...].T
    for n, i0 in enumerate(range(0, seq, rows_q)):
        start, end, off = span(i0, seq)
        keys = end - start
        at = slice(i0, i0 + rows_q)
        grad = mm(stack_heads(gctx[at, :], heads), value_cols[:, start:end])
        probs.piece(n)
        prob = probs.buffer[:, at, 0:keys].reshape(heads * rows_q, keys)
        wide = prob.astype(f32)
        both = wide * grad
        score = both - wide * jnp.sum(both, axis=1, keepdims=True)
        spill[:, :, off : off + keys] += score.reshape(heads, rows_q, keys)
        score = score.astype(bf16)
        grad_q[at, :] = own_heads(mm(score, key_rows[start:end, :]), heads).astype(bf16)
        for h in range(heads):
            cols = slice(h * head_size, (h + 1) * head_size)
            mine = slice(h * rows_q, (h + 1) * rows_q)
            sum_k[cols, start:end] += mm(query_cols[cols, at], score[mine])
            sum_v[cols, start:end] += mm(gctx_cols[cols, at], prob[mine])
    grad_k[...] = sum_k[...].astype(bf16)
    grad_v[...] = sum_v[...].astype(bf16)
    grad_q.flush()
    grad_k.flush()
    grad_v.flush()
    late[0:columns, :] = mm_tn(grad_q[...], normed[...]).astype(bf16)
    late[columns : 2 * columns, :] = mm(grad_k[...], normed[...]).astype(bf16)
    late[2 * columns : 3 * columns, :] = mm(grad_v[...], normed[...]).astype(bf16)
    chosen = near[...] == lax.broadcasted_iota(jnp.int32, (buckets, table), 0)
    places = lax.broadcasted_iota(jnp.int32, (buckets, 128), 1)
    found = jnp.zeros((buckets, 128), f32)
    for h in range(heads):
        strip = jnp.zeros((8, table), f32)
        for a in range(0, rows_q, 8):
            strip = strip + pltpu.roll(spill[h, a : a + 8, :], (table - a) % table, 1)
        line = lax.broadcasted_iota(jnp.int32, strip.shape, 0)
        for bit in (1, 2, 4):
            strip = jnp.where((line & bit) != 0, pltpu.roll(strip, table - bit, 1), strip)
        strip = jnp.sum(strip, axis=0, keepdims=True)
        per = jnp.sum(jnp.where(chosen, strip, 0.0), axis=1, keepdims=True)
        found = found + jnp.where(places == h, per, 0.0)
    grad_bias[...] = found


def input_grad_body(t_ref, grad_q, grad_k, grad_v, weight, normed, gain, keep, send, sums):
    t = t_ref[0]
    seq, width = normed.shape
    own = seq // 4
    total_gain = jnp.zeros((1, width), f32)
    for k in range(4):
        at = pl.ds(pl.multiple_of((t ^ k) * own, own), own)
        part = mm(grad_q[at, :], weight[0])
        part = part + mm_tn(grad_k[:, at], weight[1])
        part = part + mm_tn(grad_v[:, at], weight[2])
        total_gain = total_gain + jnp.sum(part * normed[at, :].astype(f32), axis=0, keepdims=True)
        out = keep if k in (0, 2) else send
        out[(k // 2) * own : (k // 2 + 1) * own, :] = part.astype(bf16)
    sums[...] = total_gain / gain[...]


def sum_copies(copies, ref):
    full = ref[...].astype(f32)
    rows = full.shape[0] // copies
    total = full[0:rows]
    for i in range(1, copies):
        total = total + full[i * rows : (i + 1) * rows]
    return total


def share_body(copies, early, late, sums, grad_bias, out):
    width = early.shape[1]
    found = grad_bias[...]
    lanes = found.shape[1]
    found = jnp.concatenate([found, jnp.zeros((lanes - found.shape[0], lanes), f32)], axis=0).T
    found = jnp.concatenate([found[0:8], jnp.zeros((8, width - lanes), f32)], axis=1)
    line = lax.broadcasted_iota(jnp.int32, found.shape, 0)
    found = jnp.where(line == 7, sums[...], found)
    total = [found, sum_copies(copies, early), sum_copies(copies, late)]
    out[...] = jnp.concatenate(total, axis=0).astype(bf16)


def finish_body(early_rows, i_ref, *refs):
    shares = refs[:-7]
    qkv, out, bias, gain_attn, gain_moe, router, early = refs[-7:]
    columns = out.shape[0]
    experts = router.shape[0]
    small = None
    for j, ref in enumerate(shares):
        full = ref[...].astype(f32)
        owner = i_ref[0] ^ j
        small = full[0:8] if small is None else small + full[0:8]
        early[owner] = full[8 : 8 + early_rows]
        qkv[owner] = full[8 + early_rows :]
    whole = jnp.concatenate([early[i] for i in range(early.shape[0])], axis=0)
    out[...] = whole[0:columns]
    router[...] = whole[columns : columns + experts]
    gain_moe[...] = whole[columns + experts]
    bias[...] = small[0 : bias.shape[0], 0 : bias.shape[1]]
    gain_attn[...] = small[7]


def last_body(kept, got, far, x_ref, gain, h_own, grad):
    total = kept[...].astype(f32) + got[...].astype(f32) + far[...].astype(f32)
    x = x_ref[...].astype(f32)
    inv = lax.rsqrt(jnp.mean(x * x, axis=1, keepdims=True) + epsilon)
    n1 = x * inv
    a = total * gain[...]
    grad[...] = h_own[...] + inv * (a - n1 * jnp.mean(a * n1, axis=1, keepdims=True))


def output_body(t_ref, f0, f1, f2, f3, code_col, h_own, out, slots):
    t = t_ref[0]
    own = h_own.shape[0]
    quarter = f0.shape[0]
    for j, ref in enumerate((f0, f1, f2, f3)):
        slots[pl.ds(pl.multiple_of((t ^ j) * quarter, quarter), quarter), :] = ref[...]
    codes = code_col[pl.ds(pl.multiple_of(t * own, own), own), :]
    place = lax.broadcasted_iota(jnp.int32, (own, 4 * quarter), 1)
    out[...] = (h_own[...] + mm((place == codes).astype(bf16), slots[...])).astype(bf16)


def turn(value):
    return lax.all_to_all(value, "dp", split_axis=0, concat_axis=0, tiled=True)


def per_device(
    inputs,
    segments,
    buckets,
    routes,
    qkv_weight,
    out_weight,
    rel_bias,
    norm_attn,
    norm_moe,
    router_weight,
    expert_in,
    expert_out,
    cotangent,
):
    own, width = inputs.shape
    seq = 4 * own
    dp = lax.axis_size("dp")
    experts = router_weight.shape[1]
    capacity = max(2, 5 * seq // (4 * experts))
    quarter = (experts // 2) * (capacity // 2)
    heads = rel_bias.shape[1]
    columns = heads * head_size
    t_one = lax.axis_index("tensor").astype(jnp.int32)[None]
    x_side = t_one >> 1
    dp_one = lax.axis_index("dp").astype(jnp.int32)[None]
    first_expert = 2 * dp_one
    near_expert = jnp.concatenate([x_side, first_expert + x_side])
    far_expert = jnp.concatenate([1 - x_side, first_expert + 1 - x_side])
    inputs, t_one, dp_one, near_expert, far_expert = lax.optimization_barrier(
        (inputs, t_one, dp_one, near_expert, far_expert)
    )
    gain_attn = norm_attn[None, :]
    gain_moe = norm_moe[None, :]
    near = lax.slice_in_dim(buckets, seq - 1 - reach, seq - 1 - reach + table, axis=0)[None, :]
    weight = jnp.swapaxes(qkv_weight, 1, 2)
    router = router_weight.T

    code_row, code_col, seg_col, tile = run(
        functools.partial(slots_body, experts, capacity),
        [
            shape((1, seq), jnp.int32),
            shape((seq, 1), jnp.int32),
            shape((seq, 1), jnp.int32),
            shape((heads, rows_q, window), f32),
        ],
        [routes.reshape(1, seq), segments, near, rel_bias.T],
        smem=(3,),
        us=2,
        stores=(3,),
        name="slots",
    )
    xs = gather4(inputs, code_row)
    x_all, normed, ctx = run(
        attend_body,
        [
            shape((seq, width), bf16),
            shape((seq, width), bf16),
            shape((seq + seq // 2 + columns * width // 128, 128), bf16),
        ],
        [t_one, *xs, gain_attn, weight, segments, seg_col, tile, out_weight],
        smem=(0,),
        scratch=[
            pltpu.VMEM((seq, columns), bf16),
            pltpu.VMEM((columns, seq), bf16),
            pltpu.VMEM((seq, columns + head_size), bf16),
        ],
        us=10,
        loads=(1, 6, 9, 10),
        stores=(0, 1, 2),
        name="attend",
    )
    gs = gather4(cotangent, ctx)
    g_all, g_rows = run(
        spread_body,
        [shape((seq, width), bf16), shape((quarter, width), bf16)],
        [t_one, *gs, code_row],
        smem=(0,),
        us=0.1,
        loads=(1,),
        stores=(0,),
        name="spread",
    )
    cs = gather4(ctx, g_rows)
    h_one, h_own, rows = run(
        mid_body,
        [
            shape((seq, width), bf16),
            shape((own, width), f32),
            shape((quarter, width), bf16),
        ],
        [t_one, x_all, *cs, gain_moe, code_row],
        smem=(0,),
        scratch=[pltpu.VMEM((seq, width), bf16), pltpu.VMEM((seq, width), f32)],
        us=0.1,
        loads=(2, 1),
        stores=(0, 1),
        name="mid",
    )
    g_got = turn(g_rows)
    query_cols, value_cols, ctx_cols = run(
        columns_body,
        [shape((columns, seq), bf16)] * 3,
        [normed, weight, ctx],
        deps=[rows],
        us=3,
        loads=(0, 1, 2),
        stores=(0, 1, 2),
        name="columns",
    )
    g_far = x_hop(after(g_got, query_cols))
    probs, key_rows = run(
        probs_body,
        [shape((heads, seq, window), bf16), shape((seq, columns), bf16)],
        [normed, weight, segments, seg_col, tile],
        deps=[query_cols],
        scratch=[pltpu.VMEM((seq, columns), bf16)],
        us=7,
        loads=(0, 1, 4),
        stores=(0, 1),
        name="probs",
    )
    row_got = after(turn(rows), probs)
    near_rows = (row_got, core_hop(row_got))
    g_near = after(g_got, probs)
    near_out = expert(
        True, near_expert, *near_rows, g_near, core_hop(g_near), router, expert_in, expert_out
    )
    far_mine = after(x_hop(row_got), near_out[0])
    far_rows = (far_mine, core_hop(far_mine))
    far_out = expert(
        False, far_expert, *far_rows, g_far, core_hop(g_far), router, expert_in, expert_out
    )
    far = far_out[2] + core_hop(far_out[3])
    router_part = near_out[7] + far_out[7]
    router_part = router_part + core_hop(router_part)
    router_far = x_hop(router_part)
    weight_grads = expert_grads(near_expert, *near_rows, *near_out[4:7], deps=[far])
    far, router_far = lax.optimization_barrier((x_hop(far), router_far, weight_grads[0]))[:2]
    router_part = router_part + router_far
    kept = near_out[2] + core_hop(near_out[3]) + far
    home = turn(kept)
    far = after(far_out[0], kept) + core_hop(far_out[1])
    weight_grads = expert_grads(
        far_expert, *far_rows, *far_out[4:7], so_far=weight_grads, deps=[far]
    )
    home = after(home, weight_grads[0])
    fwd = after(near_out[0], home) + core_hop(near_out[1]) + x_hop(far)
    bs = gather4(home, fwd)
    fwd = turn(fwd)
    small = -(-(experts + 1) // 64) * 64
    gh_own, gctx, early = run(
        back_body,
        [
            shape((own, width), f32),
            shape((seq, columns), bf16),
            shape((columns + small, width), bf16),
        ],
        [t_one, *bs, code_col, h_one, gain_moe, g_all, out_weight, ctx_cols, router_part],
        smem=(0,),
        loads=((6, 4, 0), (8, 4, 0), 9, 10),
        stores=(0, 1),
        scratch=[
            pltpu.VMEM((seq, width), bf16),
            pltpu.VMEM((4 * quarter, width), bf16),
            pltpu.VMEM((seq, width), f32),
        ],
        us=2,
        name="back",
    )
    early_got = turn(early)
    grad_q, grad_k, grad_v, late, grad_bias = run(
        attend_back_body,
        [
            shape((seq, columns), bf16),
            shape((columns, seq), bf16),
            shape((columns, seq), bf16),
            shape((3 * columns, width), bf16),
            shape((rel_bias.shape[0], 128), f32),
        ],
        [gctx, value_cols, key_rows, query_cols, probs, normed, near],
        loads=(0, 1, 2, 3, (4, seq // rows_q, 1), 5),
        stores=(0, 1, 2),
        deps=[fwd],
        scratch=[
            pltpu.VMEM((heads, rows_q, table), f32),
            pltpu.VMEM((columns, seq), f32),
            pltpu.VMEM((columns, seq), f32),
        ],
        us=14,
        name="attend_back",
    )
    f_far = x_hop(after(fwd, gctx))
    fs = (fwd, core_hop(fwd), f_far, core_hop(f_far))
    late_got = turn(after(late, f_far))
    keep, send, gain_part = run(
        input_grad_body,
        [
            shape((2 * own, width), bf16),
            shape((2 * own, width), bf16),
            shape((1, width), f32),
        ],
        [t_one, grad_q, grad_k, grad_v, weight, normed, gain_attn],
        smem=(0,),
        us=0.1,
        loads=(1, 2, 3, 4, 5),
        name="input_grad",
    )
    gain_part = gain_part + core_hop(gain_part)
    gain_part = gain_part + x_hop(gain_part)
    keep, send = lax.optimization_barrier((keep, send, gain_part))[:2]
    got = core_hop(send)
    far = x_hop(keep[own:] + got[own:])
    (grad_inputs,) = run(
        last_body,
        [shape((own, width), f32)],
        [keep[:own], got[:own], far, inputs, gain_attn, gh_own],
        loads=(3, 5),
        us=0.1,
        name="last",
    )
    (output,) = run(
        output_body,
        [shape((own, width), bf16)],
        [t_one, *fs, code_col, h_own],
        smem=(0,),
        loads=(6,),
        scratch=[pltpu.VMEM((4 * quarter, width), bf16)],
        us=0.1,
        name="output",
    )
    early_rows = early.shape[0] // dp
    late_rows = late.shape[0] // dp
    (share,) = run(
        functools.partial(share_body, dp),
        [shape((8 + early_rows + late_rows, width), bf16)],
        [early_got, late_got, gain_part, grad_bias],
        deps=[output],
        us=1,
        name="share",
    )
    shares = [share]
    for j in range(2, dp, 2):
        shares.append(lax.ppermute(share, "dp", [(i, i ^ j) for i in range(dp)]))
    shares = [
        one
        for share in shares
        for one in (share, lax.ppermute(share, "dp", [(i, i ^ 1) for i in range(dp)]))
    ]
    qkv_grad, out_grad, bias_grad, gain_attn_grad, gain_moe_grad, router_grad = run(
        functools.partial(finish_body, early_rows),
        [
            shape((dp, late_rows, width), f32),
            shape((columns, width), f32),
            shape((heads, rel_bias.shape[0]), f32),
            shape((width,), f32),
            shape((width,), f32),
            shape((experts, width), f32),
        ],
        [dp_one, *shares],
        smem=(0,),
        scratch=[pltpu.VMEM((dp, early_rows, width), f32)],
        us=2,
        name="finish",
    )
    return (
        output,
        grad_inputs,
        jnp.swapaxes(qkv_grad.reshape(3, columns, width), 1, 2),
        out_grad,
        bias_grad.T,
        gain_attn_grad,
        gain_moe_grad,
        router_grad.T,
        *weight_grads,
    )


def solution(mesh):
    placed = (
        P(("dp", "tensor"), None),
        P("dp", None),
        P(),
        P("dp", None, None),
        P(None, None, "tensor"),
        P("tensor", None),
        P(None, "tensor"),
        P(),
        P(),
        P(),
        P("dp", None, "tensor"),
        P("dp", "tensor", None),
        P(("dp", "tensor"), None),
    )
    return jax.shard_map(
        per_device,
        mesh=mesh,
        in_specs=placed,
        out_specs=(
            P(("dp", "tensor"), None),
            P(("dp", "tensor"), None),
            P(None, None, "tensor"),
            P("tensor", None),
            P(None, "tensor"),
            P(),
            P(),
            P(),
            P("dp", None, "tensor"),
            P("dp", "tensor", None),
        ),
        check_vma=False,
    )
```

```python
import functools

import jax
import jax.numpy as jnp
from jax import lax
from jax.experimental import pallas as pl
from jax.experimental.pallas import tpu as pltpu
from jax.sharding import PartitionSpec as P

epsilon = 1e-06
negative = -1000000000.0
bf16 = jnp.bfloat16
f32 = jnp.float32
reach = 256
rows_q = 128
window = rows_q + 2 * reach
table = window + rows_q
head_size = 64
mega = 1024 * 1024

core_pairs = [(0, 1), (1, 0), (2, 3), (3, 2)]
x_pairs = [(0, 2), (2, 0), (1, 3), (3, 1)]


def core_hop(value):
    return lax.ppermute(value, "tensor", core_pairs)


def x_hop(value):
    return lax.ppermute(value, "tensor", x_pairs)


def after(value, *deps):
    return lax.optimization_barrier((value, *deps))[0]


def gather4(value, *deps):
    other = x_hop(value)
    if deps:
        other = after(other, *deps)
    return value, core_hop(value), other, core_hop(other)


def dot(a, b, dims):
    return lax.dot_general(a, b, (dims, ((), ())), preferred_element_type=f32)


def mm(a, b):
    return dot(a, b, ((1,), (0,)))


def mm_nt(a, b):
    return dot(a, b, ((1,), (1,)))


def mm_tn(a, b):
    return dot(a, b, ((0,), (0,)))


def shape(dims, kind):
    return jax.ShapeDtypeStruct(dims, kind)


class Loaded:
    def __init__(self, source, buffer, sems, axis=0):
        self.buffer, self.axis = buffer, axis
        self.shape, self.dtype = buffer.shape, buffer.dtype
        count = len(sems)
        self.step = self.shape[axis] // count
        self.copies = []
        for i, sem in enumerate(sems):
            at = self.place(i) if count > 1 else ()
            part = (source.at[at], buffer.at[at]) if at else (source, buffer)
            self.copies.append(pltpu.make_async_copy(*part, sem))
            self.copies[-1].start()
        self.here = [False] * count

    def place(self, i):
        return (slice(None),) * self.axis + (pl.ds(i * self.step, self.step),)

    def piece(self, i):
        if not self.here[i]:
            self.copies[i].wait()
            self.here[i] = True

    def wait(self):
        for i in range(len(self.copies)):
            self.piece(i)

    def __getitem__(self, place):
        self.wait()
        return self.buffer[place]


class Stored:
    def __init__(self, target, buffer, sem):
        self.buffer, self.target, self.sem = buffer, target, sem
        self.shape, self.dtype = buffer.shape, buffer.dtype
        self.gone = 0

    def flush(self, first=0, rows=None):
        rows = self.shape[0] if rows is None else rows
        at = pl.ds(first, rows)
        pltpu.make_async_copy(self.buffer.at[at], self.target.at[at], self.sem).start()
        self.gone += rows

    def close(self):
        if not self.gone:
            self.flush()

    def wait(self):
        pltpu.make_async_copy(self.buffer, self.target, self.sem).wait()

    def __getitem__(self, place):
        return self.buffer[place]

    def __setitem__(self, place, value):
        self.buffer[place] = value


def run(
    body, outs, args, smem=(), loads=(), stores=(), hbm=(), hbm_outs=(), deps=(), aliases=None,
    scratch=(), us=2, name=None,
):
    args = list(args)
    if deps:
        args[0] = after(args[0], *deps)
    n_in, n_out, n_own = len(args), len(outs), len(scratch)
    cuts = [one if isinstance(one, tuple) else (one, 1, 0) for one in loads]
    loads = [one[0] for one in cuts]
    n_sems = sum(one[1] for one in cuts) + len(stores)

    def inner(*refs):
        ins = list(refs[:n_in])
        results = list(refs[n_in : n_in + n_out])
        own = refs[n_in + n_out : n_in + n_out + n_own]
        rest = refs[n_in + n_out + n_own :]
        buffers, sems = rest[:-1], rest[-1]
        used = 0
        for n, (i, pieces, axis) in enumerate(cuts):
            mine = [sems.at[used + j] for j in range(pieces)]
            ins[i] = Loaded(ins[i], buffers[n], mine, axis)
            used += pieces
        for n, i in enumerate(stores):
            results[i] = Stored(results[i], buffers[len(loads) + n], sems.at[used + n])
        body(*ins, *results, *own)
        for i in loads:
            ins[i].wait()
        for i in stores:
            results[i].close()
        for i in stores:
            results[i].wait()

    def space(i):
        if i in smem:
            return pltpu.SMEM
        return pltpu.HBM if i in hbm or i in loads else pltpu.VMEM

    for i in (*loads, *hbm):
        if i < n_in:
            args[i] = pltpu.with_memory_space_constraint(args[i], pltpu.HBM)
    kinds = [
        pltpu.HBM(o.shape, o.dtype) if i in hbm_outs or i in stores else o
        for i, o in enumerate(outs)
    ]
    staged = [pltpu.VMEM(args[i].shape, args[i].dtype) for i in loads]
    staged += [pltpu.VMEM(outs[i].shape, outs[i].dtype) for i in stores]
    return pl.pallas_call(
        inner,
        out_shape=kinds,
        in_specs=[pl.BlockSpec(memory_space=space(i)) for i in range(n_in)],
        out_specs=[
            pl.BlockSpec(
                memory_space=pltpu.HBM if i in hbm_outs or i in stores else pltpu.VMEM
            )
            for i in range(n_out)
        ],
        scratch_shapes=[
            *scratch, *staged, pltpu.SemaphoreType.DMA((max(1, n_sems),))
        ],
        input_output_aliases=aliases or {},
        compiler_params=pltpu.CompilerParams(vmem_limit_bytes=44 * mega),
        cost_estimate=pl.CostEstimate(
            flops=int(us * 1.1e9), bytes_accessed=mega // 4, transcendentals=0
        ),
        name=name,
    )(*args)


def as_column(row):
    wide = jnp.broadcast_to(row.astype(f32), (8, row.shape[1]))
    return wide.T[:, 0:1].astype(jnp.int32)


def slots_body(
    experts, capacity, row_ref, seg_row, near, bias, code_row, code_col, seg_col, tile
):
    seq = row_ref.shape[1]
    half = capacity // 2
    quarter = (experts // 2) * half
    first = lax.broadcasted_iota(jnp.int32, (seq, seq), 0)
    second = lax.broadcasted_iota(jnp.int32, (seq, seq), 1)
    route = row_ref[...]
    chosen = route == lax.broadcasted_iota(jnp.int32, (experts, seq), 0)
    count = mm(chosen.astype(bf16), (first < second).astype(bf16))
    slot = jnp.sum(jnp.where(chosen, count, 0.0), axis=0, keepdims=True).astype(jnp.int32)
    upper = jnp.where(slot >= half, 1, 0)
    code = (2 * (route & 1) + upper) * quarter + (route >> 1) * half + slot - half * upper
    code_row[...] = code
    code_col[...] = as_column(code)
    seg_col[...] = as_column(seg_row[...])
    bucket = near[...]
    for h in range(bias.shape[0]):
        line = jnp.zeros(bucket.shape, f32)
        for b in range(bias.shape[1]):
            line = jnp.where(bucket == b, bias[h, b], line)
        wide = jnp.broadcast_to(line, (rows_q, table))
        tile[h] = pltpu.roll(wide, 0, 1, stride=1, stride_axis=0)[:, :window]


def span(i0, seq):
    start = max(0, i0 - reach)
    end = min(seq, i0 + rows_q + reach)
    return start, end, start - (i0 - reach)


def masked_probs(score, same, tile):
    score = jnp.where(same, score + tile, negative)
    score = jnp.exp(score - jnp.max(score, axis=1, keepdims=True))
    return (score * (1.0 / jnp.sum(score, axis=1, keepdims=True))).astype(bf16)


def stack_heads(block, heads):
    lane = lax.broadcasted_iota(jnp.int32, block.shape, 1) // head_size
    return jnp.concatenate(
        [jnp.where(lane == h, block, jnp.zeros_like(block)) for h in range(heads)], axis=0
    )


def own_heads(stacked, heads):
    rows = stacked.shape[0] // heads
    lane = lax.broadcasted_iota(jnp.int32, (rows, stacked.shape[1]), 1) // head_size
    out = stacked[(heads - 1) * rows :]
    for h in range(heads - 1):
        out = jnp.where(lane == h, stacked[h * rows : (h + 1) * rows], out)
    return out


def masked_exp(score, same, tile):
    heads, rows, keys = tile.shape
    score = score.reshape(heads, rows, keys) + tile
    score = jnp.where(same[None], score, negative)
    return jnp.exp(score - jnp.max(score, axis=2, keepdims=True))


def attend_body(
    t_ref, x0, x1, x2, x3, gain, weight, seg_row, seg_col, tile, out_weight,
    x_all, normed, ctx, query, key, value,
):
    t = t_ref[0]
    own = x0.shape[0]
    seq = 4 * own
    heads = tile.shape[0]
    columns = heads * head_size
    for k, ref in ((1, x1), (2, x2), (3, x3), (0, x0)):
        at = pl.ds(pl.multiple_of((t ^ k) * own, own), own)
        x = ref[...]
        x_all[at, :] = x
        x = x.astype(f32)
        inv = lax.rsqrt(jnp.mean(x * x, axis=1, keepdims=True) + epsilon)
        normed[at, :] = (x * inv * gain[...]).astype(bf16)
    x_all.flush()
    normed.flush()
    query[...] = mm_nt(normed[...], weight[0]).astype(bf16)
    key[...] = mm_nt(weight[1], normed[...]).astype(bf16)
    value[:, 0:columns] = mm_nt(normed[...], weight[2]).astype(bf16)
    value[:, columns:] = jnp.ones((seq, head_size), bf16)
    for i0 in range(0, seq, rows_q):
        start, end, off = span(i0, seq)
        same = seg_col[i0 : i0 + rows_q, :] == seg_row[:, start:end]
        score = mm(stack_heads(query[i0 : i0 + rows_q, :], heads), key[:, start:end])
        weights = masked_exp(score, same, tile[:, :, off : off + end - start]).astype(bf16)
        out = mm(weights.reshape(heads * rows_q, end - start), value[start:end, :])
        out = out[:, 0:columns] * (1.0 / out[:, columns : columns + 1])
        out = own_heads(out, heads).astype(bf16)
        ctx[i0 : i0 + rows_q, :] = out[:, 0 : 2 * head_size]
        lane = 0 if i0 < seq // 2 else head_size
        at = seq + i0 % (seq // 2)
        ctx[at : at + rows_q, lane : lane + head_size] = out[:, 2 * head_size :]
    first = seq + seq // 2
    for j in range(out_weight.shape[1] // 128):
        ctx[first + j * columns : first + (j + 1) * columns, :] = out_weight[
            :, j * 128 : (j + 1) * 128
        ]


def probs_body(normed, weight, seg_row, seg_col, tile, probs, key_rows, query):
    seq = normed.shape[0]
    heads = tile.shape[0]
    query[...] = mm_nt(normed[...], weight[0]).astype(bf16)
    key_rows[...] = mm_nt(normed[...], weight[1]).astype(bf16)
    for i0 in range(0, seq, rows_q):
        start, end, off = span(i0, seq)
        same = seg_col[i0 : i0 + rows_q, :] == seg_row[:, start:end]
        score = mm_nt(stack_heads(query[i0 : i0 + rows_q, :], heads), key_rows[start:end, :])
        weights = masked_exp(score, same, tile[:, :, off : off + end - start])
        inv = 1.0 / jnp.sum(weights, axis=2, keepdims=True)
        probs[:, i0 : i0 + rows_q, 0 : end - start] = (weights * inv).astype(bf16)


def columns_body(normed, weight, ctx, query_cols, value_cols, ctx_cols):
    seq = normed.shape[0]
    columns = weight.shape[1]
    query_cols[...] = mm_nt(weight[0], normed[...]).astype(bf16)
    value_cols[...] = mm_nt(weight[2], normed[...]).astype(bf16)
    pair = 2 * head_size
    ctx_cols[0:pair, :] = ctx[0:seq, :].T
    last = ctx[seq : seq + seq // 2, :].T
    ctx_cols[pair:columns, 0 : seq // 2] = last[0:head_size, :]
    ctx_cols[pair:columns, seq // 2 :] = last[head_size:, :]


def third(ctx, r0, rows, seq):
    lane = 0 if r0 < seq // 2 else head_size
    at = seq + r0 % (seq // 2)
    return ctx[at : at + rows, lane : lane + head_size]


def mid_body(
    t_ref, x_all, c0, c1, c2, c3, gain, code_row,
    h_one, h_own, rows, normed, sums,
):
    t = t_ref[0]
    seq, width = x_all.shape
    own = seq // 4
    quarter = rows.shape[0]
    ctxs = (c0, c1, c2, c3)
    columns = 3 * head_size
    first = seq + seq // 2
    weights = [
        jnp.concatenate(
            [c[first + j * columns : first + (j + 1) * columns, :] for j in range(width // 128)],
            axis=1,
        )
        for c in ctxs
    ]
    pair = 2 * head_size
    packed = [
        jnp.concatenate([weights[2 * i][0:pair, :], weights[2 * i + 1][0:pair, :]], axis=0)
        for i in range(2)
    ]
    last = jnp.concatenate([w[pair : pair + head_size, :] for w in weights], axis=0)
    for r0 in range(0, seq, own):
        at = slice(r0, r0 + own)
        left = jnp.concatenate([ctxs[2][at, :], ctxs[3][at, :]], axis=1)
        total = mm(left, packed[1])
        left = jnp.concatenate([ctxs[0][at, :], ctxs[1][at, :]], axis=1)
        total = total + mm(left, packed[0])
        left = jnp.concatenate([third(c, r0, own, seq) for c in ctxs], axis=1)
        total = total + mm(left, last)
        total = total + x_all[at, :].astype(f32)
        h_one[at, :] = total.astype(bf16)
        h_one.flush(r0, own)
        sums[at, :] = total
        inv = lax.rsqrt(jnp.mean(total * total, axis=1, keepdims=True) + epsilon)
        normed[at, :] = (total * inv * gain[...]).astype(bf16)
    h_own[...] = sums[pl.ds(pl.multiple_of(t * own, own), own), :]
    h_own.flush()
    place = lax.broadcasted_iota(jnp.int32, (quarter, seq), 0) + t * quarter
    rows[...] = mm((place == code_row[...]).astype(bf16), normed[...]).astype(bf16)


def spread_body(t_ref, g0, g1, g2, g3, code_row, g_all, rows):
    t = t_ref[0]
    own = g0.shape[0]
    quarter = rows.shape[0]
    for k, ref in ((1, g1), (2, g2), (3, g3), (0, g0)):
        g_all[pl.ds(pl.multiple_of((t ^ k) * own, own), own), :] = ref[...]
    g_all.flush()
    place = lax.broadcasted_iota(jnp.int32, (quarter, g_all.shape[0]), 0) + t * quarter
    rows[...] = mm((place == code_row[...]).astype(bf16), g_all[...]).astype(bf16)


gelu_scale = 0.7978845608028654
gelu_cubic = 0.044715


def expert_body(
    near, e_ref, r0, r1, g0, g1, router, w_in_all, w_out_all,
    back0, back1, grad0, grad1, hidden_out, gated_out, pre_out, router_out,
    w_in, w_out, rows_all, g_rows, backs, grads, sem, out_sem,
):
    half = r0.shape[0]
    if near:
        load_in = pltpu.make_async_copy(w_in_all.at[e_ref[0]], w_in, sem.at[0])
        load_out = pltpu.make_async_copy(w_out_all.at[e_ref[0]], w_out, sem.at[1])
        load_in.start()
        load_out.start()
    else:
        w_in = w_in_all.at[e_ref[0]]
        w_out = w_out_all.at[e_ref[0]]
    rows_all[0] = r0[...]
    rows_all[1] = r1[...]
    g_rows[0] = g0[...]
    g_rows[1] = g1[...]
    router_out[...] = jnp.zeros(router_out.shape, f32)
    if near:
        load_in.wait()
        load_out.wait()
    sends = [
        [
            pltpu.make_async_copy(backs.at[i], back, out_sem.at[2 * i]),
            pltpu.make_async_copy(grads.at[i], grad, out_sem.at[2 * i + 1]),
        ]
        for i, (back, grad) in enumerate(((back0, grad0), (back1, grad1)))
    ]

    def one_half(i, carry):
        first = pl.multiple_of(i * half, half)
        at = pl.ds(first, half)
        rows = rows_all[i]
        cot = g_rows[i].astype(f32)
        logits = mm_nt(rows, router[...])
        logits = jnp.exp(logits - jnp.max(logits, axis=1, keepdims=True))
        prob = logits / jnp.sum(logits, axis=1, keepdims=True)
        mine = lax.broadcasted_iota(jnp.int32, prob.shape, 1) == e_ref[1]
        gate = jnp.sum(jnp.where(mine, prob, 0.0), axis=1, keepdims=True)
        gated = (gate * cot).astype(bf16)
        gated_out[at, :] = gated
        pre = mm(rows, w_in[...])
        square = pre * pre
        inner = jnp.tanh(gelu_scale * pre * (1.0 + gelu_cubic * square))
        half_up = 0.5 + 0.5 * inner
        hidden = (pre * half_up).astype(bf16)
        hidden_out[at, :] = hidden
        slope = half_up + (0.5 * gelu_scale) * pre * (1.0 - inner * inner) * (
            1.0 + (3.0 * gelu_cubic) * square
        )
        part = mm(hidden, w_out[...])
        backs[i] = (gate * part).astype(bf16)
        grad_gate = jnp.sum(cot * part, axis=1, keepdims=True)
        grad_pre = (mm_nt(gated, w_out[...]) * slope).astype(bf16)
        pre_out[at, :] = grad_pre
        grad_logits = (gate * grad_gate * (jnp.where(mine, 1.0, 0.0) - prob)).astype(bf16)
        grads[i] = (mm_nt(grad_pre, w_in[...]) + mm(grad_logits, router[...])).astype(bf16)
        for n in range(2):

            @pl.when(i == n)
            def _(n=n):
                sends[n][0].start()
                sends[n][1].start()

        router_out[...] += mm_tn(grad_logits, rows)
        return carry

    lax.fori_loop(0, 2, one_half, 0)
    hidden_out.flush()
    gated_out.flush()
    pre_out.flush()
    for pair in sends:
        for one in pair:
            one.wait()


def expert(near, scalars, r0, r1, g0, g1, router, w_in, w_out):
    half, width = r0.shape
    hidden = w_in.shape[2]
    rows = 2 * half
    return run(
        functools.partial(expert_body, near),
        [shape((half, width), bf16)] * 4
        + [
            shape((rows, hidden), bf16),
            shape((rows, width), bf16),
            shape((rows, hidden), bf16),
            shape(router.shape, f32),
        ],
        [scalars, r0, r1, g0, g1, router, w_in, w_out],
        smem=(0,),
        hbm=(6, 7) if near else (),
        hbm_outs=(0, 1, 2, 3),
        stores=(4, 5, 6),
        scratch=[
            pltpu.VMEM((width, hidden), bf16),
            pltpu.VMEM((hidden, width), bf16),
            pltpu.VMEM((2, half, width), bf16),
            pltpu.VMEM((2, half, width), bf16),
            pltpu.VMEM((2, half, width), bf16),
            pltpu.VMEM((2, half, width), bf16),
            pltpu.SemaphoreType.DMA((2,)),
            pltpu.SemaphoreType.DMA((4,)),
        ],
        us=7,
        name="expert",
    )


def expert_grad_body(first, e_ref, r0, r1, hidden, gated, pre, *refs):
    d_in, d_out, sum_in, sum_out, sem = refs[-5:]
    rows = jnp.concatenate([r0[...], r1[...]], axis=0)
    sum_in[...] = mm_tn(rows, pre[...])
    store_in = pltpu.make_async_copy(sum_in, d_in.at[e_ref[0]], sem.at[0])
    store_in.start()
    sum_out[...] = mm_tn(hidden[...], gated[...])
    store_out = pltpu.make_async_copy(sum_out, d_out.at[e_ref[0]], sem.at[1])
    store_out.start()
    store_in.wait()
    store_out.wait()


def expert_grads(scalars, r0, r1, hidden, gated, pre, so_far=(), deps=()):
    columns, width = hidden.shape[1], gated.shape[1]
    return run(
        functools.partial(expert_grad_body, not so_far),
        [shape((2, width, columns), f32), shape((2, columns, width), f32)],
        [scalars, r0, r1, hidden, gated, pre, *so_far],
        smem=(0,),
        loads=(3, 4, 5),
        hbm=(6, 7),
        hbm_outs=(0, 1),
        aliases={6: 0, 7: 1} if so_far else None,
        deps=deps,
        scratch=[
            pltpu.VMEM((width, columns), f32),
            pltpu.VMEM((columns, width), f32),
            pltpu.SemaphoreType.DMA((2,)),
        ],
        us=4,
        name="expert_grads",
    )


def back_body(
    t_ref, b0, b1, b2, b3, code_col, h_one, gain, g_all, weight, ctx_cols, router,
    h_own, gctx, early, grad_h, slots, sums,
):
    t = t_ref[0]
    seq, width = h_one.shape
    own = seq // 4
    quarter = b0.shape[0]
    columns = gctx.shape[1]
    for j, ref in enumerate((b0, b1, b2, b3)):
        slots[pl.ds(pl.multiple_of((t ^ j) * quarter, quarter), quarter), :] = ref[...]
    sum_gain = jnp.zeros((1, width), f32)
    place = lax.broadcasted_iota(jnp.int32, (own, 4 * quarter), 1)
    for n, r0 in enumerate(range(0, seq, own)):
        at = slice(r0, r0 + own)
        total = mm((place == code_col[at, :]).astype(bf16), slots[...])
        h_one.piece(n)
        g_all.piece(n)
        h = h_one.buffer[at, :].astype(f32)
        inv = lax.rsqrt(jnp.mean(h * h, axis=1, keepdims=True) + epsilon)
        n2 = h * inv
        sum_gain = sum_gain + jnp.sum(total * n2, axis=0, keepdims=True)
        a = total * gain[...]
        mean = jnp.mean(a * n2, axis=1, keepdims=True)
        full = g_all.buffer[at, :].astype(f32) + inv * (a - n2 * mean)
        grad_h[at, :] = full.astype(bf16)
        sums[at, :] = full
    h_own[...] = sums[pl.ds(pl.multiple_of(t * own, own), own), :]
    h_own.flush()
    gctx[...] = mm_nt(grad_h[...], weight[...]).astype(bf16)
    gctx.flush()
    early[0:columns, :] = mm(ctx_cols[...], grad_h[...]).astype(bf16)
    rest = jnp.concatenate([router[...], sum_gain], axis=0)
    spare = early.shape[0] - columns - rest.shape[0]
    rest = jnp.concatenate([rest, jnp.zeros((spare, width), f32)], axis=0)
    early[columns:, :] = rest.astype(bf16)


def attend_back_body(
    gctx, value_cols, key_rows, query_cols, probs, normed, near,
    grad_q, grad_k, grad_v, late, grad_bias, spill, sum_k, sum_v,
):
    seq, columns = gctx.shape
    heads = columns // head_size
    buckets = grad_bias.shape[0]
    spill[...] = jnp.zeros(spill.shape, f32)
    sum_k[...] = jnp.zeros(sum_k.shape, f32)
    sum_v[...] = jnp.zeros(sum_v.shape, f32)
    gctx_cols = gctx[...].T
    for n, i0 in enumerate(range(0, seq, rows_q)):
        start, end, off = span(i0, seq)
        keys = end - start
        at = slice(i0, i0 + rows_q)
        grad = mm(stack_heads(gctx[at, :], heads), value_cols[:, start:end])
        probs.piece(n)
        prob = probs.buffer[:, at, 0:keys].reshape(heads * rows_q, keys)
        wide = prob.astype(f32)
        both = wide * grad
        score = both - wide * jnp.sum(both, axis=1, keepdims=True)
        spill[:, :, off : off + keys] += score.reshape(heads, rows_q, keys)
        score = score.astype(bf16)
        grad_q[at, :] = own_heads(mm(score, key_rows[start:end, :]), heads).astype(bf16)
        for h in range(heads):
            cols = slice(h * head_size, (h + 1) * head_size)
            mine = slice(h * rows_q, (h + 1) * rows_q)
            sum_k[cols, start:end] += mm(query_cols[cols, at], score[mine])
            sum_v[cols, start:end] += mm(gctx_cols[cols, at], prob[mine])
    grad_k[...] = sum_k[...].astype(bf16)
    grad_v[...] = sum_v[...].astype(bf16)
    grad_q.flush()
    grad_k.flush()
    grad_v.flush()
    late[0:columns, :] = mm_tn(grad_q[...], normed[...]).astype(bf16)
    late[columns : 2 * columns, :] = mm(grad_k[...], normed[...]).astype(bf16)
    late[2 * columns : 3 * columns, :] = mm(grad_v[...], normed[...]).astype(bf16)
    chosen = near[...] == lax.broadcasted_iota(jnp.int32, (buckets, table), 0)
    places = lax.broadcasted_iota(jnp.int32, (buckets, 128), 1)
    found = jnp.zeros((buckets, 128), f32)
    for h in range(heads):
        strip = jnp.zeros((8, table), f32)
        for a in range(0, rows_q, 8):
            strip = strip + pltpu.roll(spill[h, a : a + 8, :], (table - a) % table, 1)
        line = lax.broadcasted_iota(jnp.int32, strip.shape, 0)
        for bit in (1, 2, 4):
            strip = jnp.where((line & bit) != 0, pltpu.roll(strip, table - bit, 1), strip)
        strip = jnp.sum(strip, axis=0, keepdims=True)
        per = jnp.sum(jnp.where(chosen, strip, 0.0), axis=1, keepdims=True)
        found = found + jnp.where(places == h, per, 0.0)
    grad_bias[...] = found


def input_grad_body(t_ref, grad_q, grad_k, grad_v, weight, normed, gain, keep, send, sums):
    t = t_ref[0]
    seq, width = normed.shape
    own = seq // 4
    total_gain = jnp.zeros((1, width), f32)
    for k in range(4):
        at = pl.ds(pl.multiple_of((t ^ k) * own, own), own)
        part = mm(grad_q[at, :], weight[0])
        part = part + mm_tn(grad_k[:, at], weight[1])
        part = part + mm_tn(grad_v[:, at], weight[2])
        total_gain = total_gain + jnp.sum(part * normed[at, :].astype(f32), axis=0, keepdims=True)
        out = keep if k in (0, 2) else send
        out[(k // 2) * own : (k // 2 + 1) * own, :] = part.astype(bf16)
    sums[...] = total_gain / gain[...]


def sum_copies(copies, ref):
    full = ref[...].astype(f32)
    rows = full.shape[0] // copies
    total = full[0:rows]
    for i in range(1, copies):
        total = total + full[i * rows : (i + 1) * rows]
    return total


def share_body(copies, early, late, sums, grad_bias, out):
    width = early.shape[1]
    found = grad_bias[...]
    lanes = found.shape[1]
    found = jnp.concatenate([found, jnp.zeros((lanes - found.shape[0], lanes), f32)], axis=0).T
    found = jnp.concatenate([found[0:8], jnp.zeros((8, width - lanes), f32)], axis=1)
    line = lax.broadcasted_iota(jnp.int32, found.shape, 0)
    found = jnp.where(line == 7, sums[...], found)
    total = [found, sum_copies(copies, early), sum_copies(copies, late)]
    out[...] = jnp.concatenate(total, axis=0).astype(bf16)


def finish_body(early_rows, i_ref, *refs):
    shares = refs[:-7]
    qkv, out, bias, gain_attn, gain_moe, router, early = refs[-7:]
    columns = out.shape[0]
    experts = router.shape[0]
    small = None
    for j, ref in enumerate(shares):
        full = ref[...].astype(f32)
        owner = i_ref[0] ^ j
        small = full[0:8] if small is None else small + full[0:8]
        early[owner] = full[8 : 8 + early_rows]
        qkv[owner] = full[8 + early_rows :]
    whole = jnp.concatenate([early[i] for i in range(early.shape[0])], axis=0)
    out[...] = whole[0:columns]
    router[...] = whole[columns : columns + experts]
    gain_moe[...] = whole[columns + experts]
    bias[...] = small[0 : bias.shape[0], 0 : bias.shape[1]]
    gain_attn[...] = small[7]


def last_body(kept, got, far, x_ref, gain, h_own, grad):
    total = kept[...].astype(f32) + got[...].astype(f32) + far[...].astype(f32)
    x = x_ref[...].astype(f32)
    inv = lax.rsqrt(jnp.mean(x * x, axis=1, keepdims=True) + epsilon)
    n1 = x * inv
    a = total * gain[...]
    grad[...] = h_own[...] + inv * (a - n1 * jnp.mean(a * n1, axis=1, keepdims=True))


def output_body(t_ref, f0, f1, f2, f3, code_col, h_own, out, slots):
    t = t_ref[0]
    own = h_own.shape[0]
    quarter = f0.shape[0]
    for j, ref in enumerate((f0, f1, f2, f3)):
        slots[pl.ds(pl.multiple_of((t ^ j) * quarter, quarter), quarter), :] = ref[...]
    codes = code_col[pl.ds(pl.multiple_of(t * own, own), own), :]
    place = lax.broadcasted_iota(jnp.int32, (own, 4 * quarter), 1)
    out[...] = (h_own[...] + mm((place == codes).astype(bf16), slots[...])).astype(bf16)


def turn(value):
    return lax.all_to_all(value, "dp", split_axis=0, concat_axis=0, tiled=True)


def per_device(
    inputs,
    segments,
    buckets,
    routes,
    qkv_weight,
    out_weight,
    rel_bias,
    norm_attn,
    norm_moe,
    router_weight,
    expert_in,
    expert_out,
    cotangent,
):
    own, width = inputs.shape
    seq = 4 * own
    dp = lax.axis_size("dp")
    experts = router_weight.shape[1]
    capacity = max(2, 5 * seq // (4 * experts))
    quarter = (experts // 2) * (capacity // 2)
    heads = rel_bias.shape[1]
    columns = heads * head_size
    t_one = lax.axis_index("tensor").astype(jnp.int32)[None]
    x_side = t_one >> 1
    dp_one = lax.axis_index("dp").astype(jnp.int32)[None]
    first_expert = 2 * dp_one
    near_expert = jnp.concatenate([x_side, first_expert + x_side])
    far_expert = jnp.concatenate([1 - x_side, first_expert + 1 - x_side])
    inputs, t_one, dp_one, near_expert, far_expert = lax.optimization_barrier(
        (inputs, t_one, dp_one, near_expert, far_expert)
    )
    gain_attn = norm_attn[None, :]
    gain_moe = norm_moe[None, :]
    near = lax.slice_in_dim(buckets, seq - 1 - reach, seq - 1 - reach + table, axis=0)[None, :]
    weight = jnp.swapaxes(qkv_weight, 1, 2)
    router = router_weight.T

    code_row, code_col, seg_col, tile = run(
        functools.partial(slots_body, experts, capacity),
        [
            shape((1, seq), jnp.int32),
            shape((seq, 1), jnp.int32),
            shape((seq, 1), jnp.int32),
            shape((heads, rows_q, window), f32),
        ],
        [routes.reshape(1, seq), segments, near, rel_bias.T],
        smem=(3,),
        us=2,
        stores=(3,),
        name="slots",
    )
    xs = gather4(inputs, code_row)
    g_core = core_hop(cotangent)
    x_all, normed, ctx = run(
        attend_body,
        [
            shape((seq, width), bf16),
            shape((seq, width), bf16),
            shape((seq + seq // 2 + columns * width // 128, 128), bf16),
        ],
        [t_one, *xs, gain_attn, weight, segments, seg_col, tile, out_weight],
        smem=(0,),
        scratch=[
            pltpu.VMEM((seq, columns), bf16),
            pltpu.VMEM((columns, seq), bf16),
            pltpu.VMEM((seq, columns + head_size), bf16),
        ],
        us=10,
        loads=(1, 6, 9, 10),
        stores=(0, 1, 2),
        deps=[g_core],
        name="attend",
    )
    g_far_block = after(x_hop(cotangent), ctx)
    gs = (cotangent, g_core, g_far_block, core_hop(g_far_block))
    g_all, g_rows = run(
        spread_body,
        [shape((seq, width), bf16), shape((quarter, width), bf16)],
        [t_one, *gs, code_row],
        smem=(0,),
        us=0.1,
        loads=(1,),
        stores=(0,),
        name="spread",
    )
    query_cols, value_cols, ctx_cols = run(
        columns_body,
        [shape((columns, seq), bf16)] * 3,
        [normed, weight, ctx],
        deps=[g_rows],
        us=0.1,
        loads=(0, 1, 2),
        stores=(0, 1, 2),
        name="columns",
    )
    cs = gather4(ctx, query_cols)
    h_one, h_own, rows = run(
        mid_body,
        [
            shape((seq, width), bf16),
            shape((own, width), f32),
            shape((quarter, width), bf16),
        ],
        [t_one, x_all, *cs, gain_moe, code_row],
        smem=(0,),
        scratch=[pltpu.VMEM((seq, width), bf16), pltpu.VMEM((seq, width), f32)],
        us=0.1,
        loads=(2, 1),
        stores=(0, 1),
        name="mid",
    )
    g_got = turn(g_rows)
    g_far = x_hop(after(g_got, rows))
    probs, key_rows = run(
        probs_body,
        [shape((heads, seq, window), bf16), shape((seq, columns), bf16)],
        [normed, weight, segments, seg_col, tile],
        deps=[rows],
        scratch=[pltpu.VMEM((seq, columns), bf16)],
        us=7,
        loads=(0, 1, 4),
        stores=(0, 1),
        name="probs",
    )
    row_got = after(turn(rows), probs, g_far)
    near_rows = (row_got, core_hop(row_got))
    g_near = after(g_got, probs)
    near_out = expert(
        True, near_expert, *near_rows, g_near, core_hop(g_near), router, expert_in, expert_out
    )
    far_mine = after(x_hop(row_got), near_out[0])
    far_rows = (far_mine, core_hop(far_mine))
    far_out = expert(
        False, far_expert, *far_rows, g_far, core_hop(g_far), router, expert_in, expert_out
    )
    far = far_out[2] + core_hop(far_out[3])
    router_part = near_out[7] + far_out[7]
    router_part = router_part + core_hop(router_part)
    router_far = x_hop(router_part)
    weight_grads = expert_grads(near_expert, *near_rows, *near_out[4:7], deps=[far])
    far, router_far = lax.optimization_barrier((x_hop(far), router_far, weight_grads[0]))[:2]
    router_part = router_part + router_far
    kept = near_out[2] + core_hop(near_out[3]) + far
    home = turn(kept)
    far = after(far_out[0], kept) + core_hop(far_out[1])
    weight_grads = expert_grads(
        far_expert, *far_rows, *far_out[4:7], so_far=weight_grads, deps=[far]
    )
    home = after(home, weight_grads[0])
    fwd = after(near_out[0], home) + core_hop(near_out[1]) + x_hop(far)
    bs = gather4(home, fwd)
    fwd = turn(fwd)
    small = -(-(experts + 1) // 64) * 64
    gh_own, gctx, early = run(
        back_body,
        [
            shape((own, width), f32),
            shape((seq, columns), bf16),
            shape((columns + small, width), bf16),
        ],
        [t_one, *bs, code_col, h_one, gain_moe, g_all, out_weight, ctx_cols, router_part],
        smem=(0,),
        loads=((6, 4, 0), (8, 4, 0), 9, 10),
        stores=(0, 1),
        scratch=[
            pltpu.VMEM((seq, width), bf16),
            pltpu.VMEM((4 * quarter, width), bf16),
            pltpu.VMEM((seq, width), f32),
        ],
        us=2,
        name="back",
    )
    early_got = turn(early)
    grad_q, grad_k, grad_v, late, grad_bias = run(
        attend_back_body,
        [
            shape((seq, columns), bf16),
            shape((columns, seq), bf16),
            shape((columns, seq), bf16),
            shape((3 * columns, width), bf16),
            shape((rel_bias.shape[0], 128), f32),
        ],
        [gctx, value_cols, key_rows, query_cols, probs, normed, near],
        loads=(0, 1, 2, 3, (4, seq // rows_q, 1), 5),
        stores=(0, 1, 2),
        deps=[fwd],
        scratch=[
            pltpu.VMEM((heads, rows_q, table), f32),
            pltpu.VMEM((columns, seq), f32),
            pltpu.VMEM((columns, seq), f32),
        ],
        us=14,
        name="attend_back",
    )
    f_far = x_hop(after(fwd, gctx))
    fs = (fwd, core_hop(fwd), f_far, core_hop(f_far))
    late_got = turn(after(late, f_far))
    keep, send, gain_part = run(
        input_grad_body,
        [
            shape((2 * own, width), bf16),
            shape((2 * own, width), bf16),
            shape((1, width), f32),
        ],
        [t_one, grad_q, grad_k, grad_v, weight, normed, gain_attn],
        smem=(0,),
        us=0.1,
        loads=(1, 2, 3, 4, 5),
        name="input_grad",
    )
    gain_part = gain_part + core_hop(gain_part)
    gain_part = gain_part + x_hop(gain_part)
    keep, send = lax.optimization_barrier((keep, send, gain_part))[:2]
    got = core_hop(send)
    far = x_hop(keep[own:] + got[own:])
    (grad_inputs,) = run(
        last_body,
        [shape((own, width), f32)],
        [keep[:own], got[:own], far, inputs, gain_attn, gh_own],
        loads=(3, 5),
        us=0.1,
        name="last",
    )
    (output,) = run(
        output_body,
        [shape((own, width), bf16)],
        [t_one, *fs, code_col, h_own],
        smem=(0,),
        loads=(6,),
        scratch=[pltpu.VMEM((4 * quarter, width), bf16)],
        us=0.1,
        name="output",
    )
    early_rows = early.shape[0] // dp
    late_rows = late.shape[0] // dp
    (share,) = run(
        functools.partial(share_body, dp),
        [shape((8 + early_rows + late_rows, width), bf16)],
        [early_got, late_got, gain_part, grad_bias],
        deps=[output],
        us=1,
        name="share",
    )
    shares = [share]
    for j in range(2, dp, 2):
        shares.append(lax.ppermute(share, "dp", [(i, i ^ j) for i in range(dp)]))
    shares = [
        one
        for share in shares
        for one in (share, lax.ppermute(share, "dp", [(i, i ^ 1) for i in range(dp)]))
    ]
    qkv_grad, out_grad, bias_grad, gain_attn_grad, gain_moe_grad, router_grad = run(
        functools.partial(finish_body, early_rows),
        [
            shape((dp, late_rows, width), f32),
            shape((columns, width), f32),
            shape((heads, rel_bias.shape[0]), f32),
            shape((width,), f32),
            shape((width,), f32),
            shape((experts, width), f32),
        ],
        [dp_one, *shares],
        smem=(0,),
        scratch=[pltpu.VMEM((dp, early_rows, width), f32)],
        us=2,
        name="finish",
    )
    return (
        output,
        grad_inputs,
        jnp.swapaxes(qkv_grad.reshape(3, columns, width), 1, 2),
        out_grad,
        bias_grad.T,
        gain_attn_grad,
        gain_moe_grad,
        router_grad.T,
        *weight_grads,
    )


def solution(mesh):
    placed = (
        P(("dp", "tensor"), None),
        P("dp", None),
        P(),
        P("dp", None, None),
        P(None, None, "tensor"),
        P("tensor", None),
        P(None, "tensor"),
        P(),
        P(),
        P(),
        P("dp", None, "tensor"),
        P("dp", "tensor", None),
        P(("dp", "tensor"), None),
    )
    return jax.shard_map(
        per_device,
        mesh=mesh,
        in_specs=placed,
        out_specs=(
            P(("dp", "tensor"), None),
            P(("dp", "tensor"), None),
            P(None, None, "tensor"),
            P("tensor", None),
            P(None, "tensor"),
            P(),
            P(),
            P(),
            P("dp", None, "tensor"),
            P("dp", "tensor", None),
        ),
        check_vma=False,
    )
```

```python
import functools

import jax
import jax.numpy as jnp
from jax import lax
from jax.experimental import pallas as pl
from jax.experimental.pallas import tpu as pltpu
from jax.sharding import PartitionSpec as P

epsilon = 1e-06
negative = -1000000000.0
bf16 = jnp.bfloat16
f32 = jnp.float32
reach = 256
rows_q = 128
window = rows_q + 2 * reach
table = window + rows_q
head_size = 64
mega = 1024 * 1024

core_pairs = [(0, 1), (1, 0), (2, 3), (3, 2)]
x_pairs = [(0, 2), (2, 0), (1, 3), (3, 1)]


def core_hop(value):
    return lax.ppermute(value, "tensor", core_pairs)


def x_hop(value):
    return lax.ppermute(value, "tensor", x_pairs)


def after(value, *deps):
    return lax.optimization_barrier((value, *deps))[0]


def gather4(value, *deps):
    other = x_hop(value)
    if deps:
        other = after(other, *deps)
    return value, core_hop(value), other, core_hop(other)


def dot(a, b, dims):
    return lax.dot_general(a, b, (dims, ((), ())), preferred_element_type=f32)


def mm(a, b):
    return dot(a, b, ((1,), (0,)))


def mm_nt(a, b):
    return dot(a, b, ((1,), (1,)))


def mm_tn(a, b):
    return dot(a, b, ((0,), (0,)))


def shape(dims, kind):
    return jax.ShapeDtypeStruct(dims, kind)


class Loaded:
    def __init__(self, source, buffer, sems, axis=0):
        self.buffer, self.axis = buffer, axis
        self.shape, self.dtype = buffer.shape, buffer.dtype
        count = len(sems)
        self.step = self.shape[axis] // count
        self.copies = []
        for i, sem in enumerate(sems):
            at = self.place(i) if count > 1 else ()
            part = (source.at[at], buffer.at[at]) if at else (source, buffer)
            self.copies.append(pltpu.make_async_copy(*part, sem))
            self.copies[-1].start()
        self.here = [False] * count

    def place(self, i):
        return (slice(None),) * self.axis + (pl.ds(i * self.step, self.step),)

    def piece(self, i):
        if not self.here[i]:
            self.copies[i].wait()
            self.here[i] = True

    def wait(self):
        for i in range(len(self.copies)):
            self.piece(i)

    def __getitem__(self, place):
        self.wait()
        return self.buffer[place]


class Stored:
    def __init__(self, target, buffer, sem):
        self.buffer, self.target, self.sem = buffer, target, sem
        self.shape, self.dtype = buffer.shape, buffer.dtype
        self.gone = 0

    def flush(self, first=0, rows=None):
        rows = self.shape[0] if rows is None else rows
        at = pl.ds(first, rows)
        pltpu.make_async_copy(self.buffer.at[at], self.target.at[at], self.sem).start()
        self.gone += rows

    def close(self):
        if not self.gone:
            self.flush()

    def wait(self):
        pltpu.make_async_copy(self.buffer, self.target, self.sem).wait()

    def __getitem__(self, place):
        return self.buffer[place]

    def __setitem__(self, place, value):
        self.buffer[place] = value


def run(
    body, outs, args, smem=(), loads=(), stores=(), hbm=(), hbm_outs=(), deps=(), aliases=None,
    scratch=(), us=2, name=None,
):
    args = list(args)
    if deps:
        args[0] = after(args[0], *deps)
    n_in, n_out, n_own = len(args), len(outs), len(scratch)
    cuts = [one if isinstance(one, tuple) else (one, 1, 0) for one in loads]
    loads = [one[0] for one in cuts]
    n_sems = sum(one[1] for one in cuts) + len(stores)

    def inner(*refs):
        ins = list(refs[:n_in])
        results = list(refs[n_in : n_in + n_out])
        own = refs[n_in + n_out : n_in + n_out + n_own]
        rest = refs[n_in + n_out + n_own :]
        buffers, sems = rest[:-1], rest[-1]
        used = 0
        for n, (i, pieces, axis) in enumerate(cuts):
            mine = [sems.at[used + j] for j in range(pieces)]
            ins[i] = Loaded(ins[i], buffers[n], mine, axis)
            used += pieces
        for n, i in enumerate(stores):
            results[i] = Stored(results[i], buffers[len(loads) + n], sems.at[used + n])
        body(*ins, *results, *own)
        for i in loads:
            ins[i].wait()
        for i in stores:
            results[i].close()
        for i in stores:
            results[i].wait()

    def space(i):
        if i in smem:
            return pltpu.SMEM
        return pltpu.HBM if i in hbm or i in loads else pltpu.VMEM

    for i in (*loads, *hbm):
        if i < n_in:
            args[i] = pltpu.with_memory_space_constraint(args[i], pltpu.HBM)
    kinds = [
        pltpu.HBM(o.shape, o.dtype) if i in hbm_outs or i in stores else o
        for i, o in enumerate(outs)
    ]
    staged = [pltpu.VMEM(args[i].shape, args[i].dtype) for i in loads]
    staged += [pltpu.VMEM(outs[i].shape, outs[i].dtype) for i in stores]
    return pl.pallas_call(
        inner,
        out_shape=kinds,
        in_specs=[pl.BlockSpec(memory_space=space(i)) for i in range(n_in)],
        out_specs=[
            pl.BlockSpec(
                memory_space=pltpu.HBM if i in hbm_outs or i in stores else pltpu.VMEM
            )
            for i in range(n_out)
        ],
        scratch_shapes=[
            *scratch, *staged, pltpu.SemaphoreType.DMA((max(1, n_sems),))
        ],
        input_output_aliases=aliases or {},
        compiler_params=pltpu.CompilerParams(vmem_limit_bytes=44 * mega),
        cost_estimate=pl.CostEstimate(
            flops=int(us * 1.1e9), bytes_accessed=mega // 4, transcendentals=0
        ),
        name=name,
    )(*args)


def as_column(row):
    wide = jnp.broadcast_to(row.astype(f32), (8, row.shape[1]))
    return wide.T[:, 0:1].astype(jnp.int32)


def slots_body(
    experts, capacity, row_ref, seg_row, near, bias, code_row, code_col, seg_col, tile
):
    seq = row_ref.shape[1]
    half = capacity // 2
    quarter = (experts // 2) * half
    first = lax.broadcasted_iota(jnp.int32, (seq, seq), 0)
    second = lax.broadcasted_iota(jnp.int32, (seq, seq), 1)
    route = row_ref[...]
    chosen = route == lax.broadcasted_iota(jnp.int32, (experts, seq), 0)
    count = mm(chosen.astype(bf16), (first < second).astype(bf16))
    slot = jnp.sum(jnp.where(chosen, count, 0.0), axis=0, keepdims=True).astype(jnp.int32)
    upper = jnp.where(slot >= half, 1, 0)
    code = (2 * (route & 1) + upper) * quarter + (route >> 1) * half + slot - half * upper
    code_row[...] = code
    code_col[...] = as_column(code)
    seg_col[...] = as_column(seg_row[...])
    bucket = near[...]
    for h in range(bias.shape[0]):
        line = jnp.zeros(bucket.shape, f32)
        for b in range(bias.shape[1]):
            line = jnp.where(bucket == b, bias[h, b], line)
        wide = jnp.broadcast_to(line, (rows_q, table))
        tile[h] = pltpu.roll(wide, 0, 1, stride=1, stride_axis=0)[:, :window]


def span(i0, seq):
    start = max(0, i0 - reach)
    end = min(seq, i0 + rows_q + reach)
    return start, end, start - (i0 - reach)


def masked_probs(score, same, tile):
    score = jnp.where(same, score + tile, negative)
    score = jnp.exp(score - jnp.max(score, axis=1, keepdims=True))
    return (score * (1.0 / jnp.sum(score, axis=1, keepdims=True))).astype(bf16)


def stack_heads(block, heads):
    lane = lax.broadcasted_iota(jnp.int32, block.shape, 1) // head_size
    return jnp.concatenate(
        [jnp.where(lane == h, block, jnp.zeros_like(block)) for h in range(heads)], axis=0
    )


def own_heads(stacked, heads):
    rows = stacked.shape[0] // heads
    lane = lax.broadcasted_iota(jnp.int32, (rows, stacked.shape[1]), 1) // head_size
    out = stacked[(heads - 1) * rows :]
    for h in range(heads - 1):
        out = jnp.where(lane == h, stacked[h * rows : (h + 1) * rows], out)
    return out


def masked_exp(score, same, tile):
    heads, rows, keys = tile.shape
    score = score.reshape(heads, rows, keys) + tile
    score = jnp.where(same[None], score, negative)
    return jnp.exp(score - jnp.max(score, axis=2, keepdims=True))


def attend_body(
    t_ref, x0, x1, x2, x3, gain, weight, seg_row, seg_col, tile, out_weight,
    x_all, normed, ctx, query, key, value,
):
    t = t_ref[0]
    own = x0.shape[0]
    seq = 4 * own
    heads = tile.shape[0]
    columns = heads * head_size
    for k, ref in ((1, x1), (2, x2), (3, x3), (0, x0)):
        at = pl.ds(pl.multiple_of((t ^ k) * own, own), own)
        x = ref[...]
        x_all[at, :] = x
        x = x.astype(f32)
        inv = lax.rsqrt(jnp.mean(x * x, axis=1, keepdims=True) + epsilon)
        normed[at, :] = (x * inv * gain[...]).astype(bf16)
    x_all.flush()
    normed.flush()
    query[...] = mm_nt(normed[...], weight[0]).astype(bf16)
    key[...] = mm_nt(weight[1], normed[...]).astype(bf16)
    value[:, 0:columns] = mm_nt(normed[...], weight[2]).astype(bf16)
    value[:, columns:] = jnp.ones((seq, head_size), bf16)
    for i0 in range(0, seq, rows_q):
        start, end, off = span(i0, seq)
        same = seg_col[i0 : i0 + rows_q, :] == seg_row[:, start:end]
        score = mm(stack_heads(query[i0 : i0 + rows_q, :], heads), key[:, start:end])
        weights = masked_exp(score, same, tile[:, :, off : off + end - start]).astype(bf16)
        out = mm(weights.reshape(heads * rows_q, end - start), value[start:end, :])
        out = out[:, 0:columns] * (1.0 / out[:, columns : columns + 1])
        out = own_heads(out, heads).astype(bf16)
        ctx[i0 : i0 + rows_q, :] = out[:, 0 : 2 * head_size]
        lane = 0 if i0 < seq // 2 else head_size
        at = seq + i0 % (seq // 2)
        ctx[at : at + rows_q, lane : lane + head_size] = out[:, 2 * head_size :]
    first = seq + seq // 2
    for j in range(out_weight.shape[1] // 128):
        ctx[first + j * columns : first + (j + 1) * columns, :] = out_weight[
            :, j * 128 : (j + 1) * 128
        ]


def probs_body(normed, weight, seg_row, seg_col, tile, probs, key_rows, query):
    seq = normed.shape[0]
    heads = tile.shape[0]
    query[...] = mm_nt(normed[...], weight[0]).astype(bf16)
    key_rows[...] = mm_nt(normed[...], weight[1]).astype(bf16)
    for i0 in range(0, seq, rows_q):
        start, end, off = span(i0, seq)
        same = seg_col[i0 : i0 + rows_q, :] == seg_row[:, start:end]
        score = mm_nt(stack_heads(query[i0 : i0 + rows_q, :], heads), key_rows[start:end, :])
        weights = masked_exp(score, same, tile[:, :, off : off + end - start])
        inv = 1.0 / jnp.sum(weights, axis=2, keepdims=True)
        probs[:, i0 : i0 + rows_q, 0 : end - start] = (weights * inv).astype(bf16)


def columns_body(normed, weight, ctx, query_cols, value_cols, ctx_cols):
    seq = normed.shape[0]
    columns = weight.shape[1]
    query_cols[...] = mm_nt(weight[0], normed[...]).astype(bf16)
    value_cols[...] = mm_nt(weight[2], normed[...]).astype(bf16)
    pair = 2 * head_size
    ctx_cols[0:pair, :] = ctx[0:seq, :].T
    last = ctx[seq : seq + seq // 2, :].T
    ctx_cols[pair:columns, 0 : seq // 2] = last[0:head_size, :]
    ctx_cols[pair:columns, seq // 2 :] = last[head_size:, :]


def third(ctx, r0, rows, seq):
    lane = 0 if r0 < seq // 2 else head_size
    at = seq + r0 % (seq // 2)
    return ctx[at : at + rows, lane : lane + head_size]


def mid_body(
    t_ref, x_all, c0, c1, c2, c3, gain, code_row,
    h_one, h_own, rows, normed, sums,
):
    t = t_ref[0]
    seq, width = x_all.shape
    own = seq // 4
    quarter = rows.shape[0]
    ctxs = (c0, c1, c2, c3)
    columns = 3 * head_size
    first = seq + seq // 2
    weights = [
        jnp.concatenate(
            [c[first + j * columns : first + (j + 1) * columns, :] for j in range(width // 128)],
            axis=1,
        )
        for c in ctxs
    ]
    pair = 2 * head_size
    packed = [
        jnp.concatenate([weights[2 * i][0:pair, :], weights[2 * i + 1][0:pair, :]], axis=0)
        for i in range(2)
    ]
    last = jnp.concatenate([w[pair : pair + head_size, :] for w in weights], axis=0)
    for r0 in range(0, seq, own):
        at = slice(r0, r0 + own)
        left = jnp.concatenate([ctxs[2][at, :], ctxs[3][at, :]], axis=1)
        total = mm(left, packed[1])
        left = jnp.concatenate([ctxs[0][at, :], ctxs[1][at, :]], axis=1)
        total = total + mm(left, packed[0])
        left = jnp.concatenate([third(c, r0, own, seq) for c in ctxs], axis=1)
        total = total + mm(left, last)
        total = total + x_all[at, :].astype(f32)
        h_one[at, :] = total.astype(bf16)
        h_one.flush(r0, own)
        sums[at, :] = total
        inv = lax.rsqrt(jnp.mean(total * total, axis=1, keepdims=True) + epsilon)
        normed[at, :] = (total * inv * gain[...]).astype(bf16)
    h_own[...] = sums[pl.ds(pl.multiple_of(t * own, own), own), :]
    h_own.flush()
    place = lax.broadcasted_iota(jnp.int32, (quarter, seq), 0) + t * quarter
    rows[...] = mm((place == code_row[...]).astype(bf16), normed[...]).astype(bf16)


def spread_body(t_ref, g0, g1, g2, g3, code_row, g_all, rows):
    t = t_ref[0]
    own = g0.shape[0]
    quarter = rows.shape[0]
    for k, ref in ((1, g1), (2, g2), (3, g3), (0, g0)):
        g_all[pl.ds(pl.multiple_of((t ^ k) * own, own), own), :] = ref[...]
    g_all.flush()
    place = lax.broadcasted_iota(jnp.int32, (quarter, g_all.shape[0]), 0) + t * quarter
    rows[...] = mm((place == code_row[...]).astype(bf16), g_all[...]).astype(bf16)


gelu_scale = 0.7978845608028654
gelu_cubic = 0.044715


def expert_body(
    near, e_ref, r0, r1, g0, g1, router, w_in_all, w_out_all,
    back0, back1, grad0, grad1, hidden_out, gated_out, pre_out, router_out,
    w_in, w_out, rows_all, g_rows, backs, grads, sem, out_sem,
):
    half = r0.shape[0]
    if near:
        load_in = pltpu.make_async_copy(w_in_all.at[e_ref[0]], w_in, sem.at[0])
        load_out = pltpu.make_async_copy(w_out_all.at[e_ref[0]], w_out, sem.at[1])
        load_in.start()
        load_out.start()
    else:
        w_in = w_in_all.at[e_ref[0]]
        w_out = w_out_all.at[e_ref[0]]
    rows_all[0] = r0[...]
    rows_all[1] = r1[...]
    g_rows[0] = g0[...]
    g_rows[1] = g1[...]
    router_out[...] = jnp.zeros(router_out.shape, f32)
    if near:
        load_in.wait()
        load_out.wait()
    sends = [
        [
            pltpu.make_async_copy(backs.at[i], back, out_sem.at[2 * i]),
            pltpu.make_async_copy(grads.at[i], grad, out_sem.at[2 * i + 1]),
        ]
        for i, (back, grad) in enumerate(((back0, grad0), (back1, grad1)))
    ]

    def one_half(i, carry):
        first = pl.multiple_of(i * half, half)
        at = pl.ds(first, half)
        rows = rows_all[i]
        cot = g_rows[i].astype(f32)
        logits = mm_nt(rows, router[...])
        logits = jnp.exp(logits - jnp.max(logits, axis=1, keepdims=True))
        prob = logits / jnp.sum(logits, axis=1, keepdims=True)
        mine = lax.broadcasted_iota(jnp.int32, prob.shape, 1) == e_ref[1]
        gate = jnp.sum(jnp.where(mine, prob, 0.0), axis=1, keepdims=True)
        gated = (gate * cot).astype(bf16)
        gated_out[at, :] = gated
        pre = mm(rows, w_in[...])
        square = pre * pre
        inner = jnp.tanh(gelu_scale * pre * (1.0 + gelu_cubic * square))
        half_up = 0.5 + 0.5 * inner
        hidden = (pre * half_up).astype(bf16)
        hidden_out[at, :] = hidden
        slope = half_up + (0.5 * gelu_scale) * pre * (1.0 - inner * inner) * (
            1.0 + (3.0 * gelu_cubic) * square
        )
        part = mm(hidden, w_out[...])
        backs[i] = (gate * part).astype(bf16)
        grad_gate = jnp.sum(cot * part, axis=1, keepdims=True)
        grad_pre = (mm_nt(gated, w_out[...]) * slope).astype(bf16)
        pre_out[at, :] = grad_pre
        grad_logits = (gate * grad_gate * (jnp.where(mine, 1.0, 0.0) - prob)).astype(bf16)
        grads[i] = (mm_nt(grad_pre, w_in[...]) + mm(grad_logits, router[...])).astype(bf16)
        for n in range(2):

            @pl.when(i == n)
            def _(n=n):
                sends[n][0].start()
                sends[n][1].start()

        router_out[...] += mm_tn(grad_logits, rows)
        return carry

    lax.fori_loop(0, 2, one_half, 0)
    hidden_out.flush()
    gated_out.flush()
    pre_out.flush()
    for pair in sends:
        for one in pair:
            one.wait()


def expert(near, scalars, r0, r1, g0, g1, router, w_in, w_out):
    half, width = r0.shape
    hidden = w_in.shape[2]
    rows = 2 * half
    return run(
        functools.partial(expert_body, near),
        [shape((half, width), bf16)] * 4
        + [
            shape((rows, hidden), bf16),
            shape((rows, width), bf16),
            shape((rows, hidden), bf16),
            shape(router.shape, f32),
        ],
        [scalars, r0, r1, g0, g1, router, w_in, w_out],
        smem=(0,),
        hbm=(6, 7) if near else (),
        hbm_outs=(0, 1, 2, 3),
        stores=(4, 5, 6),
        scratch=[
            pltpu.VMEM((width, hidden), bf16),
            pltpu.VMEM((hidden, width), bf16),
            pltpu.VMEM((2, half, width), bf16),
            pltpu.VMEM((2, half, width), bf16),
            pltpu.VMEM((2, half, width), bf16),
            pltpu.VMEM((2, half, width), bf16),
            pltpu.SemaphoreType.DMA((2,)),
            pltpu.SemaphoreType.DMA((4,)),
        ],
        us=7,
        name="expert",
    )


def expert_grad_body(first, e_ref, r0, r1, hidden, gated, pre, *refs):
    d_in, d_out, sum_in, sum_out, sem = refs[-5:]
    rows = jnp.concatenate([r0[...], r1[...]], axis=0)
    sum_in[...] = mm_tn(rows, pre[...])
    store_in = pltpu.make_async_copy(sum_in, d_in.at[e_ref[0]], sem.at[0])
    store_in.start()
    sum_out[...] = mm_tn(hidden[...], gated[...])
    store_out = pltpu.make_async_copy(sum_out, d_out.at[e_ref[0]], sem.at[1])
    store_out.start()
    store_in.wait()
    store_out.wait()


def expert_grads(scalars, r0, r1, hidden, gated, pre, so_far=(), deps=()):
    columns, width = hidden.shape[1], gated.shape[1]
    return run(
        functools.partial(expert_grad_body, not so_far),
        [shape((2, width, columns), f32), shape((2, columns, width), f32)],
        [scalars, r0, r1, hidden, gated, pre, *so_far],
        smem=(0,),
        loads=(3, 4, 5),
        hbm=(6, 7),
        hbm_outs=(0, 1),
        aliases={6: 0, 7: 1} if so_far else None,
        deps=deps,
        scratch=[
            pltpu.VMEM((width, columns), f32),
            pltpu.VMEM((columns, width), f32),
            pltpu.SemaphoreType.DMA((2,)),
        ],
        us=4,
        name="expert_grads",
    )


def back_body(
    t_ref, b0, b1, b2, b3, code_col, h_one, gain, g_all, weight, ctx_cols, router,
    h_own, gctx, early, grad_h, slots, sums,
):
    t = t_ref[0]
    seq, width = h_one.shape
    own = seq // 4
    quarter = b0.shape[0]
    columns = gctx.shape[1]
    for j, ref in enumerate((b0, b1, b2, b3)):
        slots[pl.ds(pl.multiple_of((t ^ j) * quarter, quarter), quarter), :] = ref[...]
    sum_gain = jnp.zeros((1, width), f32)
    step = 2 * own
    place = lax.broadcasted_iota(jnp.int32, (step, 4 * quarter), 1)
    for n, r0 in enumerate(range(0, seq, step)):
        at = slice(r0, r0 + step)
        total = mm((place == code_col[at, :]).astype(bf16), slots[...])
        for half in (2 * n, 2 * n + 1):
            h_one.piece(half)
            g_all.piece(half)
        h = h_one.buffer[at, :].astype(f32)
        inv = lax.rsqrt(jnp.mean(h * h, axis=1, keepdims=True) + epsilon)
        n2 = h * inv
        sum_gain = sum_gain + jnp.sum(total * n2, axis=0, keepdims=True)
        a = total * gain[...]
        mean = jnp.mean(a * n2, axis=1, keepdims=True)
        full = g_all.buffer[at, :].astype(f32) + inv * (a - n2 * mean)
        grad_h[at, :] = full.astype(bf16)
        sums[at, :] = full
    h_own[...] = sums[pl.ds(pl.multiple_of(t * own, own), own), :]
    h_own.flush()
    gctx[...] = mm_nt(grad_h[...], weight[...]).astype(bf16)
    gctx.flush()
    early[0:columns, :] = mm(ctx_cols[...], grad_h[...]).astype(bf16)
    rest = jnp.concatenate([router[...], sum_gain], axis=0)
    spare = early.shape[0] - columns - rest.shape[0]
    rest = jnp.concatenate([rest, jnp.zeros((spare, width), f32)], axis=0)
    early[columns:, :] = rest.astype(bf16)


def attend_back_body(
    gctx, value_cols, key_rows, query_cols, probs, normed, near,
    grad_q, grad_k, grad_v, late, grad_bias, spill, sum_k, sum_v,
):
    seq, columns = gctx.shape
    heads = columns // head_size
    buckets = grad_bias.shape[0]
    spill[...] = jnp.zeros(spill.shape, f32)
    sum_k[...] = jnp.zeros(sum_k.shape, f32)
    sum_v[...] = jnp.zeros(sum_v.shape, f32)
    gctx_cols = gctx[...].T
    for n, i0 in enumerate(range(0, seq, rows_q)):
        start, end, off = span(i0, seq)
        keys = end - start
        at = slice(i0, i0 + rows_q)
        grad = mm(stack_heads(gctx[at, :], heads), value_cols[:, start:end])
        probs.piece(n)
        prob = probs.buffer[:, at, 0:keys].reshape(heads * rows_q, keys)
        wide = prob.astype(f32)
        both = wide * grad
        score = both - wide * jnp.sum(both, axis=1, keepdims=True)
        spill[:, :, off : off + keys] += score.reshape(heads, rows_q, keys)
        score = score.astype(bf16)
        grad_q[at, :] = own_heads(mm(score, key_rows[start:end, :]), heads).astype(bf16)
        for h in range(heads):
            cols = slice(h * head_size, (h + 1) * head_size)
            mine = slice(h * rows_q, (h + 1) * rows_q)
            sum_k[cols, start:end] += mm(query_cols[cols, at], score[mine])
            sum_v[cols, start:end] += mm(gctx_cols[cols, at], prob[mine])
    grad_k[...] = sum_k[...].astype(bf16)
    grad_v[...] = sum_v[...].astype(bf16)
    grad_q.flush()
    grad_k.flush()
    grad_v.flush()
    late[0:columns, :] = mm_tn(grad_q[...], normed[...]).astype(bf16)
    late[columns : 2 * columns, :] = mm(grad_k[...], normed[...]).astype(bf16)
    late[2 * columns : 3 * columns, :] = mm(grad_v[...], normed[...]).astype(bf16)
    chosen = near[...] == lax.broadcasted_iota(jnp.int32, (buckets, table), 0)
    places = lax.broadcasted_iota(jnp.int32, (buckets, 128), 1)
    found = jnp.zeros((buckets, 128), f32)
    for h in range(heads):
        strip = jnp.zeros((8, table), f32)
        for a in range(0, rows_q, 8):
            strip = strip + pltpu.roll(spill[h, a : a + 8, :], (table - a) % table, 1)
        line = lax.broadcasted_iota(jnp.int32, strip.shape, 0)
        for bit in (1, 2, 4):
            strip = jnp.where((line & bit) != 0, pltpu.roll(strip, table - bit, 1), strip)
        strip = jnp.sum(strip, axis=0, keepdims=True)
        per = jnp.sum(jnp.where(chosen, strip, 0.0), axis=1, keepdims=True)
        found = found + jnp.where(places == h, per, 0.0)
    grad_bias[...] = found


def input_grad_body(t_ref, grad_q, grad_k, grad_v, weight, normed, gain, keep, send, sums):
    t = t_ref[0]
    seq, width = normed.shape
    own = seq // 4
    total_gain = jnp.zeros((1, width), f32)
    for k in range(4):
        at = pl.ds(pl.multiple_of((t ^ k) * own, own), own)
        part = mm(grad_q[at, :], weight[0])
        part = part + mm_tn(grad_k[:, at], weight[1])
        part = part + mm_tn(grad_v[:, at], weight[2])
        total_gain = total_gain + jnp.sum(part * normed[at, :].astype(f32), axis=0, keepdims=True)
        out = keep if k in (0, 2) else send
        out[(k // 2) * own : (k // 2 + 1) * own, :] = part.astype(bf16)
    sums[...] = total_gain / gain[...]


def sum_copies(copies, ref):
    full = ref[...].astype(f32)
    rows = full.shape[0] // copies
    total = full[0:rows]
    for i in range(1, copies):
        total = total + full[i * rows : (i + 1) * rows]
    return total


def share_body(copies, early, late, sums, grad_bias, out):
    width = early.shape[1]
    found = grad_bias[...]
    lanes = found.shape[1]
    found = jnp.concatenate([found, jnp.zeros((lanes - found.shape[0], lanes), f32)], axis=0).T
    found = jnp.concatenate([found[0:8], jnp.zeros((8, width - lanes), f32)], axis=1)
    line = lax.broadcasted_iota(jnp.int32, found.shape, 0)
    found = jnp.where(line == 7, sums[...], found)
    total = [found, sum_copies(copies, early), sum_copies(copies, late)]
    out[...] = jnp.concatenate(total, axis=0).astype(bf16)


def finish_body(early_rows, i_ref, *refs):
    shares = refs[:-7]
    qkv, out, bias, gain_attn, gain_moe, router, early = refs[-7:]
    columns = out.shape[0]
    experts = router.shape[0]
    small = None
    for j, ref in enumerate(shares):
        full = ref[...].astype(f32)
        owner = i_ref[0] ^ j
        small = full[0:8] if small is None else small + full[0:8]
        early[owner] = full[8 : 8 + early_rows]
        qkv[owner] = full[8 + early_rows :]
    whole = jnp.concatenate([early[i] for i in range(early.shape[0])], axis=0)
    out[...] = whole[0:columns]
    router[...] = whole[columns : columns + experts]
    gain_moe[...] = whole[columns + experts]
    bias[...] = small[0 : bias.shape[0], 0 : bias.shape[1]]
    gain_attn[...] = small[7]


def last_body(kept, got, far, x_ref, gain, h_own, grad):
    total = kept[...].astype(f32) + got[...].astype(f32) + far[...].astype(f32)
    x = x_ref[...].astype(f32)
    inv = lax.rsqrt(jnp.mean(x * x, axis=1, keepdims=True) + epsilon)
    n1 = x * inv
    a = total * gain[...]
    grad[...] = h_own[...] + inv * (a - n1 * jnp.mean(a * n1, axis=1, keepdims=True))


def output_body(t_ref, f0, f1, f2, f3, code_col, h_own, out, slots):
    t = t_ref[0]
    own = h_own.shape[0]
    quarter = f0.shape[0]
    for j, ref in enumerate((f0, f1, f2, f3)):
        slots[pl.ds(pl.multiple_of((t ^ j) * quarter, quarter), quarter), :] = ref[...]
    codes = code_col[pl.ds(pl.multiple_of(t * own, own), own), :]
    place = lax.broadcasted_iota(jnp.int32, (own, 4 * quarter), 1)
    out[...] = (h_own[...] + mm((place == codes).astype(bf16), slots[...])).astype(bf16)


def turn(value):
    return lax.all_to_all(value, "dp", split_axis=0, concat_axis=0, tiled=True)


def per_device(
    inputs,
    segments,
    buckets,
    routes,
    qkv_weight,
    out_weight,
    rel_bias,
    norm_attn,
    norm_moe,
    router_weight,
    expert_in,
    expert_out,
    cotangent,
):
    own, width = inputs.shape
    seq = 4 * own
    dp = lax.axis_size("dp")
    experts = router_weight.shape[1]
    capacity = max(2, 5 * seq // (4 * experts))
    quarter = (experts // 2) * (capacity // 2)
    heads = rel_bias.shape[1]
    columns = heads * head_size
    t_one = lax.axis_index("tensor").astype(jnp.int32)[None]
    x_side = t_one >> 1
    dp_one = lax.axis_index("dp").astype(jnp.int32)[None]
    first_expert = 2 * dp_one
    near_expert = jnp.concatenate([x_side, first_expert + x_side])
    far_expert = jnp.concatenate([1 - x_side, first_expert + 1 - x_side])
    inputs, t_one, dp_one, near_expert, far_expert = lax.optimization_barrier(
        (inputs, t_one, dp_one, near_expert, far_expert)
    )
    gain_attn = norm_attn[None, :]
    gain_moe = norm_moe[None, :]
    near = lax.slice_in_dim(buckets, seq - 1 - reach, seq - 1 - reach + table, axis=0)[None, :]
    weight = jnp.swapaxes(qkv_weight, 1, 2)
    router = router_weight.T

    code_row, code_col, seg_col, tile = run(
        functools.partial(slots_body, experts, capacity),
        [
            shape((1, seq), jnp.int32),
            shape((seq, 1), jnp.int32),
            shape((seq, 1), jnp.int32),
            shape((heads, rows_q, window), f32),
        ],
        [routes.reshape(1, seq), segments, near, rel_bias.T],
        smem=(3,),
        us=2,
        stores=(3,),
        name="slots",
    )
    xs = gather4(inputs, code_row)
    g_core = core_hop(cotangent)
    x_all, normed, ctx = run(
        attend_body,
        [
            shape((seq, width), bf16),
            shape((seq, width), bf16),
            shape((seq + seq // 2 + columns * width // 128, 128), bf16),
        ],
        [t_one, *xs, gain_attn, weight, segments, seg_col, tile, out_weight],
        smem=(0,),
        scratch=[
            pltpu.VMEM((seq, columns), bf16),
            pltpu.VMEM((columns, seq), bf16),
            pltpu.VMEM((seq, columns + head_size), bf16),
        ],
        us=10,
        loads=(1, 6, 9, 10),
        stores=(0, 1, 2),
        deps=[g_core],
        name="attend",
    )
    g_far_block = after(x_hop(cotangent), ctx)
    gs = (cotangent, g_core, g_far_block, core_hop(g_far_block))
    g_all, g_rows = run(
        spread_body,
        [shape((seq, width), bf16), shape((quarter, width), bf16)],
        [t_one, *gs, code_row],
        smem=(0,),
        us=0.1,
        loads=(1,),
        stores=(0,),
        name="spread",
    )
    query_cols, value_cols, ctx_cols = run(
        columns_body,
        [shape((columns, seq), bf16)] * 3,
        [normed, weight, ctx],
        deps=[g_rows],
        us=0.1,
        loads=(0, 1, 2),
        stores=(0, 1, 2),
        name="columns",
    )
    cs = gather4(ctx, query_cols)
    h_one, h_own, rows = run(
        mid_body,
        [
            shape((seq, width), bf16),
            shape((own, width), f32),
            shape((quarter, width), bf16),
        ],
        [t_one, x_all, *cs, gain_moe, code_row],
        smem=(0,),
        scratch=[pltpu.VMEM((seq, width), bf16), pltpu.VMEM((seq, width), f32)],
        us=0.1,
        loads=(2, 1),
        stores=(0, 1),
        name="mid",
    )
    g_got = turn(g_rows)
    g_far = x_hop(after(g_got, rows))
    probs, key_rows = run(
        probs_body,
        [shape((heads, seq, window), bf16), shape((seq, columns), bf16)],
        [normed, weight, segments, seg_col, tile],
        deps=[rows],
        scratch=[pltpu.VMEM((seq, columns), bf16)],
        us=7,
        loads=(0, 1, 4),
        stores=(0, 1),
        name="probs",
    )
    row_got = after(turn(rows), probs, g_far)
    near_rows = (row_got, core_hop(row_got))
    g_near = after(g_got, probs)
    near_out = expert(
        True, near_expert, *near_rows, g_near, core_hop(g_near), router, expert_in, expert_out
    )
    far_mine = after(x_hop(row_got), near_out[0])
    far_rows = (far_mine, core_hop(far_mine))
    far_out = expert(
        False, far_expert, *far_rows, g_far, core_hop(g_far), router, expert_in, expert_out
    )
    far = far_out[2] + core_hop(far_out[3])
    router_part = near_out[7] + far_out[7]
    router_part = router_part + core_hop(router_part)
    router_far = x_hop(router_part)
    weight_grads = expert_grads(near_expert, *near_rows, *near_out[4:7], deps=[far])
    far, router_far = lax.optimization_barrier((x_hop(far), router_far, weight_grads[0]))[:2]
    router_part = router_part + router_far
    kept = near_out[2] + core_hop(near_out[3]) + far
    home = turn(kept)
    far = after(far_out[0], kept) + core_hop(far_out[1])
    weight_grads = expert_grads(
        far_expert, *far_rows, *far_out[4:7], so_far=weight_grads, deps=[far]
    )
    home = after(home, weight_grads[0])
    fwd = after(near_out[0], home) + core_hop(near_out[1]) + x_hop(far)
    bs = gather4(home, fwd)
    fwd = turn(fwd)
    small = -(-(experts + 1) // 64) * 64
    gh_own, gctx, early = run(
        back_body,
        [
            shape((own, width), f32),
            shape((seq, columns), bf16),
            shape((columns + small, width), bf16),
        ],
        [t_one, *bs, code_col, h_one, gain_moe, g_all, out_weight, ctx_cols, router_part],
        smem=(0,),
        loads=((6, 4, 0), (8, 4, 0), 9, 10),
        stores=(0, 1),
        scratch=[
            pltpu.VMEM((seq, width), bf16),
            pltpu.VMEM((4 * quarter, width), bf16),
            pltpu.VMEM((seq, width), f32),
        ],
        us=2,
        name="back",
    )
    early_got = turn(early)
    grad_q, grad_k, grad_v, late, grad_bias = run(
        attend_back_body,
        [
            shape((seq, columns), bf16),
            shape((columns, seq), bf16),
            shape((columns, seq), bf16),
            shape((3 * columns, width), bf16),
            shape((rel_bias.shape[0], 128), f32),
        ],
        [gctx, value_cols, key_rows, query_cols, probs, normed, near],
        loads=(0, 1, 2, 3, (4, seq // rows_q, 1), 5),
        stores=(0, 1, 2),
        deps=[fwd],
        scratch=[
            pltpu.VMEM((heads, rows_q, table), f32),
            pltpu.VMEM((columns, seq), f32),
            pltpu.VMEM((columns, seq), f32),
        ],
        us=14,
        name="attend_back",
    )
    f_far = x_hop(after(fwd, gctx))
    fs = (fwd, core_hop(fwd), f_far, core_hop(f_far))
    late_got = turn(after(late, f_far))
    keep, send, gain_part = run(
        input_grad_body,
        [
            shape((2 * own, width), bf16),
            shape((2 * own, width), bf16),
            shape((1, width), f32),
        ],
        [t_one, grad_q, grad_k, grad_v, weight, normed, gain_attn],
        smem=(0,),
        us=0.1,
        loads=(1, 2, 3, 4, 5),
        name="input_grad",
    )
    gain_part = gain_part + core_hop(gain_part)
    gain_part = gain_part + x_hop(gain_part)
    keep, send = lax.optimization_barrier((keep, send, gain_part))[:2]
    got = core_hop(send)
    far = x_hop(keep[own:] + got[own:])
    (grad_inputs,) = run(
        last_body,
        [shape((own, width), f32)],
        [keep[:own], got[:own], far, inputs, gain_attn, gh_own],
        loads=(3, 5),
        us=16,
        name="last",
    )
    (output,) = run(
        output_body,
        [shape((own, width), bf16)],
        [t_one, *fs, code_col, h_own],
        smem=(0,),
        loads=(6,),
        scratch=[pltpu.VMEM((4 * quarter, width), bf16)],
        us=1,
        name="output",
    )
    early_rows = early.shape[0] // dp
    late_rows = late.shape[0] // dp
    (share,) = run(
        functools.partial(share_body, dp),
        [shape((8 + early_rows + late_rows, width), bf16)],
        [early_got, late_got, gain_part, grad_bias],
        deps=[output],
        us=1,
        name="share",
    )
    shares = [share]
    for j in range(2, dp, 2):
        shares.append(lax.ppermute(share, "dp", [(i, i ^ j) for i in range(dp)]))
    shares = [
        one
        for share in shares
        for one in (share, lax.ppermute(share, "dp", [(i, i ^ 1) for i in range(dp)]))
    ]
    qkv_grad, out_grad, bias_grad, gain_attn_grad, gain_moe_grad, router_grad = run(
        functools.partial(finish_body, early_rows),
        [
            shape((dp, late_rows, width), f32),
            shape((columns, width), f32),
            shape((heads, rel_bias.shape[0]), f32),
            shape((width,), f32),
            shape((width,), f32),
            shape((experts, width), f32),
        ],
        [dp_one, *shares],
        smem=(0,),
        scratch=[pltpu.VMEM((dp, early_rows, width), f32)],
        us=2,
        name="finish",
    )
    return (
        output,
        grad_inputs,
        jnp.swapaxes(qkv_grad.reshape(3, columns, width), 1, 2),
        out_grad,
        bias_grad.T,
        gain_attn_grad,
        gain_moe_grad,
        router_grad.T,
        *weight_grads,
    )


def solution(mesh):
    placed = (
        P(("dp", "tensor"), None),
        P("dp", None),
        P(),
        P("dp", None, None),
        P(None, None, "tensor"),
        P("tensor", None),
        P(None, "tensor"),
        P(),
        P(),
        P(),
        P("dp", None, "tensor"),
        P("dp", "tensor", None),
        P(("dp", "tensor"), None),
    )
    return jax.shard_map(
        per_device,
        mesh=mesh,
        in_specs=placed,
        out_specs=(
            P(("dp", "tensor"), None),
            P(("dp", "tensor"), None),
            P(None, None, "tensor"),
            P("tensor", None),
            P(None, "tensor"),
            P(),
            P(),
            P(),
            P("dp", None, "tensor"),
            P("dp", "tensor", None),
        ),
        check_vma=False,
    )
```

```python
import functools

import jax
import jax.numpy as jnp
from jax import lax
from jax.experimental import pallas as pl
from jax.experimental.pallas import tpu as pltpu
from jax.sharding import PartitionSpec as P

epsilon = 1e-06
negative = -1000000000.0
bf16 = jnp.bfloat16
f32 = jnp.float32
reach = 256
rows_q = 128
window = rows_q + 2 * reach
table = window + rows_q
head_size = 64
mega = 1024 * 1024

core_pairs = [(0, 1), (1, 0), (2, 3), (3, 2)]
x_pairs = [(0, 2), (2, 0), (1, 3), (3, 1)]


def core_hop(value):
    return lax.ppermute(value, "tensor", core_pairs)


def x_hop(value):
    return lax.ppermute(value, "tensor", x_pairs)


def after(value, *deps):
    return lax.optimization_barrier((value, *deps))[0]


def gather4(value, *deps):
    other = x_hop(value)
    if deps:
        other = after(other, *deps)
    return value, core_hop(value), other, core_hop(other)


def dot(a, b, dims):
    return lax.dot_general(a, b, (dims, ((), ())), preferred_element_type=f32)


def mm(a, b):
    return dot(a, b, ((1,), (0,)))


def mm_nt(a, b):
    return dot(a, b, ((1,), (1,)))


def mm_tn(a, b):
    return dot(a, b, ((0,), (0,)))


def shape(dims, kind):
    return jax.ShapeDtypeStruct(dims, kind)


class Loaded:
    def __init__(self, source, buffer, sems, axis=0):
        self.buffer, self.axis = buffer, axis
        self.shape, self.dtype = buffer.shape, buffer.dtype
        count = len(sems)
        self.step = self.shape[axis] // count
        self.copies = []
        for i, sem in enumerate(sems):
            at = self.place(i) if count > 1 else ()
            part = (source.at[at], buffer.at[at]) if at else (source, buffer)
            self.copies.append(pltpu.make_async_copy(*part, sem))
            self.copies[-1].start()
        self.here = [False] * count

    def place(self, i):
        return (slice(None),) * self.axis + (pl.ds(i * self.step, self.step),)

    def piece(self, i):
        if not self.here[i]:
            self.copies[i].wait()
            self.here[i] = True

    def wait(self):
        for i in range(len(self.copies)):
            self.piece(i)

    def __getitem__(self, place):
        self.wait()
        return self.buffer[place]


class Stored:
    def __init__(self, target, buffer, sem):
        self.buffer, self.target, self.sem = buffer, target, sem
        self.shape, self.dtype = buffer.shape, buffer.dtype
        self.gone = 0

    def flush(self, first=0, rows=None):
        rows = self.shape[0] if rows is None else rows
        at = pl.ds(first, rows)
        pltpu.make_async_copy(self.buffer.at[at], self.target.at[at], self.sem).start()
        self.gone += rows

    def close(self):
        if not self.gone:
            self.flush()

    def wait(self):
        pltpu.make_async_copy(self.buffer, self.target, self.sem).wait()

    def __getitem__(self, place):
        return self.buffer[place]

    def __setitem__(self, place, value):
        self.buffer[place] = value


def run(
    body, outs, args, smem=(), loads=(), stores=(), hbm=(), hbm_outs=(), deps=(), aliases=None,
    scratch=(), us=2, name=None,
):
    args = list(args)
    if deps:
        args[0] = after(args[0], *deps)
    n_in, n_out, n_own = len(args), len(outs), len(scratch)
    cuts = [one if isinstance(one, tuple) else (one, 1, 0) for one in loads]
    loads = [one[0] for one in cuts]
    n_sems = sum(one[1] for one in cuts) + len(stores)

    def inner(*refs):
        ins = list(refs[:n_in])
        results = list(refs[n_in : n_in + n_out])
        own = refs[n_in + n_out : n_in + n_out + n_own]
        rest = refs[n_in + n_out + n_own :]
        buffers, sems = rest[:-1], rest[-1]
        used = 0
        for n, (i, pieces, axis) in enumerate(cuts):
            mine = [sems.at[used + j] for j in range(pieces)]
            ins[i] = Loaded(ins[i], buffers[n], mine, axis)
            used += pieces
        for n, i in enumerate(stores):
            results[i] = Stored(results[i], buffers[len(loads) + n], sems.at[used + n])
        body(*ins, *results, *own)
        for i in loads:
            ins[i].wait()
        for i in stores:
            results[i].close()
        for i in stores:
            results[i].wait()

    def space(i):
        if i in smem:
            return pltpu.SMEM
        return pltpu.HBM if i in hbm or i in loads else pltpu.VMEM

    for i in (*loads, *hbm):
        if i < n_in:
            args[i] = pltpu.with_memory_space_constraint(args[i], pltpu.HBM)
    kinds = [
        pltpu.HBM(o.shape, o.dtype) if i in hbm_outs or i in stores else o
        for i, o in enumerate(outs)
    ]
    staged = [pltpu.VMEM(args[i].shape, args[i].dtype) for i in loads]
    staged += [pltpu.VMEM(outs[i].shape, outs[i].dtype) for i in stores]
    return pl.pallas_call(
        inner,
        out_shape=kinds,
        in_specs=[pl.BlockSpec(memory_space=space(i)) for i in range(n_in)],
        out_specs=[
            pl.BlockSpec(
                memory_space=pltpu.HBM if i in hbm_outs or i in stores else pltpu.VMEM
            )
            for i in range(n_out)
        ],
        scratch_shapes=[
            *scratch, *staged, pltpu.SemaphoreType.DMA((max(1, n_sems),))
        ],
        input_output_aliases=aliases or {},
        compiler_params=pltpu.CompilerParams(vmem_limit_bytes=44 * mega),
        cost_estimate=pl.CostEstimate(
            flops=int(us * 1.1e9), bytes_accessed=mega // 4, transcendentals=0
        ),
        name=name,
    )(*args)


def as_column(row):
    wide = jnp.broadcast_to(row.astype(f32), (8, row.shape[1]))
    return wide.T[:, 0:1].astype(jnp.int32)


def slots_body(
    experts, capacity, row_ref, seg_row, near, bias, code_row, code_col, seg_col, tile
):
    seq = row_ref.shape[1]
    half = capacity // 2
    quarter = (experts // 2) * half
    first = lax.broadcasted_iota(jnp.int32, (seq, seq), 0)
    second = lax.broadcasted_iota(jnp.int32, (seq, seq), 1)
    route = row_ref[...]
    chosen = route == lax.broadcasted_iota(jnp.int32, (experts, seq), 0)
    count = mm(chosen.astype(bf16), (first < second).astype(bf16))
    slot = jnp.sum(jnp.where(chosen, count, 0.0), axis=0, keepdims=True).astype(jnp.int32)
    upper = jnp.where(slot >= half, 1, 0)
    code = (2 * (route & 1) + upper) * quarter + (route >> 1) * half + slot - half * upper
    code_row[...] = code
    code_col[...] = as_column(code)
    seg_col[...] = as_column(seg_row[...])
    bucket = near[...]
    for h in range(bias.shape[0]):
        line = jnp.zeros(bucket.shape, f32)
        for b in range(bias.shape[1]):
            line = jnp.where(bucket == b, bias[h, b], line)
        wide = jnp.broadcast_to(line, (rows_q, table))
        tile[h] = pltpu.roll(wide, 0, 1, stride=1, stride_axis=0)[:, :window]


def span(i0, seq):
    start = max(0, i0 - reach)
    end = min(seq, i0 + rows_q + reach)
    return start, end, start - (i0 - reach)


def masked_probs(score, same, tile):
    score = jnp.where(same, score + tile, negative)
    score = jnp.exp(score - jnp.max(score, axis=1, keepdims=True))
    return (score * (1.0 / jnp.sum(score, axis=1, keepdims=True))).astype(bf16)


def stack_heads(block, heads):
    lane = lax.broadcasted_iota(jnp.int32, block.shape, 1) // head_size
    return jnp.concatenate(
        [jnp.where(lane == h, block, jnp.zeros_like(block)) for h in range(heads)], axis=0
    )


def own_heads(stacked, heads):
    rows = stacked.shape[0] // heads
    lane = lax.broadcasted_iota(jnp.int32, (rows, stacked.shape[1]), 1) // head_size
    out = stacked[(heads - 1) * rows :]
    for h in range(heads - 1):
        out = jnp.where(lane == h, stacked[h * rows : (h + 1) * rows], out)
    return out


def masked_exp(score, same, tile):
    heads, rows, keys = tile.shape
    score = score.reshape(heads, rows, keys) + tile
    score = jnp.where(same[None], score, negative)
    return jnp.exp(score - jnp.max(score, axis=2, keepdims=True))


def attend_body(
    t_ref, x0, x1, x2, x3, gain, weight, seg_row, seg_col, tile, out_weight,
    x_all, normed, ctx, query, key, value,
):
    t = t_ref[0]
    own = x0.shape[0]
    seq = 4 * own
    heads = tile.shape[0]
    columns = heads * head_size
    for k, ref in ((1, x1), (2, x2), (3, x3), (0, x0)):
        at = pl.ds(pl.multiple_of((t ^ k) * own, own), own)
        x = ref[...]
        x_all[at, :] = x
        x = x.astype(f32)
        inv = lax.rsqrt(jnp.mean(x * x, axis=1, keepdims=True) + epsilon)
        normed[at, :] = (x * inv * gain[...]).astype(bf16)
    x_all.flush()
    normed.flush()
    query[...] = mm_nt(normed[...], weight[0]).astype(bf16)
    key[...] = mm_nt(weight[1], normed[...]).astype(bf16)
    value[:, 0:columns] = mm_nt(normed[...], weight[2]).astype(bf16)
    value[:, columns:] = jnp.ones((seq, head_size), bf16)
    for i0 in range(0, seq, rows_q):
        start, end, off = span(i0, seq)
        same = seg_col[i0 : i0 + rows_q, :] == seg_row[:, start:end]
        score = mm(stack_heads(query[i0 : i0 + rows_q, :], heads), key[:, start:end])
        weights = masked_exp(score, same, tile[:, :, off : off + end - start]).astype(bf16)
        out = mm(weights.reshape(heads * rows_q, end - start), value[start:end, :])
        out = out[:, 0:columns] * (1.0 / out[:, columns : columns + 1])
        out = own_heads(out, heads).astype(bf16)
        ctx[i0 : i0 + rows_q, :] = out[:, 0 : 2 * head_size]
        lane = 0 if i0 < seq // 2 else head_size
        at = seq + i0 % (seq // 2)
        ctx[at : at + rows_q, lane : lane + head_size] = out[:, 2 * head_size :]
    first = seq + seq // 2
    for j in range(out_weight.shape[1] // 128):
        ctx[first + j * columns : first + (j + 1) * columns, :] = out_weight[
            :, j * 128 : (j + 1) * 128
        ]


def probs_body(normed, weight, seg_row, seg_col, tile, probs, key_rows, query):
    seq = normed.shape[0]
    heads = tile.shape[0]
    query[...] = mm_nt(normed[...], weight[0]).astype(bf16)
    key_rows[...] = mm_nt(normed[...], weight[1]).astype(bf16)
    for i0 in range(0, seq, rows_q):
        start, end, off = span(i0, seq)
        same = seg_col[i0 : i0 + rows_q, :] == seg_row[:, start:end]
        score = mm_nt(stack_heads(query[i0 : i0 + rows_q, :], heads), key_rows[start:end, :])
        weights = masked_exp(score, same, tile[:, :, off : off + end - start])
        inv = 1.0 / jnp.sum(weights, axis=2, keepdims=True)
        probs[:, i0 : i0 + rows_q, 0 : end - start] = (weights * inv).astype(bf16)


def columns_body(normed, weight, ctx, query_cols, value_cols, ctx_cols):
    seq = normed.shape[0]
    columns = weight.shape[1]
    query_cols[...] = mm_nt(weight[0], normed[...]).astype(bf16)
    value_cols[...] = mm_nt(weight[2], normed[...]).astype(bf16)
    pair = 2 * head_size
    ctx_cols[0:pair, :] = ctx[0:seq, :].T
    last = ctx[seq : seq + seq // 2, :].T
    ctx_cols[pair:columns, 0 : seq // 2] = last[0:head_size, :]
    ctx_cols[pair:columns, seq // 2 :] = last[head_size:, :]


def third(ctx, r0, rows, seq):
    lane = 0 if r0 < seq // 2 else head_size
    at = seq + r0 % (seq // 2)
    return ctx[at : at + rows, lane : lane + head_size]


def mid_body(
    t_ref, x_all, c0, c1, c2, c3, gain, code_row,
    h_one, h_own, rows, normed, sums,
):
    t = t_ref[0]
    seq, width = x_all.shape
    own = seq // 4
    quarter = rows.shape[0]
    ctxs = (c0, c1, c2, c3)
    columns = 3 * head_size
    first = seq + seq // 2
    weights = [
        jnp.concatenate(
            [c[first + j * columns : first + (j + 1) * columns, :] for j in range(width // 128)],
            axis=1,
        )
        for c in ctxs
    ]
    pair = 2 * head_size
    packed = [
        jnp.concatenate([weights[2 * i][0:pair, :], weights[2 * i + 1][0:pair, :]], axis=0)
        for i in range(2)
    ]
    last = jnp.concatenate([w[pair : pair + head_size, :] for w in weights], axis=0)
    for r0 in range(0, seq, own):
        at = slice(r0, r0 + own)
        left = jnp.concatenate([ctxs[2][at, :], ctxs[3][at, :]], axis=1)
        total = mm(left, packed[1])
        left = jnp.concatenate([ctxs[0][at, :], ctxs[1][at, :]], axis=1)
        total = total + mm(left, packed[0])
        left = jnp.concatenate([third(c, r0, own, seq) for c in ctxs], axis=1)
        total = total + mm(left, last)
        total = total + x_all[at, :].astype(f32)
        h_one[at, :] = total.astype(bf16)
        h_one.flush(r0, own)
        sums[at, :] = total
        inv = lax.rsqrt(jnp.mean(total * total, axis=1, keepdims=True) + epsilon)
        normed[at, :] = (total * inv * gain[...]).astype(bf16)
    h_own[...] = sums[pl.ds(pl.multiple_of(t * own, own), own), :]
    h_own.flush()
    place = lax.broadcasted_iota(jnp.int32, (quarter, seq), 0) + t * quarter
    rows[...] = mm((place == code_row[...]).astype(bf16), normed[...]).astype(bf16)


def spread_body(t_ref, g0, g1, g2, g3, code_row, g_all, rows):
    t = t_ref[0]
    own = g0.shape[0]
    quarter = rows.shape[0]
    for k, ref in ((1, g1), (2, g2), (3, g3), (0, g0)):
        g_all[pl.ds(pl.multiple_of((t ^ k) * own, own), own), :] = ref[...]
    g_all.flush()
    place = lax.broadcasted_iota(jnp.int32, (quarter, g_all.shape[0]), 0) + t * quarter
    rows[...] = mm((place == code_row[...]).astype(bf16), g_all[...]).astype(bf16)


gelu_scale = 0.7978845608028654
gelu_cubic = 0.044715


def expert_body(
    near, e_ref, r0, r1, g0, g1, router, w_in_all, w_out_all,
    back0, back1, grad0, grad1, hidden_out, gated_out, pre_out, router_out,
    w_in, w_out, rows_all, g_rows, backs, grads, sem, out_sem,
):
    half = r0.shape[0]
    if near:
        load_in = pltpu.make_async_copy(w_in_all.at[e_ref[0]], w_in, sem.at[0])
        load_out = pltpu.make_async_copy(w_out_all.at[e_ref[0]], w_out, sem.at[1])
        load_in.start()
        load_out.start()
    else:
        w_in = w_in_all.at[e_ref[0]]
        w_out = w_out_all.at[e_ref[0]]
    rows_all[0] = r0[...]
    rows_all[1] = r1[...]
    g_rows[0] = g0[...]
    g_rows[1] = g1[...]
    router_out[...] = jnp.zeros(router_out.shape, f32)
    if near:
        load_in.wait()
        load_out.wait()
    sends = [
        [
            pltpu.make_async_copy(backs.at[i], back, out_sem.at[2 * i]),
            pltpu.make_async_copy(grads.at[i], grad, out_sem.at[2 * i + 1]),
        ]
        for i, (back, grad) in enumerate(((back0, grad0), (back1, grad1)))
    ]

    def one_half(i, carry):
        first = pl.multiple_of(i * half, half)
        at = pl.ds(first, half)
        rows = rows_all[i]
        cot = g_rows[i].astype(f32)
        logits = mm_nt(rows, router[...])
        logits = jnp.exp(logits - jnp.max(logits, axis=1, keepdims=True))
        prob = logits / jnp.sum(logits, axis=1, keepdims=True)
        mine = lax.broadcasted_iota(jnp.int32, prob.shape, 1) == e_ref[1]
        gate = jnp.sum(jnp.where(mine, prob, 0.0), axis=1, keepdims=True)
        gated = (gate * cot).astype(bf16)
        gated_out[at, :] = gated
        pre = mm(rows, w_in[...])
        square = pre * pre
        inner = jnp.tanh(gelu_scale * pre * (1.0 + gelu_cubic * square))
        half_up = 0.5 + 0.5 * inner
        hidden = (pre * half_up).astype(bf16)
        hidden_out[at, :] = hidden
        slope = half_up + (0.5 * gelu_scale) * pre * (1.0 - inner * inner) * (
            1.0 + (3.0 * gelu_cubic) * square
        )
        part = mm(hidden, w_out[...])
        backs[i] = (gate * part).astype(bf16)
        grad_gate = jnp.sum(cot * part, axis=1, keepdims=True)
        grad_pre = (mm_nt(gated, w_out[...]) * slope).astype(bf16)
        pre_out[at, :] = grad_pre
        grad_logits = (gate * grad_gate * (jnp.where(mine, 1.0, 0.0) - prob)).astype(bf16)
        grads[i] = (mm_nt(grad_pre, w_in[...]) + mm(grad_logits, router[...])).astype(bf16)
        for n in range(2):

            @pl.when(i == n)
            def _(n=n):
                sends[n][0].start()
                sends[n][1].start()

        router_out[...] += mm_tn(grad_logits, rows)
        return carry

    lax.fori_loop(0, 2, one_half, 0)
    hidden_out.flush()
    gated_out.flush()
    pre_out.flush()
    for pair in sends:
        for one in pair:
            one.wait()


def expert(near, scalars, r0, r1, g0, g1, router, w_in, w_out):
    half, width = r0.shape
    hidden = w_in.shape[2]
    rows = 2 * half
    return run(
        functools.partial(expert_body, near),
        [shape((half, width), bf16)] * 4
        + [
            shape((rows, hidden), bf16),
            shape((rows, width), bf16),
            shape((rows, hidden), bf16),
            shape(router.shape, f32),
        ],
        [scalars, r0, r1, g0, g1, router, w_in, w_out],
        smem=(0,),
        hbm=(6, 7) if near else (),
        hbm_outs=(0, 1, 2, 3),
        stores=(4, 5, 6),
        scratch=[
            pltpu.VMEM((width, hidden), bf16),
            pltpu.VMEM((hidden, width), bf16),
            pltpu.VMEM((2, half, width), bf16),
            pltpu.VMEM((2, half, width), bf16),
            pltpu.VMEM((2, half, width), bf16),
            pltpu.VMEM((2, half, width), bf16),
            pltpu.SemaphoreType.DMA((2,)),
            pltpu.SemaphoreType.DMA((4,)),
        ],
        us=7,
        name="expert",
    )


def expert_grad_body(first, e_ref, r0, r1, hidden, gated, pre, *refs):
    d_in, d_out, sum_in, sum_out, sem = refs[-5:]
    rows = jnp.concatenate([r0[...], r1[...]], axis=0)
    sum_in[...] = mm_tn(rows, pre[...])
    store_in = pltpu.make_async_copy(sum_in, d_in.at[e_ref[0]], sem.at[0])
    store_in.start()
    sum_out[...] = mm_tn(hidden[...], gated[...])
    store_out = pltpu.make_async_copy(sum_out, d_out.at[e_ref[0]], sem.at[1])
    store_out.start()
    store_in.wait()
    store_out.wait()


def expert_grads(scalars, r0, r1, hidden, gated, pre, so_far=(), deps=()):
    columns, width = hidden.shape[1], gated.shape[1]
    return run(
        functools.partial(expert_grad_body, not so_far),
        [shape((2, width, columns), f32), shape((2, columns, width), f32)],
        [scalars, r0, r1, hidden, gated, pre, *so_far],
        smem=(0,),
        loads=(3, 4, 5),
        hbm=(6, 7),
        hbm_outs=(0, 1),
        aliases={6: 0, 7: 1} if so_far else None,
        deps=deps,
        scratch=[
            pltpu.VMEM((width, columns), f32),
            pltpu.VMEM((columns, width), f32),
            pltpu.SemaphoreType.DMA((2,)),
        ],
        us=4,
        name="expert_grads",
    )


def back_body(
    t_ref, b0, b1, b2, b3, code_col, h_one, gain, g_all, weight, ctx_cols, router,
    h_own, gctx, early, grad_h, slots, sums,
):
    t = t_ref[0]
    seq, width = h_one.shape
    own = seq // 4
    quarter = b0.shape[0]
    columns = gctx.shape[1]
    for j, ref in enumerate((b0, b1, b2, b3)):
        slots[pl.ds(pl.multiple_of((t ^ j) * quarter, quarter), quarter), :] = ref[...]
    sum_gain = jnp.zeros((1, width), f32)
    step = 2 * own
    place = lax.broadcasted_iota(jnp.int32, (step, 4 * quarter), 1)
    for n, r0 in enumerate(range(0, seq, step)):
        at = slice(r0, r0 + step)
        total = mm((place == code_col[at, :]).astype(bf16), slots[...])
        for half in (2 * n, 2 * n + 1):
            h_one.piece(half)
            g_all.piece(half)
        h = h_one.buffer[at, :].astype(f32)
        inv = lax.rsqrt(jnp.mean(h * h, axis=1, keepdims=True) + epsilon)
        n2 = h * inv
        sum_gain = sum_gain + jnp.sum(total * n2, axis=0, keepdims=True)
        a = total * gain[...]
        mean = jnp.mean(a * n2, axis=1, keepdims=True)
        full = g_all.buffer[at, :].astype(f32) + inv * (a - n2 * mean)
        grad_h[at, :] = full.astype(bf16)
        sums[at, :] = full
    h_own[...] = sums[pl.ds(pl.multiple_of(t * own, own), own), :]
    h_own.flush()
    gctx[...] = mm_nt(grad_h[...], weight[...]).astype(bf16)
    gctx.flush()
    early[0:columns, :] = mm(ctx_cols[...], grad_h[...]).astype(bf16)
    rest = jnp.concatenate([router[...], sum_gain], axis=0)
    spare = early.shape[0] - columns - rest.shape[0]
    rest = jnp.concatenate([rest, jnp.zeros((spare, width), f32)], axis=0)
    early[columns:, :] = rest.astype(bf16)


def attend_back_body(
    gctx, value_cols, key_rows, query_cols, probs, normed, near,
    grad_q, grad_k, grad_v, late, grad_bias, spill, sum_k, sum_v,
):
    seq, columns = gctx.shape
    heads = columns // head_size
    buckets = grad_bias.shape[0]
    spill[...] = jnp.zeros(spill.shape, f32)
    sum_k[...] = jnp.zeros(sum_k.shape, f32)
    sum_v[...] = jnp.zeros(sum_v.shape, f32)
    gctx_cols = gctx[...].T
    for n, i0 in enumerate(range(0, seq, rows_q)):
        start, end, off = span(i0, seq)
        keys = end - start
        at = slice(i0, i0 + rows_q)
        grad = mm(stack_heads(gctx[at, :], heads), value_cols[:, start:end])
        probs.piece(n)
        prob = probs.buffer[:, at, 0:keys].reshape(heads * rows_q, keys)
        wide = prob.astype(f32)
        both = wide * grad
        score = both - wide * jnp.sum(both, axis=1, keepdims=True)
        spill[:, :, off : off + keys] += score.reshape(heads, rows_q, keys)
        score = score.astype(bf16)
        grad_q[at, :] = own_heads(mm(score, key_rows[start:end, :]), heads).astype(bf16)
        for h in range(heads):
            cols = slice(h * head_size, (h + 1) * head_size)
            mine = slice(h * rows_q, (h + 1) * rows_q)
            sum_k[cols, start:end] += mm(query_cols[cols, at], score[mine])
            sum_v[cols, start:end] += mm(gctx_cols[cols, at], prob[mine])
    grad_k[...] = sum_k[...].astype(bf16)
    grad_v[...] = sum_v[...].astype(bf16)
    grad_q.flush()
    grad_k.flush()
    grad_v.flush()
    late[0:columns, :] = mm_tn(grad_q[...], normed[...]).astype(bf16)
    late[columns : 2 * columns, :] = mm(grad_k[...], normed[...]).astype(bf16)
    late[2 * columns : 3 * columns, :] = mm(grad_v[...], normed[...]).astype(bf16)
    late.flush()
    chosen = near[...] == lax.broadcasted_iota(jnp.int32, (buckets, table), 0)
    places = lax.broadcasted_iota(jnp.int32, (buckets, 128), 1)
    found = jnp.zeros((buckets, 128), f32)
    for h in range(heads):
        strip = jnp.zeros((8, table), f32)
        for a in range(0, rows_q, 8):
            strip = strip + pltpu.roll(spill[h, a : a + 8, :], (table - a) % table, 1)
        line = lax.broadcasted_iota(jnp.int32, strip.shape, 0)
        for bit in (1, 2, 4):
            strip = jnp.where((line & bit) != 0, pltpu.roll(strip, table - bit, 1), strip)
        strip = jnp.sum(strip, axis=0, keepdims=True)
        per = jnp.sum(jnp.where(chosen, strip, 0.0), axis=1, keepdims=True)
        found = found + jnp.where(places == h, per, 0.0)
    grad_bias[...] = found


def input_grad_body(t_ref, grad_q, grad_k, grad_v, weight, normed, gain, keep, send, sums):
    t = t_ref[0]
    seq, width = normed.shape
    own = seq // 4
    total_gain = jnp.zeros((1, width), f32)
    for k in range(4):
        at = pl.ds(pl.multiple_of((t ^ k) * own, own), own)
        part = mm(grad_q[at, :], weight[0])
        part = part + mm_tn(grad_k[:, at], weight[1])
        part = part + mm_tn(grad_v[:, at], weight[2])
        total_gain = total_gain + jnp.sum(part * normed[at, :].astype(f32), axis=0, keepdims=True)
        out = keep if k in (0, 2) else send
        out[(k // 2) * own : (k // 2 + 1) * own, :] = part.astype(bf16)
    sums[...] = total_gain / gain[...]


def sum_copies(copies, ref):
    full = ref[...].astype(f32)
    rows = full.shape[0] // copies
    total = full[0:rows]
    for i in range(1, copies):
        total = total + full[i * rows : (i + 1) * rows]
    return total


def share_body(copies, early, late, sums, grad_bias, out):
    width = early.shape[1]
    found = grad_bias[...]
    lanes = found.shape[1]
    found = jnp.concatenate([found, jnp.zeros((lanes - found.shape[0], lanes), f32)], axis=0).T
    found = jnp.concatenate([found[0:8], jnp.zeros((8, width - lanes), f32)], axis=1)
    line = lax.broadcasted_iota(jnp.int32, found.shape, 0)
    found = jnp.where(line == 7, sums[...], found)
    total = [found, sum_copies(copies, early), sum_copies(copies, late)]
    out[...] = jnp.concatenate(total, axis=0).astype(bf16)


def finish_body(early_rows, i_ref, *refs):
    shares = refs[:-7]
    qkv, out, bias, gain_attn, gain_moe, router, early = refs[-7:]
    columns = out.shape[0]
    experts = router.shape[0]
    small = None
    for j, ref in enumerate(shares):
        full = ref[...].astype(f32)
        owner = i_ref[0] ^ j
        small = full[0:8] if small is None else small + full[0:8]
        early[owner] = full[8 : 8 + early_rows]
        qkv[owner] = full[8 + early_rows :]
    whole = jnp.concatenate([early[i] for i in range(early.shape[0])], axis=0)
    out[...] = whole[0:columns]
    router[...] = whole[columns : columns + experts]
    gain_moe[...] = whole[columns + experts]
    bias[...] = small[0 : bias.shape[0], 0 : bias.shape[1]]
    gain_attn[...] = small[7]


def last_body(kept, got, far, x_ref, gain, h_own, grad):
    total = kept[...].astype(f32) + got[...].astype(f32) + far[...].astype(f32)
    x = x_ref[...].astype(f32)
    inv = lax.rsqrt(jnp.mean(x * x, axis=1, keepdims=True) + epsilon)
    n1 = x * inv
    a = total * gain[...]
    grad[...] = h_own[...] + inv * (a - n1 * jnp.mean(a * n1, axis=1, keepdims=True))


def output_body(t_ref, f0, f1, f2, f3, code_col, h_own, out, slots):
    t = t_ref[0]
    own = h_own.shape[0]
    quarter = f0.shape[0]
    for j, ref in enumerate((f0, f1, f2, f3)):
        slots[pl.ds(pl.multiple_of((t ^ j) * quarter, quarter), quarter), :] = ref[...]
    codes = code_col[pl.ds(pl.multiple_of(t * own, own), own), :]
    place = lax.broadcasted_iota(jnp.int32, (own, 4 * quarter), 1)
    out[...] = (h_own[...] + mm((place == codes).astype(bf16), slots[...])).astype(bf16)


def turn(value):
    return lax.all_to_all(value, "dp", split_axis=0, concat_axis=0, tiled=True)


def per_device(
    inputs,
    segments,
    buckets,
    routes,
    qkv_weight,
    out_weight,
    rel_bias,
    norm_attn,
    norm_moe,
    router_weight,
    expert_in,
    expert_out,
    cotangent,
):
    own, width = inputs.shape
    seq = 4 * own
    dp = lax.axis_size("dp")
    experts = router_weight.shape[1]
    capacity = max(2, 5 * seq // (4 * experts))
    quarter = (experts // 2) * (capacity // 2)
    heads = rel_bias.shape[1]
    columns = heads * head_size
    t_one = lax.axis_index("tensor").astype(jnp.int32)[None]
    x_side = t_one >> 1
    dp_one = lax.axis_index("dp").astype(jnp.int32)[None]
    first_expert = 2 * dp_one
    near_expert = jnp.concatenate([x_side, first_expert + x_side])
    far_expert = jnp.concatenate([1 - x_side, first_expert + 1 - x_side])
    inputs, t_one, dp_one, near_expert, far_expert = lax.optimization_barrier(
        (inputs, t_one, dp_one, near_expert, far_expert)
    )
    gain_attn = norm_attn[None, :]
    gain_moe = norm_moe[None, :]
    near = lax.slice_in_dim(buckets, seq - 1 - reach, seq - 1 - reach + table, axis=0)[None, :]
    weight = jnp.swapaxes(qkv_weight, 1, 2)
    router = router_weight.T

    code_row, code_col, seg_col, tile = run(
        functools.partial(slots_body, experts, capacity),
        [
            shape((1, seq), jnp.int32),
            shape((seq, 1), jnp.int32),
            shape((seq, 1), jnp.int32),
            shape((heads, rows_q, window), f32),
        ],
        [routes.reshape(1, seq), segments, near, rel_bias.T],
        smem=(3,),
        us=2,
        stores=(3,),
        name="slots",
    )
    xs = gather4(inputs, code_row)
    g_core = core_hop(cotangent)
    x_all, normed, ctx = run(
        attend_body,
        [
            shape((seq, width), bf16),
            shape((seq, width), bf16),
            shape((seq + seq // 2 + columns * width // 128, 128), bf16),
        ],
        [t_one, *xs, gain_attn, weight, segments, seg_col, tile, out_weight],
        smem=(0,),
        scratch=[
            pltpu.VMEM((seq, columns), bf16),
            pltpu.VMEM((columns, seq), bf16),
            pltpu.VMEM((seq, columns + head_size), bf16),
        ],
        us=10,
        loads=(1, 6, 9, 10),
        stores=(0, 1, 2),
        deps=[g_core],
        name="attend",
    )
    g_far_block = after(x_hop(cotangent), ctx)
    gs = (cotangent, g_core, g_far_block, core_hop(g_far_block))
    g_all, g_rows = run(
        spread_body,
        [shape((seq, width), bf16), shape((quarter, width), bf16)],
        [t_one, *gs, code_row],
        smem=(0,),
        us=0.1,
        loads=(1,),
        stores=(0,),
        name="spread",
    )
    query_cols, value_cols, ctx_cols = run(
        columns_body,
        [shape((columns, seq), bf16)] * 3,
        [normed, weight, ctx],
        deps=[g_rows],
        us=0.1,
        loads=(0, 1, 2),
        stores=(0, 1, 2),
        name="columns",
    )
    cs = gather4(ctx, query_cols)
    h_one, h_own, rows = run(
        mid_body,
        [
            shape((seq, width), bf16),
            shape((own, width), f32),
            shape((quarter, width), bf16),
        ],
        [t_one, x_all, *cs, gain_moe, code_row],
        smem=(0,),
        scratch=[pltpu.VMEM((seq, width), bf16), pltpu.VMEM((seq, width), f32)],
        us=0.1,
        loads=(2, 1),
        stores=(0, 1),
        name="mid",
    )
    g_got = turn(g_rows)
    g_far = x_hop(after(g_got, rows))
    probs, key_rows = run(
        probs_body,
        [shape((heads, seq, window), bf16), shape((seq, columns), bf16)],
        [normed, weight, segments, seg_col, tile],
        deps=[rows],
        scratch=[pltpu.VMEM((seq, columns), bf16)],
        us=7,
        loads=(0, 1, 4),
        stores=(0, 1),
        name="probs",
    )
    row_got = after(turn(rows), probs, g_far)
    near_rows = (row_got, core_hop(row_got))
    g_near = after(g_got, probs)
    near_out = expert(
        True, near_expert, *near_rows, g_near, core_hop(g_near), router, expert_in, expert_out
    )
    far_mine = after(x_hop(row_got), near_out[0])
    far_rows = (far_mine, core_hop(far_mine))
    far_out = expert(
        False, far_expert, *far_rows, g_far, core_hop(g_far), router, expert_in, expert_out
    )
    far = far_out[2] + core_hop(far_out[3])
    router_part = near_out[7] + far_out[7]
    router_part = router_part + core_hop(router_part)
    router_far = x_hop(router_part)
    weight_grads = expert_grads(near_expert, *near_rows, *near_out[4:7], deps=[far])
    far, router_far = lax.optimization_barrier((x_hop(far), router_far, weight_grads[0]))[:2]
    router_part = router_part + router_far
    kept = near_out[2] + core_hop(near_out[3]) + far
    home = turn(kept)
    far = after(far_out[0], kept) + core_hop(far_out[1])
    weight_grads = expert_grads(
        far_expert, *far_rows, *far_out[4:7], so_far=weight_grads, deps=[far]
    )
    home = after(home, weight_grads[0])
    fwd = after(near_out[0], home) + core_hop(near_out[1]) + x_hop(far)
    bs = gather4(home, fwd)
    fwd = turn(fwd)
    small = -(-(experts + 1) // 64) * 64
    gh_own, gctx, early = run(
        back_body,
        [
            shape((own, width), f32),
            shape((seq, columns), bf16),
            shape((columns + small, width), bf16),
        ],
        [t_one, *bs, code_col, h_one, gain_moe, g_all, out_weight, ctx_cols, router_part],
        smem=(0,),
        loads=((6, 4, 0), (8, 4, 0), 9, 10),
        stores=(0, 1),
        scratch=[
            pltpu.VMEM((seq, width), bf16),
            pltpu.VMEM((4 * quarter, width), bf16),
            pltpu.VMEM((seq, width), f32),
        ],
        us=2,
        name="back",
    )
    early_got = turn(early)
    grad_q, grad_k, grad_v, late, grad_bias = run(
        attend_back_body,
        [
            shape((seq, columns), bf16),
            shape((columns, seq), bf16),
            shape((columns, seq), bf16),
            shape((3 * columns, width), bf16),
            shape((rel_bias.shape[0], 128), f32),
        ],
        [gctx, value_cols, key_rows, query_cols, probs, normed, near],
        loads=(0, 1, 2, 3, (4, seq // rows_q, 1), 5),
        stores=(0, 1, 2, 3),
        deps=[fwd],
        scratch=[
            pltpu.VMEM((heads, rows_q, table), f32),
            pltpu.VMEM((columns, seq), f32),
            pltpu.VMEM((columns, seq), f32),
        ],
        us=14,
        name="attend_back",
    )
    f_far = x_hop(after(fwd, gctx))
    fs = (fwd, core_hop(fwd), f_far, core_hop(f_far))
    late_got = turn(after(late, f_far))
    keep, send, gain_part = run(
        input_grad_body,
        [
            shape((2 * own, width), bf16),
            shape((2 * own, width), bf16),
            shape((1, width), f32),
        ],
        [t_one, grad_q, grad_k, grad_v, weight, normed, gain_attn],
        smem=(0,),
        us=0.1,
        loads=(1, 2, 3, 4, 5),
        name="input_grad",
    )
    gain_part = gain_part + core_hop(gain_part)
    gain_part = gain_part + x_hop(gain_part)
    keep, send = lax.optimization_barrier((keep, send, gain_part))[:2]
    got = core_hop(send)
    far = x_hop(keep[own:] + got[own:])
    (grad_inputs,) = run(
        last_body,
        [shape((own, width), f32)],
        [keep[:own], got[:own], far, inputs, gain_attn, gh_own],
        loads=(3, 5),
        us=16,
        name="last",
    )
    (output,) = run(
        output_body,
        [shape((own, width), bf16)],
        [t_one, *fs, code_col, h_own],
        smem=(0,),
        loads=(6,),
        scratch=[pltpu.VMEM((4 * quarter, width), bf16)],
        us=1,
        name="output",
    )
    early_rows = early.shape[0] // dp
    late_rows = late.shape[0] // dp
    (share,) = run(
        functools.partial(share_body, dp),
        [shape((8 + early_rows + late_rows, width), bf16)],
        [early_got, late_got, gain_part, grad_bias],
        deps=[output],
        us=1,
        name="share",
    )
    shares = [share]
    for j in range(2, dp, 2):
        shares.append(lax.ppermute(share, "dp", [(i, i ^ j) for i in range(dp)]))
    shares = [
        one
        for share in shares
        for one in (share, lax.ppermute(share, "dp", [(i, i ^ 1) for i in range(dp)]))
    ]
    qkv_grad, out_grad, bias_grad, gain_attn_grad, gain_moe_grad, router_grad = run(
        functools.partial(finish_body, early_rows),
        [
            shape((dp, late_rows, width), f32),
            shape((columns, width), f32),
            shape((heads, rel_bias.shape[0]), f32),
            shape((width,), f32),
            shape((width,), f32),
            shape((experts, width), f32),
        ],
        [dp_one, *shares],
        smem=(0,),
        scratch=[pltpu.VMEM((dp, early_rows, width), f32)],
        us=2,
        name="finish",
    )
    return (
        output,
        grad_inputs,
        jnp.swapaxes(qkv_grad.reshape(3, columns, width), 1, 2),
        out_grad,
        bias_grad.T,
        gain_attn_grad,
        gain_moe_grad,
        router_grad.T,
        *weight_grads,
    )


def solution(mesh):
    placed = (
        P(("dp", "tensor"), None),
        P("dp", None),
        P(),
        P("dp", None, None),
        P(None, None, "tensor"),
        P("tensor", None),
        P(None, "tensor"),
        P(),
        P(),
        P(),
        P("dp", None, "tensor"),
        P("dp", "tensor", None),
        P(("dp", "tensor"), None),
    )
    return jax.shard_map(
        per_device,
        mesh=mesh,
        in_specs=placed,
        out_specs=(
            P(("dp", "tensor"), None),
            P(("dp", "tensor"), None),
            P(None, None, "tensor"),
            P("tensor", None),
            P(None, "tensor"),
            P(),
            P(),
            P(),
            P("dp", None, "tensor"),
            P("dp", "tensor", None),
        ),
        check_vma=False,
    )
```
